32 devices in a mesh: frame: 4 (over y, x), pix: 8 (over z, core).
Axes of the slice: x: 2, y: 2, z: 4, core: 2. Of those that a mesh axis runs over, the one named last changes fastest.
Arguments:
- frames: bfloat16 [128, 4, 128, 512], P('frame', None, 'pix'), may hold values from -26 to 26
- prev_fg: bfloat16 [128, 4, 128, 512], P('frame', None, 'pix'), may hold values from -3 to 3
- depth_valid: int32 [128, 128, 512], P('frame', 'pix'), may hold values 0 or 1
- sketch: float32 [128, 64], replicated, may hold values from -0.5 to 0.5
- tv_weight: float32 [4], replicated, may hold values from 0.1 to 1
Outputs:
- background: bfloat16 [128, 4, 128, 512], P('frame', None, 'pix')
- foreground: bfloat16 [128, 4, 128, 512], P('frame', None, 'pix')
The draws below stay inside these ranges and needn't reach their ends.
All inputs are finite; a program needn't handle non-finite values. No bound on the sum of `depth_valid` on one device may be relied on, other than what follows from the above.
Results may differ from the reference program's by a relative error of at most 0.012.
The reference program's roundings to bfloat16 on the way count: a program that leaves them out, or rounds other values in their place, can miss the bound.
Values may be sent and summed in bfloat16 or wider, within the bound.
No kernel may reach another device: no remote copies, remote signals or barrier semaphores. Data moves between devices by JAX's collectives and lax.ppermute only.
A program may use at most 64 MiB of HBM per device.

```python
import math
import jax
import jax.numpy as jnp
from jax import lax

CH = 4
RANK = 64
COLS = 512
POWER = 3
NSWEEP = 5
FRAMES = 128
HEIGHT = 128


def draw_frames(key, part):
    subkeys = jax.random.split(key, 8)
    shape = (FRAMES, CH, HEIGHT, COLS)
    pixel_shape = (1, CH, HEIGHT, COLS)
    level = jnp.exp(jax.random.uniform(subkeys[0], (FRAMES, 1, 1, 1), jnp.float32, math.log(0.3), math.log(3.0)))
    row_pos = lax.broadcasted_iota(jnp.float32, (1, 1, HEIGHT, 1), 2)
    rise = jnp.sqrt(1.0 + 2.0 * row_pos / max(HEIGHT - 1, 1))
    moments = lax.broadcasted_iota(jnp.float32, (FRAMES, 1, 1, 1), 0)
    exponent = 2.0
    motion = 0.5 * jax.random.truncated_normal(subkeys[1], -4.0, 4.0, shape, jnp.float32)
    for wave in range(2):
        frequency = math.pi * jax.random.uniform(subkeys[2 + 3 * wave], pixel_shape, jnp.float32) ** exponent
        phase = jax.random.uniform(subkeys[3 + 3 * wave], pixel_shape, jnp.float32, -math.pi, math.pi)
        amplitude = jax.random.uniform(subkeys[4 + 3 * wave], pixel_shape, jnp.float32, 0.5, 1.5)
        motion = motion + amplitude * jnp.cos(frequency * moments + phase)
    return (motion * level * rise).astype(jnp.bfloat16)


def place_ends(entries, own_key, smallest, top_value):
    place = [jax.random.randint(jax.random.fold_in(own_key, axis), (), 0, length) for axis, length in enumerate(entries.shape)]
    longest = entries.shape.index(max(entries.shape))
    beside = place[:longest] + [(place[longest] + 1) % entries.shape[longest]] + place[longest + 1:]
    return entries.at[tuple(place)].set(smallest).at[tuple(beside)].set(top_value)


def steps_of(own_key, shape, cuts, low, top_value):
    def one(dim, parts):
        steps = jax.random.uniform(jax.random.fold_in(jax.random.fold_in(own_key, 6), dim), (parts,), jnp.float32, low / len(cuts), top_value / len(cuts))
        return jnp.repeat(jnp.exp(steps), shape[dim] // parts).reshape((-1,) + (1,) * (len(shape) - dim - 1))

    loudness = one(*cuts[0])
    for cut in cuts[1:]:
        loudness = loudness * one(*cut)
    return loudness


def centred(stream_key, dims, width, bound, shards=(), held_as=jnp.bfloat16):
    loudness = steps_of(stream_key, dims, shards, -0.22, 0.18) if shards else 1.0
    drawn = jax.random.normal(stream_key, dims, jnp.float32) * width * loudness
    return jnp.minimum(jnp.maximum(drawn, -bound), bound).astype(held_as)


def setup_inputs(seed: int = 0) -> dict:
    streams_of = jax.random.split(jax.random.key(seed), 6)
    frames = draw_frames(jax.random.fold_in(streams_of[5], 71), 0)
    prev_fg = centred(streams_of[1], (FRAMES, CH, HEIGHT, COLS), 0.5, 3.0, ((0, 4), (2, 8)))
    depth_valid = place_ends((jax.random.randint(streams_of[2], (FRAMES, HEIGHT, COLS), 0, 8) < 7).astype(jnp.int32), jax.random.fold_in(streams_of[2], 1), 0, 1)
    sketch = centred(streams_of[3], (FRAMES, RANK), FRAMES ** -0.5, 0.5, (), jnp.float32)
    tv_weight = jnp.clip(jnp.exp(jax.random.uniform(streams_of[4], (CH,), jnp.float32, math.log(0.1), math.log(1.0))), 0.1, 1.0)
    return {"frames": frames, "prev_fg": prev_fg, "depth_valid": depth_valid, "sketch": sketch, "tv_weight": tv_weight}


STEP_SIZE = 0.125

def exact_dot(left, right):
    return jnp.dot(left, right, precision=lax.Precision.HIGHEST)

def mixing_matrix(gram, sketch):
    basis = sketch
    for turn in range(POWER):
        image = exact_dot(gram, basis)
        factor = jnp.linalg.cholesky(exact_dot(basis.T, image))
        basis = lax.linalg.triangular_solve(factor, image, left_side=False, lower=True, transpose_a=True)
    image = exact_dot(gram, basis)
    factor = jnp.linalg.cholesky(exact_dot(basis.T, image))
    middle = lax.linalg.triangular_solve(factor, exact_dot(basis.T, gram), left_side=True, lower=True)
    coeffs = lax.linalg.triangular_solve(factor, middle, left_side=True, lower=True, transpose_a=True)
    return exact_dot(basis, coeffs)

def dual_update(first, second, down, across, step):
    size = jnp.sqrt(down * down + across * across)
    scale = 1.0 + step * size
    return ((first - step * down) / scale, (second - step * across) / scale)

def reference(frames, prev_fg, depth_valid, sketch, tv_weight):
    chan_ids = lax.broadcasted_iota(jnp.int32, (1, CH, 1, 1), 1)
    depth_ok = depth_valid[:, None, :, :].astype(jnp.float32)
    valid = jnp.where(chan_ids == CH - 1, depth_ok, jnp.float32(1.0))
    resid = ((frames.astype(jnp.float32) - prev_fg.astype(jnp.float32)) * valid).astype(jnp.bfloat16)
    flat = resid.reshape(FRAMES, CH * HEIGHT * COLS)
    gram = jnp.dot(flat.astype(jnp.float32), flat.T.astype(jnp.float32), preferred_element_type=jnp.float32) / (CH * HEIGHT * COLS)
    mixing = mixing_matrix(gram, sketch)
    back = jnp.dot(mixing.astype(jnp.bfloat16).T.astype(jnp.float32), flat.astype(jnp.float32), preferred_element_type=jnp.float32)
    back = back.reshape(FRAMES, CH, HEIGHT, COLS)
    background = back.astype(jnp.bfloat16)
    rounded = lax.optimization_barrier(background).astype(jnp.float32)
    source = (frames.astype(jnp.float32) - rounded) * valid
    lam = tv_weight.reshape(CH, 1, 1)
    step = STEP_SIZE / lam
    last_row = lax.broadcasted_iota(jnp.int32, (1, HEIGHT, 1), 1) == HEIGHT - 1
    last_col = lax.broadcasted_iota(jnp.int32, (1, 1, COLS), 2) == COLS - 1

    def divergence(first, second):
        prev_rows = jnp.pad(first[:, :-1, :], ((0, 0), (1, 0), (0, 0)))
        prev_cols = jnp.pad(second[:, :, :-1], ((0, 0), (0, 0), (1, 0)))
        return first - prev_rows + (second - prev_cols)

    def one_frame(image):
        first = jnp.zeros_like(image)
        second = jnp.zeros_like(image)
        for sweep in range(NSWEEP):
            smooth = image - lam * divergence(first, second)
            next_rows = jnp.pad(smooth[:, 1:, :], ((0, 0), (0, 1), (0, 0)))
            next_cols = jnp.pad(smooth[:, :, 1:], ((0, 0), (0, 0), (0, 1)))
            down = jnp.where(last_row, 0.0, next_rows - smooth)
            across = jnp.where(last_col, 0.0, next_cols - smooth)
            first, second = dual_update(first, second, down, across, step)
        return image - lam * divergence(first, second)
    foreground = lax.map(one_frame, source).astype(jnp.bfloat16)
    return (background, foreground)
```

```python
import jax
import jax.numpy as jnp
from jax import lax
from jax.sharding import PartitionSpec as P

POWER = 3
NSWEEP = 5


STEP_SIZE = 0.125


def shortened(shard):

    def short(part):
        return part.astype(jnp.bfloat16) if part.dtype == jnp.float32 else part

    return jax.tree.map(short, shard)


def from_behind(value, axis, steps):
    count = lax.axis_size(axis)
    leading, last = (max(0, -steps), min(count, count - steps))
    return lax.ppermute(value, axis, [(source, source + steps) for source in range(leading, last)])


def partners(value, axis, offsets):
    count = lax.axis_size(axis)
    return [
        lax.ppermute(value, axis, [(source, source ^ offset) for source in range(count)])
        for offset in offsets
    ]


def all_sum(value, axis):
    count = lax.axis_size(axis)
    if count & (count - 1):
        return lax.psum(value, axis)
    bit = 1
    while bit < count:
        fours = count // bit % 4 == 0 and (count // bit).bit_length() % 2 == 1
        offsets = (bit, 2 * bit, 3 * bit) if fours else (bit,)
        for other in partners(value, axis, offsets):
            value = value + other
        bit *= len(offsets) + 1
    return value


def exact_dot(left, right):
    return jnp.dot(left, right, precision=lax.Precision.HIGHEST)


def mixing_matrix(gram, sketch):
    basis = sketch
    for turn in range(POWER):
        image = exact_dot(gram, basis)
        factor = jnp.linalg.cholesky(exact_dot(basis.T, image))
        basis = lax.linalg.triangular_solve(
            factor, image, left_side=False, lower=True, transpose_a=True
        )
    image = exact_dot(gram, basis)
    factor = jnp.linalg.cholesky(exact_dot(basis.T, image))
    middle = lax.linalg.triangular_solve(
        factor, exact_dot(basis.T, gram), left_side=True, lower=True
    )
    coeffs = lax.linalg.triangular_solve(
        factor, middle, left_side=True, lower=True, transpose_a=True
    )
    return exact_dot(basis, coeffs)


def pair_rows(left, right):
    return lax.dot_general(
        left, right, (((1,), (1,)), ((), ())), preferred_element_type=jnp.float32
    )


def over_frames(weights, pixels):
    return lax.dot_general(
        weights, pixels, (((0,), (0,)), ((), ())), preferred_element_type=jnp.float32
    )


def dual_update(first, second, down, across, step):
    size = jnp.sqrt(down * down + across * across)
    scale = 1.0 + step * size
    return ((first - step * down) / scale, (second - step * across) / scale)


def col_prev(field):
    return jnp.pad(field[:, :, :, :-1], ((0, 0), (0, 0), (0, 0), (1, 0)))


def col_grad(smooth, last_col):
    next_cols = jnp.pad(smooth[:, :, :, 1:], ((0, 0), (0, 0), (0, 0), (0, 1)))
    return jnp.where(last_col, 0.0, next_cols - smooth)


def body(frames, prev_fg, depth_valid, sketch, tv_weight):
    count, chans, rows, cols = frames.shape
    height = rows * lax.axis_size("pix")
    nval = chans * height * cols
    chan_ids = lax.broadcasted_iota(jnp.int32, (1, chans, 1, 1), 1)
    depth_ok = depth_valid[:, None, :, :].astype(jnp.float32)
    valid = jnp.where(chan_ids == chans - 1, depth_ok, jnp.float32(1.0))
    resid = ((frames.astype(jnp.float32) - prev_fg.astype(jnp.float32)) * valid).astype(
        jnp.bfloat16
    )
    flat = resid.reshape(count, chans * rows * cols)
    local = lax.all_to_all(flat, "frame", split_axis=1, concat_axis=0, tiled=True)
    whole_terms = pair_rows(local, local)
    gram = all_sum(all_sum(whole_terms, "frame"), "pix") / nval
    mixing = mixing_matrix(gram, sketch)
    spread = over_frames(mixing.astype(jnp.bfloat16), local).astype(jnp.bfloat16)
    background = lax.all_to_all(spread, "frame", split_axis=0, concat_axis=1, tiled=True).reshape(
        count, chans, rows, cols
    )
    rounded = lax.optimization_barrier(background).astype(jnp.float32)
    source = (frames.astype(jnp.float32) - rounded) * valid
    lam = tv_weight.reshape(1, chans, 1, 1)
    step = STEP_SIZE / lam
    last_col = lax.broadcasted_iota(jnp.int32, (1, 1, 1, cols), 3) == cols - 1
    row_ids = lax.axis_index("pix") * rows + lax.broadcasted_iota(jnp.int32, (1, 1, rows, 1), 2)
    last_row = row_ids == height - 1

    def divergence(first, second):
        above = from_behind(shortened(first[:, :, -1:, :]), "pix", 1)
        prev_rows = jnp.concatenate([above, first[:, :, :-1, :]], axis=2)
        return first - prev_rows + (second - col_prev(second))

    first = jnp.zeros_like(source)
    second = jnp.zeros_like(source)
    for sweep in range(NSWEEP):
        smooth = source - lam * divergence(first, second)
        below = from_behind(shortened(smooth[:, :, :1, :]), "pix", -1)
        next_rows = jnp.concatenate([smooth[:, :, 1:, :], below], axis=2)
        down = jnp.where(last_row, 0.0, next_rows - smooth)
        across = col_grad(smooth, last_col)
        first, second = dual_update(first, second, down, across, step)
    smooth = source - lam * divergence(first, second)
    return (background, smooth.astype(jnp.bfloat16))


def solution(mesh):
    placed = (
        P("frame", None, "pix", None),
        P("frame", None, "pix", None),
        P("frame", "pix", None),
        P(),
        P(),
    )
    return jax.shard_map(
        body,
        mesh=mesh,
        in_specs=placed,
        out_specs=(P("frame", None, "pix", None), P("frame", None, "pix", None)),
        check_vma=False,
    )
```

```python
import jax
import jax.numpy as jnp
from jax import lax
from jax.experimental import pallas as pl
from jax.experimental.pallas import tpu as pltpu
from jax.sharding import PartitionSpec as P

POWER = 3
NSWEEP = 5
SUB = 8


STEP_SIZE = 0.125


def shortened(shard):

    def short(part):
        return part.astype(jnp.bfloat16) if part.dtype == jnp.float32 else part

    return jax.tree.map(short, shard)


def from_behind(value, axis, steps):
    count = lax.axis_size(axis)
    leading, last = (max(0, -steps), min(count, count - steps))
    return lax.ppermute(value, axis, [(source, source + steps) for source in range(leading, last)])


def partners(value, axis, offsets):
    count = lax.axis_size(axis)
    return [
        lax.ppermute(value, axis, [(source, source ^ offset) for source in range(count)])
        for offset in offsets
    ]


def all_sum(value, axis):
    count = lax.axis_size(axis)
    if count & (count - 1):
        return lax.psum(value, axis)
    bit = 1
    while bit < count:
        fours = count // bit % 4 == 0 and (count // bit).bit_length() % 2 == 1
        offsets = (bit, 2 * bit, 3 * bit) if fours else (bit,)
        for other in partners(value, axis, offsets):
            value = value + other
        bit *= len(offsets) + 1
    return value


def exact_dot(left, right, left_dim, right_dim):
    return lax.dot_general(
        left,
        right,
        (((left_dim,), (right_dim,)), ((), ())),
        precision=lax.Precision.HIGHEST,
        preferred_element_type=jnp.float32,
    )


def eliminate(square, sides):
    rank = square.shape[0]
    width = sides[0].shape[1]
    blocks = rank // SUB
    sub_ids = lax.broadcasted_iota(jnp.int32, (SUB, width), 0)
    square = jnp.concatenate([square, jnp.zeros((rank, width - rank), jnp.float32)], axis=1)

    def in_blocks(rows):
        return [rows[SUB * b : SUB * (b + 1)] for b in range(blocks)]

    def row_of(rows, j):
        return jnp.broadcast_to(rows[j : j + 1], (SUB, width))

    def col_of(rows, j):
        return jnp.broadcast_to(rows[:, j : j + 1], (SUB, width))

    square = in_blocks(square)
    sides = [in_blocks(side) for side in sides]
    solved = [[] for _ in sides]
    for k in range(blocks):
        below = range(k, blocks)
        cols = {b: [col_of(square[b], SUB * k + j) for j in range(SUB)] for b in below}
        pivots = jnp.ones((SUB, width), jnp.float32)
        for j in range(SUB):
            pivot = row_of(cols[k][j], j)
            inverse = 1.0 / pivot
            pivots = jnp.where(sub_ids == j, pivot, pivots)
            col_rows = {i: row_of(cols[k][i], j) for i in range(j + 1, SUB)}
            square_row = row_of(square[k], j)
            side_rows = [row_of(side[k], j) for side in sides]
            for b in below:
                ratio = cols[b][j] * inverse
                if b == k:
                    ratio = jnp.where(sub_ids > j, ratio, 0.0)
                for i in range(j + 1, SUB):
                    cols[b][i] = cols[b][i] - ratio * col_rows[i]
                square[b] = square[b] - ratio * square_row
                for side, side_row in zip(sides, side_rows):
                    side[b] = side[b] - ratio * side_row
        scale = lax.rsqrt(pivots)
        for rows, side in zip(solved, sides):
            rows.append(side[k] * scale)
    return [jnp.concatenate(rows, axis=0) for rows in solved]


def mixing_kernel(gram_ref, sketch_ref, mixing_ref):
    gram = gram_ref[...]
    basis = sketch_ref[...]
    for turn in range(POWER):
        image = exact_dot(basis, gram, 1, 1)
        (basis,) = eliminate(exact_dot(basis, image, 1, 1), [image])
    image = exact_dot(basis, gram, 1, 1)
    left, right = eliminate(exact_dot(basis, image, 1, 1), [basis, image])
    mixing_ref[...] = exact_dot(left, right, 0, 0).astype(mixing_ref.dtype)


def mixing_matrix(gram, sketch):
    return pl.pallas_call(
        mixing_kernel,
        out_shape=jax.ShapeDtypeStruct(gram.shape, jnp.bfloat16),
        name="mixing",
    )(gram, sketch.T)


def pair_rows(left, right):
    return lax.dot_general(
        left, right, (((1,), (1,)), ((), ())), preferred_element_type=jnp.float32
    )


def over_frames(weights, pixels):
    return lax.dot_general(
        weights, pixels, (((0,), (0,)), ((), ())), preferred_element_type=jnp.float32
    )


def dual_update(first, second, down, across, step):
    size = jnp.sqrt(down * down + across * across)
    scale = 1.0 + step * size
    return ((first - step * down) / scale, (second - step * across) / scale)


def col_prev(field):
    return jnp.pad(field[:, :, :, :-1], ((0, 0), (0, 0), (0, 0), (1, 0)))


def col_grad(smooth, last_col):
    next_cols = jnp.pad(smooth[:, :, :, 1:], ((0, 0), (0, 0), (0, 0), (0, 1)))
    return jnp.where(last_col, 0.0, next_cols - smooth)


def body(frames, prev_fg, depth_valid, sketch, tv_weight):
    count, chans, rows, cols = frames.shape
    height = rows * lax.axis_size("pix")
    nval = chans * height * cols
    chan_ids = lax.broadcasted_iota(jnp.int32, (1, chans, 1, 1), 1)
    depth_ok = depth_valid[:, None, :, :].astype(jnp.float32)
    valid = jnp.where(chan_ids == chans - 1, depth_ok, jnp.float32(1.0))
    resid = ((frames.astype(jnp.float32) - prev_fg.astype(jnp.float32)) * valid).astype(
        jnp.bfloat16
    )
    flat = resid.reshape(count, chans * rows * cols)
    local = lax.all_to_all(flat, "frame", split_axis=1, concat_axis=0, tiled=True)
    whole_terms = pair_rows(local, local)
    gram = all_sum(all_sum(whole_terms, "frame"), "pix") / nval
    mixing = mixing_matrix(gram, sketch)
    spread = over_frames(mixing, local).astype(jnp.bfloat16)
    background = lax.all_to_all(spread, "frame", split_axis=0, concat_axis=1, tiled=True).reshape(
        count, chans, rows, cols
    )
    rounded = lax.optimization_barrier(background).astype(jnp.float32)
    source = (frames.astype(jnp.float32) - rounded) * valid
    lam = tv_weight.reshape(1, chans, 1, 1)
    step = STEP_SIZE / lam
    last_col = lax.broadcasted_iota(jnp.int32, (1, 1, 1, cols), 3) == cols - 1
    row_ids = lax.axis_index("pix") * rows + lax.broadcasted_iota(jnp.int32, (1, 1, rows, 1), 2)
    last_row = row_ids == height - 1

    def divergence(first, second):
        above = from_behind(shortened(first[:, :, -1:, :]), "pix", 1)
        prev_rows = jnp.concatenate([above, first[:, :, :-1, :]], axis=2)
        return first - prev_rows + (second - col_prev(second))

    first = jnp.zeros_like(source)
    second = jnp.zeros_like(source)
    for sweep in range(NSWEEP):
        smooth = source - lam * divergence(first, second)
        below = from_behind(shortened(smooth[:, :, :1, :]), "pix", -1)
        next_rows = jnp.concatenate([smooth[:, :, 1:, :], below], axis=2)
        down = jnp.where(last_row, 0.0, next_rows - smooth)
        across = col_grad(smooth, last_col)
        first, second = dual_update(first, second, down, across, step)
    smooth = source - lam * divergence(first, second)
    return (background, smooth.astype(jnp.bfloat16))


def solution(mesh):
    placed = (
        P("frame", None, "pix", None),
        P("frame", None, "pix", None),
        P("frame", "pix", None),
        P(),
        P(),
    )
    return jax.shard_map(
        body,
        mesh=mesh,
        in_specs=placed,
        out_specs=(P("frame", None, "pix", None), P("frame", None, "pix", None)),
        check_vma=False,
    )
```

```python
import functools

import jax
import jax.numpy as jnp
from jax import lax
from jax.experimental import pallas as pl
from jax.experimental.pallas import tpu as pltpu
from jax.sharding import PartitionSpec as P

POWER = 3
NSWEEP = 5
STEP_SIZE = 0.125
SUB = 8
LANE = 128
PACK = 16
VMEM_BYTES = 32 * 1024 * 1024


def from_behind(value, axis, steps):
    count = lax.axis_size(axis)
    leading, last = (max(0, -steps), min(count, count - steps))
    return lax.ppermute(value, axis, [(source, source + steps) for source in range(leading, last)])


def power_of_two(count):
    return count & (count - 1) == 0


def partner(index, offset, count, back=False):
    if power_of_two(count):
        return index ^ offset
    return (index + (count - offset if back else offset)) % count


def swap(value, axis, offset):
    count = lax.axis_size(axis)
    pairs = [(source, partner(source, offset, count)) for source in range(count)]
    return lax.ppermute(value, axis, pairs)


def all_sum(value, axis):
    count = lax.axis_size(axis)
    if not power_of_two(count):
        return lax.psum(value, axis)
    bit = 1
    while bit < count:
        fours = (count // bit).bit_length() % 2 == 1
        offsets = (bit, 2 * bit, 3 * bit) if fours else (bit,)
        others = [swap(value, axis, offset) for offset in offsets]
        for other in others:
            value = value + other
        bit *= len(offsets) + 1
    return value


def exact_dot(left, right, left_dim, right_dim):
    return lax.dot_general(
        left,
        right,
        (((left_dim,), (right_dim,)), ((), ())),
        precision=lax.Precision.HIGHEST,
        preferred_element_type=jnp.float32,
    )


def short_dot(left, right, left_dim, right_dim):
    return lax.dot_general(
        left,
        right,
        (((left_dim,), (right_dim,)), ((), ())),
        preferred_element_type=jnp.float32,
    )


def eliminate(square, sides):
    rank = square.shape[0]
    width = sides[0].shape[1]
    blocks = rank // SUB
    sub_ids = lax.broadcasted_iota(jnp.int32, (SUB, width), 0)
    square = jnp.concatenate([square, jnp.zeros((rank, width - rank), jnp.float32)], axis=1)

    def in_blocks(rows):
        return [rows[SUB * b : SUB * (b + 1)] for b in range(blocks)]

    def row_of(rows, j):
        return jnp.broadcast_to(rows[j : j + 1], (SUB, width))

    def col_of(rows, j):
        return jnp.broadcast_to(rows[:, j : j + 1], (SUB, width))

    square = in_blocks(square)
    sides = [in_blocks(side) for side in sides]
    solved = [[] for _ in sides]
    for k in range(blocks):
        below = range(k, blocks)
        cols = {b: [col_of(square[b], SUB * k + j) for j in range(SUB)] for b in below}
        pivots = jnp.ones((SUB, width), jnp.float32)
        for j in range(SUB):
            pivot = row_of(cols[k][j], j)
            inverse = 1.0 / pivot
            pivots = jnp.where(sub_ids == j, pivot, pivots)
            col_rows = {i: row_of(cols[k][i], j) for i in range(j + 1, SUB)}
            square_row = row_of(square[k], j)
            side_rows = [row_of(side[k], j) for side in sides]
            for b in below:
                ratio = cols[b][j] * inverse
                if b == k:
                    ratio = jnp.where(sub_ids > j, ratio, 0.0)
                for i in range(j + 1, SUB):
                    cols[b][i] = cols[b][i] - ratio * col_rows[i]
                square[b] = square[b] - ratio * square_row
                for side, side_row in zip(sides, side_rows):
                    side[b] = side[b] - ratio * side_row
        scale = lax.rsqrt(pivots)
        for rows, side in zip(solved, sides):
            rows.append(side[k] * scale)
    return [jnp.concatenate(rows, axis=0) for rows in solved]


def mixing_kernel(gram_ref, sketch_ref, mixing_ref):
    gram = gram_ref[...]
    basis = sketch_ref[...]
    for turn in range(POWER):
        image = exact_dot(basis, gram, 1, 1)
        (basis,) = eliminate(exact_dot(basis, image, 1, 1), [image])
    image = exact_dot(basis, gram, 1, 1)
    left, right = eliminate(exact_dot(basis, image, 1, 1), [basis, image])
    mixing_ref[...] = exact_dot(right, left, 0, 0).astype(mixing_ref.dtype)


def mixing_matrix(gram, sketch):
    return pl.pallas_call(
        mixing_kernel,
        out_shape=jax.ShapeDtypeStruct(gram.shape, jnp.bfloat16),
        name="mixing",
    )(gram, sketch.T)


def tile(j):
    return pl.ds(LANE * j, LANE)


def turn_frames(flat, out_ref, tiles, rows):
    nf = out_ref.shape[-2]
    for h in range(rows):
        for j in range(tiles):
            out_ref[0, h, :, tile(j)] = flat[j, pl.ds(h, nf, stride=rows), :].astype(out_ref.dtype)


def residual_kernel(last, chan_ref, frames_ref, prev_ref, valid_ref, out_ref, flat):
    nf, _, rows, cols = frames_ref.shape
    tiles = cols // LANE
    keep = jnp.where(chan_ref[0] + pl.program_id(0) == last, 0.0, 1.0)
    for f in range(nf):
        ok = jnp.where(valid_ref[f] != 0, 1.0, keep)
        diff = (frames_ref[f, 0].astype(jnp.float32) - prev_ref[f, 0].astype(jnp.float32)) * ok
        for j in range(tiles):
            flat[j, pl.ds(f * rows, rows), :] = diff[:, LANE * j : LANE * (j + 1)]
    turn_frames(flat, out_ref, tiles, rows)


def residual(channel, each, frames, prev_fg, depth_valid):
    count, chans, rows, cols = frames.shape
    image = pl.BlockSpec((PACK, 1, rows, cols), lambda c, g, first: (g, first[0] + c, 0, 0))
    return pl.pallas_call(
        functools.partial(residual_kernel, chans - 1),
        grid_spec=pltpu.PrefetchScalarGridSpec(
            num_scalar_prefetch=1,
            grid=(each, count // PACK),
            in_specs=[image, image, pl.BlockSpec((PACK, rows, cols), lambda c, g, first: (g, 0, 0))],
            out_specs=pl.BlockSpec((1, rows, PACK, cols), lambda c, g, first: (c, 0, g, 0)),
            scratch_shapes=[pltpu.VMEM((cols // LANE, PACK * rows, LANE), jnp.float32)],
        ),
        out_shape=jax.ShapeDtypeStruct((each, rows, count, cols), jnp.bfloat16),
        name="residual",
    )(channel, frames, prev_fg, depth_valid)


def interleave_kernel(frames_ref, order_ref, out_ref, flat):
    nf, _, rows, cols = frames_ref.shape
    tiles = cols // LANE
    lines = frames_ref[:, 0].reshape(nf * rows, cols)
    lines = short_dot(lines, order_ref[...], 1, 0)
    for j in range(tiles):
        flat[j] = lines[:, LANE * j : LANE * (j + 1)]
    turn_frames(flat, out_ref, tiles, rows)


def interleaved(frames, order):
    count, chans, rows, cols = frames.shape
    return pl.pallas_call(
        interleave_kernel,
        grid=(chans, count // PACK),
        in_specs=[
            pl.BlockSpec((PACK, 1, rows, cols), lambda c, g: (g, c, 0, 0)),
            pl.BlockSpec((cols, cols), lambda c, g: (0, 0)),
        ],
        out_specs=pl.BlockSpec((1, rows, PACK, cols), lambda c, g: (c, 0, g, 0)),
        out_shape=jax.ShapeDtypeStruct((chans, rows, count, cols), jnp.bfloat16),
        scratch_shapes=[pltpu.VMEM((cols // LANE, PACK * rows, LANE), jnp.float32)],
        compiler_params=pltpu.CompilerParams(vmem_limit_bytes=VMEM_BYTES),
        name="interleave",
    )(frames, order)


def gram_kernel(groups, nval, ids_ref, *refs):
    blocks, (gram_ref, all_ref) = refs[:groups], refs[groups:]
    lines, count, cols = blocks[0].shape
    for k, block in enumerate(blocks):
        start = pl.multiple_of(ids_ref[groups + k] * count, count)
        all_ref[:, pl.ds(start, count), :] = block[...]

    @pl.when(pl.program_id(0) == 0)
    def clear():
        gram_ref[...] = jnp.zeros_like(gram_ref)

    total = gram_ref[...]
    for r in range(lines):
        total = total + short_dot(all_ref[r], all_ref[r], 1, 1) / nval
    gram_ref[...] = total


def gram_terms(ids, blocks, nval):
    groups = len(blocks)
    lines, count, cols = blocks[0].shape
    some = 4 if lines % 4 == 0 else 1
    part = pl.BlockSpec((some, count, cols), lambda r, ids: (r, 0, 0))
    every = groups * count
    return pl.pallas_call(
        functools.partial(gram_kernel, groups, nval),
        grid_spec=pltpu.PrefetchScalarGridSpec(
            num_scalar_prefetch=1,
            grid=(lines // some,),
            in_specs=[part] * groups,
            out_specs=[
                pl.BlockSpec((every, every), lambda r, ids: (0, 0)),
                pl.BlockSpec((some, every, cols), lambda r, ids: (r, 0, 0)),
            ],
        ),
        out_shape=[
            jax.ShapeDtypeStruct((every, every), jnp.float32),
            jax.ShapeDtypeStruct((lines, every, cols), jnp.bfloat16),
        ],
        name="gram",
    )(ids, *blocks)


def spread_kernel(groups, ids_ref, mixing_ref, all_ref, *refs):
    pieces, order = refs[:groups], refs[groups]
    lines, count, cols = pieces[0].shape
    for k in range(groups):
        start = pl.multiple_of(ids_ref[k] * count, count)
        order[pl.ds(k * count, count), :] = mixing_ref[pl.ds(start, count), :]
    weights = order[...]
    for r in range(lines):
        back = short_dot(weights, all_ref[r], 1, 0)
        for k, piece in enumerate(pieces):
            piece[r] = back[k * count : (k + 1) * count].astype(piece.dtype)


def spread(ids, mixing, pixels, groups):
    lines, every, cols = pixels.shape
    count = every // groups
    some = 4 if lines % 4 == 0 else 1
    return pl.pallas_call(
        functools.partial(spread_kernel, groups),
        grid_spec=pltpu.PrefetchScalarGridSpec(
            num_scalar_prefetch=1,
            grid=(lines // some,),
            in_specs=[
                pl.BlockSpec((every, every), lambda r, ids: (0, 0)),
                pl.BlockSpec((some, every, cols), lambda r, ids: (r, 0, 0)),
            ],
            out_specs=[pl.BlockSpec((some, count, cols), lambda r, ids: (r, 0, 0))] * groups,
            scratch_shapes=[pltpu.VMEM((every, every), jnp.bfloat16)],
        ),
        out_shape=[jax.ShapeDtypeStruct((lines, count, cols), jnp.bfloat16)] * groups,
        name="spread",
    )(ids, mixing, pixels)


def variation_kernel(chan_ref, scale_ref, order_ref, own, above, below, *refs):
    fg_ref, bg_ref, source, first, second, flat_fg, flat_bg = refs[-7:]
    edge = NSWEEP
    _, rows, nf, cols = own[0].shape
    tiles = cols // LANE
    lines = rows + 2 * edge
    lam, up_flag, down_flag = scale_ref[0], scale_ref[1], scale_ref[2]
    depth = scale_ref[3]
    step = STEP_SIZE / lam

    for start, (frames, valid, back) in ((0, above), (edge, own), (edge + rows, below)):
        height = back.shape[0]
        moved = short_dot(back[...].reshape(height * nf, cols), order_ref[...], 1, 0)
        for h in range(height):
            image = frames[0, h].astype(jnp.float32) - moved[h * nf : (h + 1) * nf]
            source[start + h] = image * step

    @pl.when(depth > 0.0)
    def mask():
        for start, (frames, valid, back) in ((0, above), (edge, own), (edge + rows, below)):
            for h in range(back.shape[0]):
                source[start + h] = source[start + h] * valid[h].astype(jnp.float32)

    end = lax.broadcasted_iota(jnp.int32, (nf, LANE), 1) == LANE - 1

    def load(ref, i):
        return [ref[i, :, tile(j)] for j in range(tiles)]

    def divergence(over, here, beside):
        left = [pltpu.roll(beside[-1], 1, 1)] + beside[:-1]
        return [(here[j] - over[j]) + (beside[j] - left[j]) for j in range(tiles)]

    def smooth(i, over, here, beside):
        div = divergence(over, here, beside)
        image = load(source, i)
        return [image[j] - STEP_SIZE * div[j] for j in range(tiles)]

    for sweep in range(NSWEEP):
        here = beside = None
        if sweep:
            here, beside = load(first, sweep), load(second, sweep)
            now = smooth(sweep, load(first, sweep - 1), here, beside)
        else:
            now = load(source, 0)
        for i in range(sweep, lines - 1 - sweep):
            next_here = next_beside = None
            if sweep:
                next_here, next_beside = load(first, i + 1), load(second, i + 1)
                later = smooth(i + 1, here, next_here, next_beside)
            else:
                later = load(source, i + 1)
            right = now[1:] + [jnp.where(end, now[-1], pltpu.roll(now[0], LANE - 1, 1))]
            for j in range(tiles):
                down = later[j] - now[j]
                if i == edge - 1:
                    down = down * up_flag
                if i == edge + rows - 1:
                    down = down * down_flag
                across = right[j] - now[j]
                square = down * down + across * across
                size = square * lax.rsqrt(jnp.maximum(square, 1e-30))
                scale = pl.reciprocal(1.0 + size, approx=True)
                first[i, :, tile(j)] = (here[j] - down if sweep else -down) * scale
                second[i, :, tile(j)] = (beside[j] - across if sweep else -across) * scale
            now, here, beside = later, next_here, next_beside

    over = load(first, edge - 1)
    for h in range(rows):
        here, beside = load(first, edge + h), load(second, edge + h)
        image = smooth(edge + h, over, here, beside)
        for j in range(tiles):
            flat_fg[j, pl.ds(h, nf, stride=rows), :] = image[j] * (lam / STEP_SIZE)
            flat_bg[j, pl.ds(h, nf, stride=rows), :] = own[2][h, :, tile(j)].astype(jnp.float32)
        over = here
    fg = jnp.concatenate([flat_fg[j].astype(fg_ref.dtype) for j in range(tiles)], axis=1)
    fg = short_dot(fg, order_ref[...], 1, 1).astype(fg_ref.dtype)
    fg_ref[:, 0] = fg.reshape(nf, rows, cols)
    for j in range(tiles):
        bg_ref[:, 0, :, tile(j)] = flat_bg[j].astype(bg_ref.dtype).reshape(nf, rows, LANE)


def variation(channel, scales, order, own, above, below, outs, shape):
    count, chans, rows, cols = shape
    edge = NSWEEP
    lines = rows + 2 * edge

    def kernel(chan_ref, scale_ref, order_ref, *refs):
        own, above, below = refs[0:3], refs[3:6], refs[6:9]
        variation_kernel(chan_ref, scale_ref, order_ref, own, above, below, *refs[9:])

    def specs(height):
        return [
            pl.BlockSpec((1, height, PACK, cols), lambda g, chan: (chan[0], 0, g, 0)),
            pl.BlockSpec((height, PACK, cols), lambda g, chan: (0, g, 0)),
            pl.BlockSpec((height, PACK, cols), lambda g, chan: (0, g, 0)),
        ]

    image = pl.BlockSpec((PACK, 1, rows, cols), lambda g, chan: (g, chan[0], 0, 0))
    flat = pltpu.VMEM((cols // LANE, PACK * rows, LANE), jnp.float32)
    field = pltpu.VMEM((lines, PACK, cols), jnp.float32)
    work = count * chans * rows * cols // chans
    return pl.pallas_call(
        kernel,
        grid_spec=pltpu.PrefetchScalarGridSpec(
            num_scalar_prefetch=1,
            grid=(count // PACK,),
            in_specs=[
                pl.BlockSpec(memory_space=pltpu.SMEM),
                pl.BlockSpec((cols, cols), lambda g, chan: (0, 0)),
            ]
            + specs(rows)
            + specs(edge)
            + specs(edge)
            + [pl.BlockSpec(memory_space=pl.ANY)] * len(outs),
            out_specs=[image, image],
            scratch_shapes=[field, field, field, flat, flat],
        ),
        out_shape=[jax.ShapeDtypeStruct(shape, jnp.bfloat16)] * 2,
        input_output_aliases={12 + n: n for n in range(len(outs))},
        compiler_params=pltpu.CompilerParams(vmem_limit_bytes=VMEM_BYTES),
        cost_estimate=pl.CostEstimate(
            flops=work * 150, bytes_accessed=work * 12, transcendentals=work * 12
        ),
        name="variation",
    )(channel, scales, order, *own, *above, *below, *outs)


def body(frames, prev_fg, depth_valid, sketch, tv_weight):
    count, chans, rows, cols = frames.shape
    groups = lax.axis_size("frame")
    strips = lax.axis_size("pix")
    each = chans // groups
    nval = chans * rows * strips * cols
    edge = NSWEEP
    tiles = cols // LANE
    me = lax.axis_index("frame")
    targets = [partner(me, k, groups) for k in range(groups)]
    sources = [partner(me, k, groups, back=True) for k in range(groups)]
    ids = jnp.stack(targets + sources).astype(jnp.int32)

    def channel(group, c=0):
        return (group * each + c).astype(jnp.int32).reshape(1)

    resid = {
        k: residual(channel(targets[k]), each, frames, prev_fg, depth_valid)
        for k in list(range(1, groups)) + [0]
    }
    blocks = [resid[0]] + [swap(resid[k], "frame", k) for k in range(1, groups)]
    blocks = [block.reshape(each * rows, count, cols) for block in blocks]

    places = lax.broadcasted_iota(jnp.int32, (cols, cols), 1)
    places = places % LANE * tiles + places // LANE
    order = (places == lax.broadcasted_iota(jnp.int32, (cols, cols), 0)).astype(jnp.bfloat16)
    lined = interleaved(frames, order)
    valid = interleaved(depth_valid.astype(jnp.bfloat16)[:, None], order)[0]
    lined_above = from_behind(lined[:, -edge:], "pix", 1)
    lined_below = from_behind(lined[:, :edge], "pix", -1)
    valid_above = from_behind(valid[-edge:], "pix", 1)
    valid_below = from_behind(valid[:edge], "pix", -1)

    terms, pixels = gram_terms(ids, blocks, nval)
    gram = all_sum(all_sum(terms, "frame"), "pix")
    mixing = mixing_matrix(gram, sketch)
    pieces = spread(ids, mixing, pixels, groups)

    strip = lax.axis_index("pix")
    flags = [(strip > 0).astype(jnp.float32), (strip < strips - 1).astype(jnp.float32)]
    outs = []
    for k in range(groups):
        piece = swap(pieces[k], "frame", k) if k else pieces[0]
        piece = piece.reshape(each, rows, count, cols)
        from_above = from_behind(piece[:, -edge:], "pix", 1)
        from_below = from_behind(piece[:, :edge], "pix", -1)
        for c in range(each):
            chan = channel(sources[k], c)
            lam = lax.dynamic_index_in_dim(tv_weight, chan[0], keepdims=False)
            scales = jnp.stack([lam] + flags + [(chan[0] == chans - 1).astype(jnp.float32)])
            outs = variation(
                chan,
                scales,
                order,
                (lined, valid, piece[c]),
                (lined_above, valid_above, from_above[c]),
                (lined_below, valid_below, from_below[c]),
                outs,
                frames.shape,
            )
    foreground, background = outs
    return (background, foreground)


def solution(mesh):
    placed = (
        P("frame", None, "pix", None),
        P("frame", None, "pix", None),
        P("frame", "pix", None),
        P(),
        P(),
    )
    return jax.shard_map(
        body,
        mesh=mesh,
        in_specs=placed,
        out_specs=(P("frame", None, "pix", None), P("frame", None, "pix", None)),
        check_vma=False,
    )
```

```python
import functools

import jax
import jax.numpy as jnp
from jax import lax
from jax.experimental import pallas as pl
from jax.experimental.pallas import tpu as pltpu
from jax.sharding import PartitionSpec as P

POWER = 3
NSWEEP = 5
STEP_SIZE = 0.125
SUB = 8
LANE = 128
PACK = 16
VMEM_BYTES = 32 * 1024 * 1024


def from_behind(value, axis, steps):
    count = lax.axis_size(axis)
    leading, last = (max(0, -steps), min(count, count - steps))
    return lax.ppermute(value, axis, [(source, source + steps) for source in range(leading, last)])


def power_of_two(count):
    return count & (count - 1) == 0


def partner(index, offset, count, back=False):
    if power_of_two(count):
        return index ^ offset
    return (index + (count - offset if back else offset)) % count


def swap(value, axis, offset):
    count = lax.axis_size(axis)
    pairs = [(source, partner(source, offset, count)) for source in range(count)]
    return lax.ppermute(value, axis, pairs)


def all_sum(value, axis):
    count = lax.axis_size(axis)
    if not power_of_two(count):
        return lax.psum(value, axis)
    bit = 1
    while bit < count:
        fours = (count // bit).bit_length() % 2 == 1
        offsets = (bit, 2 * bit, 3 * bit) if fours else (bit,)
        others = [swap(value, axis, offset) for offset in offsets]
        for other in others:
            value = value + other
        bit *= len(offsets) + 1
    return value


def exact_dot(left, right, left_dim, right_dim):
    return lax.dot_general(
        left,
        right,
        (((left_dim,), (right_dim,)), ((), ())),
        precision=lax.Precision.HIGHEST,
        preferred_element_type=jnp.float32,
    )


def short_dot(left, right, left_dim, right_dim):
    return lax.dot_general(
        left,
        right,
        (((left_dim,), (right_dim,)), ((), ())),
        preferred_element_type=jnp.float32,
    )


def eliminate(square, sides):
    rank = square.shape[0]
    width = sides[0].shape[1]
    blocks = rank // SUB
    sub_ids = lax.broadcasted_iota(jnp.int32, (SUB, width), 0)
    square = jnp.concatenate([square, jnp.zeros((rank, width - rank), jnp.float32)], axis=1)

    def in_blocks(rows):
        return [rows[SUB * b : SUB * (b + 1)] for b in range(blocks)]

    def row_of(rows, j):
        return jnp.broadcast_to(rows[j : j + 1], (SUB, width))

    def col_of(rows, j):
        return jnp.broadcast_to(rows[:, j : j + 1], (SUB, width))

    square = in_blocks(square)
    sides = [in_blocks(side) for side in sides]
    solved = [[] for _ in sides]
    for k in range(blocks):
        below = range(k, blocks)
        cols = {b: [col_of(square[b], SUB * k + j) for j in range(SUB)] for b in below}
        pivots = jnp.ones((SUB, width), jnp.float32)
        for j in range(SUB):
            pivot = row_of(cols[k][j], j)
            inverse = 1.0 / pivot
            pivots = jnp.where(sub_ids == j, pivot, pivots)
            col_rows = {i: row_of(cols[k][i], j) for i in range(j + 1, SUB)}
            square_row = row_of(square[k], j)
            side_rows = [row_of(side[k], j) for side in sides]
            for b in below:
                ratio = cols[b][j] * inverse
                if b == k:
                    ratio = jnp.where(sub_ids > j, ratio, 0.0)
                for i in range(j + 1, SUB):
                    cols[b][i] = cols[b][i] - ratio * col_rows[i]
                square[b] = square[b] - ratio * square_row
                for side, side_row in zip(sides, side_rows):
                    side[b] = side[b] - ratio * side_row
        scale = lax.rsqrt(pivots)
        for rows, side in zip(solved, sides):
            rows.append(side[k] * scale)
    return [jnp.concatenate(rows, axis=0) for rows in solved]


def mixing_kernel(gram_ref, sketch_ref, mixing_ref):
    gram = gram_ref[...]
    basis = sketch_ref[...]
    for turn in range(POWER):
        image = exact_dot(basis, gram, 1, 1)
        (basis,) = eliminate(exact_dot(basis, image, 1, 1), [image])
    image = exact_dot(basis, gram, 1, 1)
    left, right = eliminate(exact_dot(basis, image, 1, 1), [basis, image])
    mixing_ref[...] = exact_dot(right, left, 0, 0).astype(mixing_ref.dtype)


def mixing_matrix(gram, sketch):
    return pl.pallas_call(
        mixing_kernel,
        out_shape=jax.ShapeDtypeStruct(gram.shape, jnp.bfloat16),
        name="mixing",
    )(gram, sketch.T)


def tile(j):
    return pl.ds(LANE * j, LANE)


def vmem():
    return pl.BlockSpec(memory_space=pltpu.VMEM)


def smem():
    return pl.BlockSpec(memory_space=pltpu.SMEM)


def anywhere():
    return pl.BlockSpec(memory_space=pl.ANY)


def residual_kernel(last, picks, channel_ref, frames_ref, prev_ref, valid_ref, *refs):
    outs, (now, before, ok, sems) = refs[: len(picks)], refs[len(picks) :]
    _, _, count, rows, cols = now.shape
    each = now.shape[1]
    valid_copy = pltpu.make_async_copy(valid_ref, ok, sems.at[0])
    copies = []
    for n, pick in enumerate(picks):
        for c in range(each):
            chan = channel_ref[pick] + c
            at = 1 + 2 * (n * each + c)
            copies.append(
                (
                    pltpu.make_async_copy(frames_ref.at[:, chan], now.at[n, c], sems.at[at]),
                    pltpu.make_async_copy(prev_ref.at[:, chan], before.at[n, c], sems.at[at + 1]),
                )
            )
    for copy in copies[0]:
        copy.start()
    valid_copy.start()
    for pair in copies[1:]:
        for copy in pair:
            copy.start()
    valid_copy.wait()
    for n, pick in enumerate(picks):
        for c in range(each):
            for copy in copies[n * each + c]:
                copy.wait()
            keep = jnp.where(channel_ref[pick] + c == last, 0.0, 1.0)
            for g in range(count // PACK):
                some = pl.ds(g * PACK, PACK)
                for j in range(cols // LANE):
                    valid = jnp.where(ok[some, :, tile(j)] != 0, 1.0, keep)
                    diff = now[n, c, some, :, tile(j)].astype(jnp.float32)
                    diff = diff - before[n, c, some, :, tile(j)].astype(jnp.float32)
                    turned = jnp.swapaxes(diff * valid, 0, 1)
                    outs[n][c, :, some, tile(j)] = turned.astype(jnp.bfloat16)


def residual(channels, picks, each, frames, prev_fg, depth_valid):
    count, chans, rows, cols = frames.shape
    held = pltpu.VMEM((len(picks), each, count, rows, cols), jnp.bfloat16)
    return pl.pallas_call(
        functools.partial(residual_kernel, chans - 1, picks),
        in_specs=[smem(), anywhere(), anywhere(), anywhere()],
        out_specs=[vmem()] * len(picks),
        out_shape=[jax.ShapeDtypeStruct((each, rows, count, cols), jnp.bfloat16)] * len(picks),
        scratch_shapes=[
            held,
            held,
            pltpu.VMEM((count, rows, cols), jnp.int32),
            pltpu.SemaphoreType.DMA((1 + 2 * each * len(picks),)),
        ],
        compiler_params=pltpu.CompilerParams(vmem_limit_bytes=VMEM_BYTES),
        name="residual",
    )(channels, frames, prev_fg, depth_valid)


def interleave_kernel(frames_ref, valid_ref, order_ref, out_ref, top_ref, bottom_ref):
    count, chans, rows, cols = frames_ref.shape
    edge = NSWEEP
    for c in range(chans + 1):
        for g in range(count // PACK):
            some = pl.ds(g * PACK, PACK)
            if c < chans:
                lines = frames_ref[some, c]
            else:
                lines = valid_ref[some].astype(jnp.float32).astype(jnp.bfloat16)
            lines = short_dot(lines.reshape(PACK * rows, cols), order_ref[...], 1, 0)
            for j in range(cols // LANE):
                turned = lines[:, LANE * j : LANE * (j + 1)].reshape(PACK, rows, LANE)
                turned = jnp.swapaxes(turned, 0, 1).astype(jnp.bfloat16)
                out_ref[c, :, some, tile(j)] = turned
                top_ref[c, :, some, tile(j)] = turned[:edge]
                bottom_ref[c, :, some, tile(j)] = turned[rows - edge :]


def interleaved(frames, depth_valid, order):
    count, chans, rows, cols = frames.shape
    return pl.pallas_call(
        interleave_kernel,
        in_specs=[vmem()] * 3,
        out_specs=[vmem()] * 3,
        out_shape=[
            jax.ShapeDtypeStruct((chans + 1, height, count, cols), jnp.bfloat16)
            for height in (rows, NSWEEP, NSWEEP)
        ],
        compiler_params=pltpu.CompilerParams(vmem_limit_bytes=VMEM_BYTES),
        name="interleave",
    )(frames, depth_valid, order)


def gram_kernel(groups, nval, ids_ref, *refs):
    blocks, (gram_ref, all_ref) = refs[:groups], refs[-2:]
    lines, count, cols = blocks[0].shape
    for k, block in enumerate(blocks):
        start = pl.multiple_of(ids_ref[groups + k] * count, count)
        all_ref[:, pl.ds(start, count), :] = block[...]
    total = jnp.zeros(gram_ref.shape, jnp.float32)
    for r in range(lines):
        total = total + short_dot(all_ref[r], all_ref[r], 1, 1)
    gram_ref[...] = total / nval


def gram_terms(ids, blocks, nval, after):
    groups = len(blocks)
    lines, count, cols = blocks[0].shape
    every = groups * count
    return pl.pallas_call(
        functools.partial(gram_kernel, groups, nval),
        in_specs=[smem()] + [vmem()] * groups + [anywhere()] * len(after),
        out_specs=[vmem()] * 2,
        out_shape=[
            jax.ShapeDtypeStruct((every, every), jnp.float32),
            jax.ShapeDtypeStruct((lines, every, cols), jnp.bfloat16),
        ],
        compiler_params=pltpu.CompilerParams(vmem_limit_bytes=VMEM_BYTES),
        name="gram",
    )(ids, *blocks, *after)


def spread_kernel(picks, edges, n_after, ids_ref, mixing_ref, all_ref, *refs):
    refs = refs[n_after:]
    pieces, weights = refs[: len(picks)], refs[-1]
    lines, count, cols = pieces[0].shape
    for n, pick in enumerate(picks):
        start = pl.multiple_of(ids_ref[pick] * count, count)
        weights[pl.ds(n * count, count), :] = mixing_ref[pl.ds(start, count), :]
    chosen = weights[...]
    for r in range(lines):
        back = short_dot(chosen, all_ref[r], 1, 0).astype(jnp.bfloat16)
        for n, piece in enumerate(pieces):
            piece[r] = back[n * count : (n + 1) * count]
    if edges:
        each, edge = refs[len(picks)].shape[:2]
        rows = lines // each
        for c in range(each):
            refs[len(picks)][c] = pieces[0][c * rows : c * rows + edge]
            refs[len(picks) + 1][c] = pieces[0][(c + 1) * rows - edge : (c + 1) * rows]


def spread(ids, picks, mixing, pixels, groups, each, edges=False, after=()):
    lines, every, cols = pixels.shape
    count = every // groups
    piece = jax.ShapeDtypeStruct((lines, count, cols), jnp.bfloat16)
    rim = jax.ShapeDtypeStruct((each, NSWEEP, count, cols), jnp.bfloat16)
    shapes = [piece] * len(picks) + [rim] * (2 if edges else 0)
    return pl.pallas_call(
        functools.partial(spread_kernel, picks, edges, len(after)),
        in_specs=[smem(), vmem(), vmem()] + [anywhere()] * len(after),
        out_specs=[vmem()] * len(shapes),
        out_shape=shapes,
        scratch_shapes=[pltpu.VMEM((len(picks) * count, every), jnp.bfloat16)],
        compiler_params=pltpu.CompilerParams(vmem_limit_bytes=VMEM_BYTES),
        name="spread",
    )(ids, mixing, pixels, *after)


def rims_kernel(count, *refs):
    pieces, (top_ref, bottom_ref) = refs[:count], refs[-2:]
    edge = top_ref.shape[1]
    at = 0
    for piece in pieces:
        for c in range(piece.shape[0]):
            top_ref[at] = piece[c, :edge]
            bottom_ref[at] = piece[c, piece.shape[1] - edge :]
            at += 1


def rims(pieces, after):
    each, _, count, cols = pieces[0].shape
    rim = jax.ShapeDtypeStruct((each * len(pieces), NSWEEP, count, cols), jnp.bfloat16)
    return pl.pallas_call(
        functools.partial(rims_kernel, len(pieces)),
        in_specs=[vmem()] * len(pieces) + [anywhere()] * len(after),
        out_specs=[vmem()] * 2,
        out_shape=[rim, rim],
        name="rims",
    )(*pieces, *after)


def variation_kernel(n_after, scale_ref, at_ref, order_ref, *refs):
    own, above, below = refs[0:2], refs[2:4], refs[4:6]
    fg_out, bg_out, token_ref, source, first, second, flat_fg, flat_bg, fg_held, bg_held, sems = refs[
        6 + n_after :
    ]
    chan, rim, each_at = at_ref[0], at_ref[1], at_ref[2]
    edge = NSWEEP
    nf = PACK
    _, rows, count, cols = own[1].shape
    chans = own[0].shape[0] - 1
    tiles = cols // LANE
    lines = rows + 2 * edge
    lam, up_flag, down_flag = scale_ref[0], scale_ref[1], scale_ref[2]
    step = STEP_SIZE / lam
    end = lax.broadcasted_iota(jnp.int32, (nf, LANE), 1) == LANE - 1
    strips = ((0, above, rim), (edge, own, each_at), (edge + rows, below, rim))
    token_ref[...] = jnp.zeros_like(token_ref)

    def load(ref, i):
        return [ref[i, :, tile(j)] for j in range(tiles)]

    def divergence(over, here, beside):
        left = [pltpu.roll(beside[-1], 1, 1)] + beside[:-1]
        return [(here[j] - over[j]) + (beside[j] - left[j]) for j in range(tiles)]

    def smooth(i, over, here, beside):
        div = divergence(over, here, beside)
        image = load(source, i)
        return [image[j] - STEP_SIZE * div[j] for j in range(tiles)]

    @pl.loop(0, count // nf)
    def some_frames(g):
        some = pl.ds(pl.multiple_of(g * nf, nf), nf)
        copies = [
            pltpu.make_async_copy(held.at[g], out.at[some, chan], sems.at[n, g])
            for n, (held, out) in enumerate(((fg_held, fg_out), (bg_held, bg_out)))
        ]
        for h in range(rows):
            for j in range(tiles):
                back = own[1][each_at, h, some, tile(j)].astype(jnp.float32)
                flat_bg[j, pl.ds(h, nf, stride=rows), :] = back
        for j in range(tiles):
            bg_held[g, :, :, tile(j)] = flat_bg[j].astype(jnp.bfloat16).reshape(nf, rows, LANE)
        copies[1].start()

        for start, (frames, back), at in strips:
            height = back.shape[1]
            moved = back[at, :, some, :].reshape(height * nf, cols)
            moved = short_dot(moved, order_ref[...], 1, 0)
            for h in range(height):
                image = frames[chan, h, some, :].astype(jnp.float32)
                source[start + h] = (image - moved[h * nf : (h + 1) * nf]) * step

        @pl.when(chan == chans - 1)
        def mask():
            for start, (frames, back), at in strips:
                for h in range(back.shape[1]):
                    valid = frames[chans, h, some, :].astype(jnp.float32)
                    source[start + h] = source[start + h] * valid

        for sweep in range(NSWEEP):
            here = beside = None
            if sweep:
                here, beside = load(first, sweep), load(second, sweep)
                now = smooth(sweep, load(first, sweep - 1), here, beside)
            else:
                now = load(source, 0)
            for i in range(sweep, lines - 1 - sweep):
                next_here = next_beside = None
                if sweep:
                    next_here, next_beside = load(first, i + 1), load(second, i + 1)
                    later = smooth(i + 1, here, next_here, next_beside)
                else:
                    later = load(source, i + 1)
                right = now[1:] + [jnp.where(end, now[-1], pltpu.roll(now[0], LANE - 1, 1))]
                for j in range(tiles):
                    down = later[j] - now[j]
                    if i == edge - 1:
                        down = down * up_flag
                    if i == edge + rows - 1:
                        down = down * down_flag
                    across = right[j] - now[j]
                    square = down * down + across * across
                    size = square * lax.rsqrt(jnp.maximum(square, 1e-30))
                    scale = pl.reciprocal(1.0 + size, approx=True)
                    first[i, :, tile(j)] = (here[j] - down if sweep else -down) * scale
                    second[i, :, tile(j)] = (beside[j] - across if sweep else -across) * scale
                now, here, beside = later, next_here, next_beside

        over = load(first, edge - 1)
        for h in range(rows):
            here, beside = load(first, edge + h), load(second, edge + h)
            image = smooth(edge + h, over, here, beside)
            for j in range(tiles):
                flat_fg[j, pl.ds(h, nf, stride=rows), :] = image[j] * (lam / STEP_SIZE)
            over = here
        fg = jnp.concatenate([flat_fg[j].astype(jnp.bfloat16) for j in range(tiles)], axis=1)
        fg = short_dot(fg, order_ref[...], 1, 1).astype(jnp.bfloat16)
        fg_held[g] = fg.reshape(nf, rows, cols)
        copies[0].start()

    for g in range(count // nf):
        for n, (held, out) in enumerate(((fg_held, fg_out), (bg_held, bg_out))):
            pltpu.make_async_copy(held.at[g], out.at[pl.ds(g * nf, nf), chan], sems.at[n, g]).wait()


def variation(scales, at, order, own, above, below, outs, after, shape):
    count, chans, rows, cols = shape
    lines = rows + 2 * NSWEEP
    flat = pltpu.VMEM((cols // LANE, PACK * rows, LANE), jnp.float32)
    field = pltpu.VMEM((lines, PACK, cols), jnp.float32)
    held = pltpu.VMEM((count // PACK, PACK, rows, cols), jnp.bfloat16)
    work = count * rows * cols
    return pl.pallas_call(
        functools.partial(variation_kernel, len(outs) + len(after)),
        in_specs=[smem(), smem()] + [vmem()] * 7 + [anywhere()] * (len(outs) + len(after)),
        out_specs=[anywhere(), anywhere(), vmem()],
        out_shape=[jax.ShapeDtypeStruct(shape, jnp.bfloat16)] * 2
        + [jax.ShapeDtypeStruct((SUB, LANE), jnp.float32)],
        scratch_shapes=[
            field,
            field,
            field,
            flat,
            flat,
            held,
            held,
            pltpu.SemaphoreType.DMA((2, count // PACK)),
        ],
        input_output_aliases={9 + n: n for n in range(len(outs))},
        compiler_params=pltpu.CompilerParams(vmem_limit_bytes=VMEM_BYTES),
        cost_estimate=pl.CostEstimate(
            flops=work * 250, bytes_accessed=work * 12, transcendentals=work * 12
        ),
        name="variation",
    )(scales, at, order, *own, *above, *below, *outs, *after)


def body(frames, prev_fg, depth_valid, sketch, tv_weight):
    count, chans, rows, cols = frames.shape
    groups = lax.axis_size("frame")
    strips = lax.axis_size("pix")
    each = chans // groups
    nval = chans * rows * strips * cols
    tiles = cols // LANE
    me = lax.axis_index("frame")
    targets = [partner(me, k, groups) for k in range(groups)]
    sources = [partner(me, k, groups, back=True) for k in range(groups)]
    ids = jnp.stack(targets + sources).astype(jnp.int32)
    near = [k for k in range(1, groups) if power_of_two(k)]
    far = [k for k in range(1, groups) if not power_of_two(k)]

    first_channels = ids * each
    resid = {}
    for picks in (near, far + [0]):
        parts = residual(first_channels, picks, each, frames, prev_fg, depth_valid)
        resid.update(zip(picks, parts))
    blocks = [resid[0]] + [swap(resid[k], "frame", k) for k in range(1, groups)]
    blocks = [block.reshape(each * rows, count, cols) for block in blocks]

    places = lax.broadcasted_iota(jnp.int32, (cols, cols), 1)
    places = places % LANE * tiles + places // LANE
    order = (places == lax.broadcasted_iota(jnp.int32, (cols, cols), 0)).astype(jnp.bfloat16)
    lined, top, bottom = interleaved(frames, depth_valid, order)
    lined_above = from_behind(bottom, "pix", 1)
    lined_below = from_behind(top, "pix", -1)

    terms, pixels = gram_terms(ids, blocks, nval, (lined_above, lined_below))
    gram = all_sum(all_sum(terms, "frame"), "pix")
    mixing = mixing_matrix(gram, sketch)

    strip = lax.axis_index("pix")
    flags = [(strip > 0).astype(jnp.float32), (strip < strips - 1).astype(jnp.float32)]
    outs, token = [], None

    def strips_of(piece):
        return piece.reshape(each, rows, count, cols)

    def around(top, bottom):
        return from_behind(bottom, "pix", 1), from_behind(top, "pix", -1)

    def work_on(k, piece, from_above, from_below, at, after, outs):
        for c in range(each):
            chan = sources[k] * each + c
            lam = lax.dynamic_index_in_dim(tv_weight, chan, keepdims=False)
            *outs, token = variation(
                jnp.stack([lam] + flags),
                jnp.stack([chan, at + c, c]).astype(jnp.int32),
                order,
                (lined, piece),
                (lined_above, from_above),
                (lined_below, from_below),
                outs,
                after,
                frames.shape,
            )
        return outs, token

    *pieces, top, bottom = spread(ids, [0] + near, mixing, pixels, groups, each, edges=True)
    arrived = {k: swap(pieces[1 + n], "frame", k) for n, k in enumerate(near)}
    own = around(top, bottom)
    outs, token = work_on(0, strips_of(pieces[0]), *own, 0, (), outs)
    for stage in (near, far):
        if not stage:
            continue
        if stage is far:
            pieces = spread(ids, far, mixing, pixels, groups, each, after=tuple(arrived.values()))
            arrived = {k: swap(piece, "frame", k) for k, piece in zip(far, pieces)}
        held = [strips_of(arrived[k]) for k in stage]
        from_above, from_below = around(*rims(held, (token,)))
        for n, k in enumerate(stage):
            outs, done = work_on(k, held[n], from_above, from_below, n * each, (), outs)
            token = done if n == 0 else token
    foreground, background = outs
    return (background, foreground)


def solution(mesh):
    placed = (
        P("frame", None, "pix", None),
        P("frame", None, "pix", None),
        P("frame", "pix", None),
        P(),
        P(),
    )
    return jax.shard_map(
        body,
        mesh=mesh,
        in_specs=placed,
        out_specs=(P("frame", None, "pix", None), P("frame", None, "pix", None)),
        check_vma=False,
    )
```

```python
import functools
import math

import jax
import jax.numpy as jnp
from jax import lax
from jax.experimental import pallas as pl
from jax.experimental.pallas import tpu as pltpu
from jax.sharding import PartitionSpec as P

POWER = 3
NSWEEP = 5
STEP_SIZE = 0.125
SUB = 8
LANE = 128
PACK = 16
SPARE_BYTES = 12 * 1024 * 1024


def from_behind(value, axis, steps):
    count = lax.axis_size(axis)
    leading, last = (max(0, -steps), min(count, count - steps))
    return lax.ppermute(value, axis, [(source, source + steps) for source in range(leading, last)])


def power_of_two(count):
    return count & (count - 1) == 0


def partner(index, offset, count, back=False):
    if power_of_two(count):
        return index ^ offset
    return (index + (count - offset if back else offset)) % count


def swap(value, axis, offset):
    count = lax.axis_size(axis)
    pairs = [(source, partner(source, offset, count)) for source in range(count)]
    return lax.ppermute(value, axis, pairs)


def all_sum(value, axis):
    count = lax.axis_size(axis)
    if not power_of_two(count):
        return lax.psum(value, axis)
    bit = 1
    while bit < count:
        fours = (count // bit).bit_length() % 2 == 1
        offsets = (bit, 2 * bit, 3 * bit) if fours else (bit,)
        others = [swap(value, axis, offset) for offset in offsets]
        for other in others:
            value = value + other
        bit *= len(offsets) + 1
    return value


def exact_dot(left, right, left_dim, right_dim):
    return lax.dot_general(
        left,
        right,
        (((left_dim,), (right_dim,)), ((), ())),
        precision=lax.Precision.HIGHEST,
        preferred_element_type=jnp.float32,
    )


def short_dot(left, right, left_dim, right_dim):
    return lax.dot_general(
        left,
        right,
        (((left_dim,), (right_dim,)), ((), ())),
        preferred_element_type=jnp.float32,
    )


def eliminate(square, sides):
    rank = square.shape[0]
    width = sides[0].shape[1]
    blocks = rank // SUB
    sub_ids = lax.broadcasted_iota(jnp.int32, (SUB, width), 0)
    square = jnp.concatenate([square, jnp.zeros((rank, width - rank), jnp.float32)], axis=1)

    def in_blocks(rows):
        return [rows[SUB * b : SUB * (b + 1)] for b in range(blocks)]

    def row_of(rows, j):
        return jnp.broadcast_to(rows[j : j + 1], (SUB, width))

    def col_of(rows, j):
        return jnp.broadcast_to(rows[:, j : j + 1], (SUB, width))

    square = in_blocks(square)
    sides = [in_blocks(side) for side in sides]
    solved = [[] for _ in sides]
    for k in range(blocks):
        below = range(k, blocks)
        cols = {b: [col_of(square[b], SUB * k + j) for j in range(SUB)] for b in below}
        pivots = jnp.ones((SUB, width), jnp.float32)
        for j in range(SUB):
            pivot = row_of(cols[k][j], j)
            inverse = 1.0 / pivot
            pivots = jnp.where(sub_ids == j, pivot, pivots)
            col_rows = {i: row_of(cols[k][i], j) for i in range(j + 1, SUB)}
            square_row = row_of(square[k], j)
            side_rows = [row_of(side[k], j) for side in sides]
            for b in below:
                ratio = cols[b][j] * inverse
                if b == k:
                    ratio = jnp.where(sub_ids > j, ratio, 0.0)
                for i in range(j + 1, SUB):
                    cols[b][i] = cols[b][i] - ratio * col_rows[i]
                square[b] = square[b] - ratio * square_row
                for side, side_row in zip(sides, side_rows):
                    side[b] = side[b] - ratio * side_row
        scale = lax.rsqrt(pivots)
        for rows, side in zip(solved, sides):
            rows.append(side[k] * scale)
    return [jnp.concatenate(rows, axis=0) for rows in solved]


def mixing_kernel(gram_ref, sketch_ref, mixing_ref):
    gram = gram_ref[...]
    basis = sketch_ref[...]
    for turn in range(POWER):
        image = exact_dot(basis, gram, 1, 1)
        (basis,) = eliminate(exact_dot(basis, image, 1, 1), [image])
    image = exact_dot(basis, gram, 1, 1)
    left, right = eliminate(exact_dot(basis, image, 1, 1), [basis, image])
    mixing_ref[...] = exact_dot(right, left, 0, 0).astype(mixing_ref.dtype)


def mixing_matrix(gram, sketch):
    return pl.pallas_call(
        mixing_kernel,
        out_shape=jax.ShapeDtypeStruct(gram.shape, jnp.bfloat16),
        cost_estimate=cost(10.6),
        name="mixing",
    )(gram, sketch.T)


def tile(j):
    return pl.ds(LANE * j, LANE)


def vmem():
    return pl.BlockSpec(memory_space=pltpu.VMEM)


def smem():
    return pl.BlockSpec(memory_space=pltpu.SMEM)


def anywhere():
    return pl.BlockSpec(memory_space=pl.ANY)


def room(*scratch):
    held = sum(math.prod(ref.shape) * jnp.dtype(ref.dtype).itemsize for ref in scratch)
    return pltpu.CompilerParams(vmem_limit_bytes=SPARE_BYTES + held)


def cost(micros):
    return pl.CostEstimate(flops=0, bytes_accessed=int(micros * 3.6e6), transcendentals=0)


def residual_kernel(last, channel_ref, frames_ref, prev_ref, valid_ref, *outs):
    pick, c = pl.program_id(0), pl.program_id(1)
    cols = frames_ref.shape[-1]
    keep = jnp.where(channel_ref[pick] + c == last, 0.0, 1.0)
    for j in range(cols // LANE):
        valid = jnp.where(valid_ref[:, :, tile(j)] != 0, 1.0, keep)
        diff = frames_ref[:, 0, :, tile(j)].astype(jnp.float32)
        diff = diff - prev_ref[:, 0, :, tile(j)].astype(jnp.float32)
        turned = jnp.swapaxes(diff * valid, 0, 1).astype(jnp.bfloat16)
        for n, out in enumerate(outs):

            @pl.when(pick == n)
            def write(out=out, turned=turned, j=j):
                out[0, :, :, tile(j)] = turned


def residual(channels, each, frames, prev_fg, depth_valid):
    count, chans, rows, cols = frames.shape
    picks = channels.shape[0]
    halves = count // PACK

    def image_at(p, c, g, first):
        return (g, first[p] + c, 0, 0)

    def valid_at(p, c, g, first):
        return (jnp.where(first[p] + c == chans - 1, g, 0), 0, 0)

    def out_at(n, p, c, g, first):
        early, late = p < n, p > n
        c = jnp.where(early, 0, jnp.where(late, each - 1, c))
        g = jnp.where(early, 0, jnp.where(late, halves - 1, g))
        return (c, 0, g, 0)

    image = pl.BlockSpec((PACK, 1, rows, cols), image_at)
    return pl.pallas_call(
        functools.partial(residual_kernel, chans - 1),
        grid_spec=pltpu.PrefetchScalarGridSpec(
            num_scalar_prefetch=1,
            grid=(picks, each, halves),
            in_specs=[image, image, pl.BlockSpec((PACK, rows, cols), valid_at)],
            out_specs=[
                pl.BlockSpec((1, rows, PACK, cols), functools.partial(out_at, n)) for n in range(picks)
            ],
        ),
        out_shape=[jax.ShapeDtypeStruct((each, rows, count, cols), jnp.bfloat16)] * picks,
        cost_estimate=cost(1.5),
        name="residual",
    )(channels, frames, prev_fg, depth_valid)


def interleave_kernel(frames_ref, valid_ref, order_ref, *refs):
    out_ref, top_ref, bottom_ref = refs[-3:]
    count, chans, rows, cols = frames_ref.shape
    edge = NSWEEP
    for c in range(chans + 1):
        for g in range(count // PACK):
            some = pl.ds(g * PACK, PACK)
            if c < chans:
                lines = frames_ref[some, c]
            else:
                lines = valid_ref[some].astype(jnp.float32).astype(jnp.bfloat16)
            lines = short_dot(lines.reshape(PACK * rows, cols), order_ref[...], 1, 0)
            for j in range(cols // LANE):
                turned = lines[:, LANE * j : LANE * (j + 1)].reshape(PACK, rows, LANE)
                turned = jnp.swapaxes(turned, 0, 1).astype(jnp.bfloat16)
                out_ref[c, :, some, tile(j)] = turned
                top_ref[c, :, some, tile(j)] = turned[:edge]
                bottom_ref[c, :, some, tile(j)] = turned[rows - edge :]


def interleaved(frames, depth_valid, order, after):
    count, chans, rows, cols = frames.shape
    return pl.pallas_call(
        interleave_kernel,
        in_specs=[vmem()] * 3 + [anywhere()] * len(after),
        out_specs=[vmem()] * 3,
        out_shape=[
            jax.ShapeDtypeStruct((chans + 1, height, count, cols), jnp.bfloat16)
            for height in (rows, NSWEEP, NSWEEP)
        ],
        compiler_params=room(),
        cost_estimate=cost(3.3),
        name="interleave",
    )(frames, depth_valid, order, *after)


def gram_kernel(groups, each, nval, ids_ref, *refs):
    blocks, (gram_ref, all_ref, top_ref, bottom_ref) = refs[:groups], refs[-4:]
    lines, count, cols = blocks[0].shape
    for k, block in enumerate(blocks):
        start = pl.multiple_of(ids_ref[groups + k] * count, count)
        all_ref[:, pl.ds(start, count), :] = block[...]
    rows = lines // each
    for c in range(each):
        top_ref[c] = all_ref[c * rows : c * rows + NSWEEP]
        bottom_ref[c] = all_ref[(c + 1) * rows - NSWEEP : (c + 1) * rows]
    total = jnp.zeros(gram_ref.shape, jnp.float32)
    for r in range(lines):
        total = total + short_dot(all_ref[r], all_ref[r], 1, 1)
    gram_ref[...] = total / nval


def gram_terms(ids, blocks, each, nval, after):
    groups = len(blocks)
    lines, count, cols = blocks[0].shape
    every = groups * count
    return pl.pallas_call(
        functools.partial(gram_kernel, groups, each, nval),
        in_specs=[smem()] + [vmem()] * groups + [anywhere()] * len(after),
        out_specs=[vmem()] * 4,
        out_shape=[
            jax.ShapeDtypeStruct((every, every), jnp.float32),
            jax.ShapeDtypeStruct((lines, every, cols), jnp.bfloat16),
            jax.ShapeDtypeStruct((each, NSWEEP, every, cols), jnp.bfloat16),
            jax.ShapeDtypeStruct((each, NSWEEP, every, cols), jnp.bfloat16),
        ],
        compiler_params=room(),
        cost_estimate=cost(1.4),
        name="gram",
    )(ids, *blocks, *after)


def spread_kernel(ids_ref, mixing_ref, all_ref, above_ref, below_ref, *refs):
    pieces, weights = refs[:-1], refs[-1]
    each, lines, count, cols = pieces[0].shape
    rows = lines - 2 * NSWEEP
    for k in range(len(pieces)):
        start = pl.multiple_of(ids_ref[k] * count, count)
        weights[pl.ds(k * count, count), :] = mixing_ref[pl.ds(start, count), :]
    chosen = weights[...]
    for c in range(each):
        for at in range(lines):
            if at < NSWEEP:
                pixels = above_ref[c, at]
            elif at < NSWEEP + rows:
                pixels = all_ref[c * rows + at - NSWEEP]
            else:
                pixels = below_ref[c, at - NSWEEP - rows]
            back = short_dot(chosen, pixels, 1, 0).astype(jnp.bfloat16)
            for k, piece in enumerate(pieces):
                piece[c, at] = back[k * count : (k + 1) * count]


def spread(ids, mixing, pixels, above, below, groups):
    lines, every, cols = pixels.shape
    each = above.shape[0]
    count = every // groups
    piece = jax.ShapeDtypeStruct((each, lines // each + 2 * NSWEEP, count, cols), jnp.bfloat16)
    return pl.pallas_call(
        spread_kernel,
        in_specs=[smem()] + [vmem()] * 4,
        out_specs=[vmem()] * groups,
        out_shape=[piece] * groups,
        scratch_shapes=[pltpu.VMEM((every, every), jnp.bfloat16)],
        compiler_params=room(),
        cost_estimate=cost(2.5),
        name="spread",
    )(ids, mixing, pixels, above, below)


def gate_kernel(*refs):
    pass


def gate(value, after):
    return pl.pallas_call(
        gate_kernel,
        in_specs=[anywhere()] * (1 + len(after)),
        out_specs=anywhere(),
        out_shape=jax.ShapeDtypeStruct(value.shape, value.dtype),
        input_output_aliases={0: 0},
        name="gate",
    )(value, *after)


def variation_kernel(n_after, scale_ref, at_ref, order_ref, *refs):
    own, above, below, back_ref = refs[:4]
    fg_out, bg_out, token_ref, source, first, second, flat_fg, flat_bg, fg_held, bg_held, sems = refs[
        4 + n_after :
    ]
    chan, at = at_ref[0], at_ref[1]
    edge = NSWEEP
    nf = PACK
    chans, rows, count, cols = own.shape
    chans -= 1
    tiles = cols // LANE
    lines = rows + 2 * edge
    lam, up_flag, down_flag = scale_ref[0], scale_ref[1], scale_ref[2]
    step = STEP_SIZE / lam
    end = lax.broadcasted_iota(jnp.int32, (nf, LANE), 1) == LANE - 1
    strips = ((0, above), (edge, own), (edge + rows, below))
    token_ref[...] = jnp.zeros_like(token_ref)

    def load(ref, i):
        return [ref[i, :, tile(j)] for j in range(tiles)]

    def divergence(over, here, beside):
        left = [pltpu.roll(beside[-1], 1, 1)] + beside[:-1]
        return [(here[j] - over[j]) + (beside[j] - left[j]) for j in range(tiles)]

    def smooth(i, over, here, beside):
        div = divergence(over, here, beside)
        image = load(source, i)
        return [image[j] - STEP_SIZE * div[j] for j in range(tiles)]

    @pl.loop(0, count // nf)
    def some_frames(g):
        some = pl.ds(pl.multiple_of(g * nf, nf), nf)
        copies = [
            pltpu.make_async_copy(held.at[g], out.at[some, chan], sems.at[n, g])
            for n, (held, out) in enumerate(((fg_held, fg_out), (bg_held, bg_out)))
        ]
        for h in range(rows):
            for j in range(tiles):
                back = back_ref[at, edge + h, some, tile(j)].astype(jnp.float32)
                flat_bg[j, pl.ds(h, nf, stride=rows), :] = back
        for j in range(tiles):
            bg_held[g, :, :, tile(j)] = flat_bg[j].astype(jnp.bfloat16).reshape(nf, rows, LANE)
        copies[1].start()

        moved = back_ref[at, :, some, :].reshape(lines * nf, cols)
        moved = short_dot(moved, order_ref[...], 1, 0)
        for start, frames in strips:
            for h in range(frames.shape[1]):
                image = frames[chan, h, some, :].astype(jnp.float32)
                source[start + h] = (image - moved[(start + h) * nf : (start + h + 1) * nf]) * step

        @pl.when(chan == chans - 1)
        def mask():
            for start, frames in strips:
                for h in range(frames.shape[1]):
                    valid = frames[chans, h, some, :].astype(jnp.float32)
                    source[start + h] = source[start + h] * valid

        for sweep in range(NSWEEP):
            here = beside = None
            if sweep:
                here, beside = load(first, sweep), load(second, sweep)
                now = smooth(sweep, load(first, sweep - 1), here, beside)
            else:
                now = load(source, 0)
            for i in range(sweep, lines - 1 - sweep):
                next_here = next_beside = None
                if sweep:
                    next_here, next_beside = load(first, i + 1), load(second, i + 1)
                    later = smooth(i + 1, here, next_here, next_beside)
                else:
                    later = load(source, i + 1)
                right = now[1:] + [jnp.where(end, now[-1], pltpu.roll(now[0], LANE - 1, 1))]
                for j in range(tiles):
                    down = later[j] - now[j]
                    if i == edge - 1:
                        down = down * up_flag
                    if i == edge + rows - 1:
                        down = down * down_flag
                    across = right[j] - now[j]
                    square = down * down + across * across
                    size = square * lax.rsqrt(jnp.maximum(square, 1e-30))
                    scale = pl.reciprocal(1.0 + size, approx=True)
                    first[i, :, tile(j)] = (here[j] - down if sweep else -down) * scale
                    second[i, :, tile(j)] = (beside[j] - across if sweep else -across) * scale
                now, here, beside = later, next_here, next_beside

        over = load(first, edge - 1)
        for h in range(rows):
            here, beside = load(first, edge + h), load(second, edge + h)
            image = smooth(edge + h, over, here, beside)
            for j in range(tiles):
                flat_fg[j, pl.ds(h, nf, stride=rows), :] = image[j] * (lam / STEP_SIZE)
            over = here
        fg = jnp.concatenate([flat_fg[j].astype(jnp.bfloat16) for j in range(tiles)], axis=1)
        fg = short_dot(fg, order_ref[...], 1, 1).astype(jnp.bfloat16)
        fg_held[g] = fg.reshape(nf, rows, cols)
        copies[0].start()

    for g in range(count // nf):
        for n, (held, out) in enumerate(((fg_held, fg_out), (bg_held, bg_out))):
            pltpu.make_async_copy(held.at[g], out.at[pl.ds(g * nf, nf), chan], sems.at[n, g]).wait()


def variation(scales, at, order, own, above, below, back, outs, after, shape):
    count, chans, rows, cols = shape
    lines = rows + 2 * NSWEEP
    flat = pltpu.VMEM((cols // LANE, PACK * rows, LANE), jnp.float32)
    field = pltpu.VMEM((lines, PACK, cols), jnp.float32)
    held = pltpu.VMEM((count // PACK, PACK, rows, cols), jnp.bfloat16)
    return pl.pallas_call(
        functools.partial(variation_kernel, len(outs) + len(after)),
        in_specs=[smem(), smem()] + [vmem()] * 5 + [anywhere()] * (len(outs) + len(after)),
        out_specs=[anywhere(), anywhere(), vmem()],
        out_shape=[jax.ShapeDtypeStruct(shape, jnp.bfloat16)] * 2
        + [jax.ShapeDtypeStruct((SUB, LANE), jnp.float32)],
        scratch_shapes=[
            field,
            field,
            field,
            flat,
            flat,
            held,
            held,
            pltpu.SemaphoreType.DMA((2, count // PACK)),
        ],
        input_output_aliases={7 + n: n for n in range(len(outs))},
        compiler_params=room(field, field, field, flat, flat, held, held),
        cost_estimate=cost(8.5),
        name="variation",
    )(scales, at, order, own, above, below, back, *outs, *after)


def body(frames, prev_fg, depth_valid, sketch, tv_weight):
    count, chans, rows, cols = frames.shape
    groups = lax.axis_size("frame")
    strips = lax.axis_size("pix")
    each = chans // groups
    nval = chans * rows * strips * cols
    tiles = cols // LANE
    me = lax.axis_index("frame")
    targets = [partner(me, k, groups) for k in range(groups)]
    sources = [partner(me, k, groups, back=True) for k in range(groups)]
    ids = jnp.stack(targets + sources).astype(jnp.int32)
    near = [k for k in range(1, groups) if power_of_two(k)]
    far = [k for k in range(1, groups) if not power_of_two(k)]

    resid = {}
    for picks in (near, far + [0]):
        channels = jnp.stack([targets[k] * each for k in picks]).astype(jnp.int32)
        resid.update(zip(picks, residual(channels, each, frames, prev_fg, depth_valid)))
    blocks = [resid[0]] + [swap(resid[k], "frame", k) for k in range(1, groups)]
    blocks = [block.reshape(each * rows, count, cols) for block in blocks]

    places = lax.broadcasted_iota(jnp.int32, (cols, cols), 1)
    places = places % LANE * tiles + places // LANE
    order = (places == lax.broadcasted_iota(jnp.int32, (cols, cols), 0)).astype(jnp.bfloat16)
    lined, top, bottom = interleaved(frames, depth_valid, order, tuple(resid.values()))
    got = tuple(blocks[k] for k in near)
    lined_above = from_behind(gate(bottom, got), "pix", 1)
    lined_below = from_behind(gate(top, got), "pix", -1)

    after = (lined_above, lined_below)
    terms, pixels, top, bottom = gram_terms(ids, blocks, each, nval, after)
    above = from_behind(bottom, "pix", 1)
    below = from_behind(top, "pix", -1)
    gram = all_sum(all_sum(terms, "frame"), "pix")
    mixing = mixing_matrix(gram, sketch)
    pieces = spread(ids, mixing, pixels, above, below, groups)
    arrived = {0: pieces[0]}
    for k in near:
        arrived[k] = swap(pieces[k], "frame", k)

    strip = lax.axis_index("pix")
    flags = [(strip > 0).astype(jnp.float32), (strip < strips - 1).astype(jnp.float32)]
    outs = []
    for k in [0] + near + far:
        for c in range(each):
            chan = sources[k] * each + c
            lam = lax.dynamic_index_in_dim(tv_weight, chan, keepdims=False)
            *outs, token = variation(
                jnp.stack([lam] + flags),
                jnp.stack([chan, c]).astype(jnp.int32),
                order,
                lined,
                lined_above,
                lined_below,
                arrived[k],
                outs,
                (),
                frames.shape,
            )
        if k == 0:
            for other in far:
                held = gate(pieces[other], (token,) + tuple(arrived[one] for one in near))
                arrived[other] = swap(held, "frame", other)
    foreground, background = outs
    return (background, foreground)


def solution(mesh):
    placed = (
        P("frame", None, "pix", None),
        P("frame", None, "pix", None),
        P("frame", "pix", None),
        P(),
        P(),
    )
    return jax.shard_map(
        body,
        mesh=mesh,
        in_specs=placed,
        out_specs=(P("frame", None, "pix", None), P("frame", None, "pix", None)),
        check_vma=False,
    )
```

```python
import functools
import math

import jax
import jax.numpy as jnp
from jax import lax
from jax.experimental import pallas as pl
from jax.experimental.pallas import tpu as pltpu
from jax.sharding import PartitionSpec as P

POWER = 3
NSWEEP = 5
STEP_SIZE = 0.125
SUB = 8
LANE = 128
PACK = 16
SPARE_BYTES = 7 * 1024 * 1024
MOST_BYTES = 58 * 1024 * 1024


def from_behind(value, axis, steps):
    count = lax.axis_size(axis)
    leading, last = (max(0, -steps), min(count, count - steps))
    return lax.ppermute(value, axis, [(source, source + steps) for source in range(leading, last)])


def power_of_two(count):
    return count & (count - 1) == 0


def partner(index, offset, count, back=False):
    if power_of_two(count):
        return index ^ offset
    return (index + (count - offset if back else offset)) % count


def swap(value, axis, offset):
    count = lax.axis_size(axis)
    pairs = [(source, partner(source, offset, count)) for source in range(count)]
    return lax.ppermute(value, axis, pairs)


def all_sum(value, axis):
    count = lax.axis_size(axis)
    if not power_of_two(count):
        return lax.psum(value, axis)
    bit = 1
    while bit < count:
        fours = (count // bit).bit_length() % 2 == 1
        offsets = (bit, 2 * bit, 3 * bit) if fours else (bit,)
        others = [swap(value, axis, offset) for offset in offsets]
        for other in others:
            value = value + other
        bit *= len(offsets) + 1
    return value


def exact_dot(left, right, left_dim, right_dim):
    return lax.dot_general(
        left,
        right,
        (((left_dim,), (right_dim,)), ((), ())),
        precision=lax.Precision.HIGHEST,
        preferred_element_type=jnp.float32,
    )


def short_dot(left, right, left_dim, right_dim):
    return lax.dot_general(
        left,
        right,
        (((left_dim,), (right_dim,)), ((), ())),
        preferred_element_type=jnp.float32,
    )


def eliminate(square, sides):
    rank = square.shape[0]
    width = sides[0].shape[1]
    blocks = rank // SUB
    sub_ids = lax.broadcasted_iota(jnp.int32, (SUB, width), 0)
    square = jnp.concatenate([square, jnp.zeros((rank, width - rank), jnp.float32)], axis=1)

    def in_blocks(rows):
        return [rows[SUB * b : SUB * (b + 1)] for b in range(blocks)]

    def row_of(rows, j):
        return jnp.broadcast_to(rows[j : j + 1], (SUB, width))

    def col_of(rows, j):
        return jnp.broadcast_to(rows[:, j : j + 1], (SUB, width))

    square = in_blocks(square)
    sides = [in_blocks(side) for side in sides]
    solved = [[] for _ in sides]
    for k in range(blocks):
        below = range(k, blocks)
        cols = {b: [col_of(square[b], SUB * k + j) for j in range(SUB)] for b in below}
        pivots = jnp.ones((SUB, width), jnp.float32)
        for j in range(SUB):
            pivot = row_of(cols[k][j], j)
            inverse = 1.0 / pivot
            pivots = jnp.where(sub_ids == j, pivot, pivots)
            col_rows = {i: row_of(cols[k][i], j) for i in range(j + 1, SUB)}
            square_row = row_of(square[k], j)
            side_rows = [row_of(side[k], j) for side in sides]
            for b in below:
                ratio = cols[b][j] * inverse
                if b == k:
                    ratio = jnp.where(sub_ids > j, ratio, 0.0)
                for i in range(j + 1, SUB):
                    cols[b][i] = cols[b][i] - ratio * col_rows[i]
                square[b] = square[b] - ratio * square_row
                for side, side_row in zip(sides, side_rows):
                    side[b] = side[b] - ratio * side_row
        scale = lax.rsqrt(pivots)
        for rows, side in zip(solved, sides):
            rows.append(side[k] * scale)
    return [jnp.concatenate(rows, axis=0) for rows in solved]


def mixing_kernel(gram_ref, sketch_ref, mixing_ref):
    gram = gram_ref[...]
    basis = sketch_ref[...]
    for turn in range(POWER):
        image = exact_dot(basis, gram, 1, 1)
        (basis,) = eliminate(exact_dot(basis, image, 1, 1), [image])
    image = exact_dot(basis, gram, 1, 1)
    left, right = eliminate(exact_dot(basis, image, 1, 1), [basis, image])
    mixing_ref[...] = exact_dot(right, left, 0, 0).astype(mixing_ref.dtype)


def mixing_matrix(gram, sketch):
    return pl.pallas_call(
        mixing_kernel,
        out_shape=jax.ShapeDtypeStruct(gram.shape, jnp.bfloat16),
        compiler_params=room(),
        cost_estimate=cost(10.6),
        name="mixing",
    )(gram, sketch.T)


def tile(j):
    return pl.ds(LANE * j, LANE)


def vmem():
    return pl.BlockSpec(memory_space=pltpu.VMEM)


def smem():
    return pl.BlockSpec(memory_space=pltpu.SMEM)


def anywhere():
    return pl.BlockSpec(memory_space=pl.ANY)


def room(*scratch):
    held = sum(math.prod(ref.shape) * jnp.dtype(ref.dtype).itemsize for ref in scratch)
    return pltpu.CompilerParams(vmem_limit_bytes=SPARE_BYTES + held)


def cost(micros):
    return pl.CostEstimate(flops=0, bytes_accessed=int(micros * 3.6e6), transcendentals=0)


def residual_kernel(last, picks, info_ref, frames_ref, prev_ref, valid_ref, *refs):
    outs, (now, before, ok, sems) = refs[: len(picks)], refs[len(picks) :]
    _, each, count, rows, cols = now.shape
    valid_copy = pltpu.make_async_copy(valid_ref, ok, sems.at[0])
    copies = []
    for n, pick in enumerate(picks):
        for c in range(each):
            chan = info_ref[pick] * each + c
            at = 1 + 2 * (n * each + c)
            copies.append(
                (
                    pltpu.make_async_copy(frames_ref.at[:, chan], now.at[n, c], sems.at[at]),
                    pltpu.make_async_copy(prev_ref.at[:, chan], before.at[n, c], sems.at[at + 1]),
                )
            )
    for copy in copies[0]:
        copy.start()
    valid_copy.start()
    for pair in copies[1:]:
        for copy in pair:
            copy.start()
    valid_copy.wait()
    for n, pick in enumerate(picks):
        for c in range(each):
            for copy in copies[n * each + c]:
                copy.wait()
            keep = jnp.where(info_ref[pick] * each + c == last, 0.0, 1.0)
            for g in range(count // PACK):
                some = pl.ds(g * PACK, PACK)
                for j in range(cols // LANE):
                    valid = jnp.where(ok[some, :, tile(j)] != 0, 1.0, keep)
                    diff = now[n, c, some, :, tile(j)].astype(jnp.float32)
                    diff = diff - before[n, c, some, :, tile(j)].astype(jnp.float32)
                    turned = jnp.swapaxes(diff * valid, 0, 1)
                    outs[n][c, :, some, tile(j)] = turned.astype(jnp.bfloat16)


def residual(info, picks, each, frames, prev_fg, depth_valid):
    count, chans, rows, cols = frames.shape
    held = pltpu.VMEM((len(picks), each, count, rows, cols), jnp.bfloat16)
    return pl.pallas_call(
        functools.partial(residual_kernel, chans - 1, picks),
        in_specs=[smem()] + [anywhere()] * 3,
        out_specs=[vmem()] * len(picks),
        out_shape=[jax.ShapeDtypeStruct((each, rows, count, cols), jnp.bfloat16)] * len(picks),
        scratch_shapes=[
            held,
            held,
            pltpu.VMEM((count, rows, cols), jnp.int32),
            pltpu.SemaphoreType.DMA((1 + 2 * each * len(picks),)),
        ],
        compiler_params=pltpu.CompilerParams(vmem_limit_bytes=MOST_BYTES),
        cost_estimate=cost(3.0),
        name="residual",
    )(info, frames, prev_fg, depth_valid)


def interleave_kernel(frames_ref, valid_ref, order_ref, *refs):
    out_ref, top_ref, bottom_ref = refs[-3:]
    count, chans, rows, cols = frames_ref.shape
    edge = NSWEEP
    for c in range(chans + 1):
        for g in range(count // PACK):
            some = pl.ds(g * PACK, PACK)
            if c < chans:
                lines = frames_ref[some, c]
            else:
                lines = valid_ref[some].astype(jnp.float32).astype(jnp.bfloat16)
            lines = short_dot(lines.reshape(PACK * rows, cols), order_ref[...], 1, 0)
            for j in range(cols // LANE):
                turned = lines[:, LANE * j : LANE * (j + 1)].reshape(PACK, rows, LANE)
                turned = jnp.swapaxes(turned, 0, 1).astype(jnp.bfloat16)
                out_ref[c, :, some, tile(j)] = turned
                top_ref[c, :, some, tile(j)] = turned[:edge]
                bottom_ref[c, :, some, tile(j)] = turned[rows - edge :]


def interleaved(frames, depth_valid, order, after):
    count, chans, rows, cols = frames.shape
    return pl.pallas_call(
        interleave_kernel,
        in_specs=[vmem()] * 3 + [anywhere()] * len(after),
        out_specs=[vmem()] * 3,
        out_shape=[
            jax.ShapeDtypeStruct((chans + 1, height, count, cols), jnp.bfloat16)
            for height in (rows, NSWEEP, NSWEEP)
        ],
        compiler_params=room(),
        cost_estimate=cost(3.3),
        name="interleave",
    )(frames, depth_valid, order, *after)


def gram_kernel(groups, each, nval, ids_ref, *refs):
    blocks, (gram_ref, all_ref, top_ref, bottom_ref) = refs[:groups], refs[-4:]
    lines, count, cols = blocks[0].shape
    for k, block in enumerate(blocks):
        start = pl.multiple_of(ids_ref[groups + k] * count, count)
        all_ref[:, pl.ds(start, count), :] = block[...]
    rows = lines // each
    for c in range(each):
        top_ref[c] = all_ref[c * rows : c * rows + NSWEEP]
        bottom_ref[c] = all_ref[(c + 1) * rows - NSWEEP : (c + 1) * rows]
    total = jnp.zeros(gram_ref.shape, jnp.float32)
    for r in range(lines):
        total = total + short_dot(all_ref[r], all_ref[r], 1, 1)
    gram_ref[...] = total / nval


def gram_terms(ids, blocks, each, nval, after):
    groups = len(blocks)
    lines, count, cols = blocks[0].shape
    every = groups * count
    return pl.pallas_call(
        functools.partial(gram_kernel, groups, each, nval),
        in_specs=[smem()] + [vmem()] * groups + [anywhere()] * len(after),
        out_specs=[vmem()] * 4,
        out_shape=[
            jax.ShapeDtypeStruct((every, every), jnp.float32),
            jax.ShapeDtypeStruct((lines, every, cols), jnp.bfloat16),
            jax.ShapeDtypeStruct((each, NSWEEP, every, cols), jnp.bfloat16),
            jax.ShapeDtypeStruct((each, NSWEEP, every, cols), jnp.bfloat16),
        ],
        compiler_params=room(),
        cost_estimate=cost(1.4),
        name="gram",
    )(ids, *blocks, *after)


def spread_kernel(ids_ref, mixing_ref, all_ref, above_ref, below_ref, *refs):
    pieces, weights = refs[:-1], refs[-1]
    each, lines, count, cols = pieces[0].shape
    rows = lines - 2 * NSWEEP
    for k in range(len(pieces)):
        start = pl.multiple_of(ids_ref[k] * count, count)
        weights[pl.ds(k * count, count), :] = mixing_ref[pl.ds(start, count), :]
    chosen = weights[...]
    for c in range(each):
        for at in range(lines):
            if at < NSWEEP:
                pixels = above_ref[c, at]
            elif at < NSWEEP + rows:
                pixels = all_ref[c * rows + at - NSWEEP]
            else:
                pixels = below_ref[c, at - NSWEEP - rows]
            back = short_dot(chosen, pixels, 1, 0).astype(jnp.bfloat16)
            for k, piece in enumerate(pieces):
                piece[c, at] = back[k * count : (k + 1) * count]


def spread(ids, mixing, pixels, above, below, groups):
    lines, every, cols = pixels.shape
    each = above.shape[0]
    count = every // groups
    piece = jax.ShapeDtypeStruct((each, lines // each + 2 * NSWEEP, count, cols), jnp.bfloat16)
    return pl.pallas_call(
        spread_kernel,
        in_specs=[smem()] + [vmem()] * 4,
        out_specs=[vmem()] * groups,
        out_shape=[piece] * groups,
        scratch_shapes=[pltpu.VMEM((every, every), jnp.bfloat16)],
        compiler_params=room(),
        cost_estimate=cost(2.5),
        name="spread",
    )(ids, mixing, pixels, above, below)


def gate_kernel(*refs):
    pass


def gate(value, after):
    return pl.pallas_call(
        gate_kernel,
        in_specs=[anywhere()] * (1 + len(after)),
        out_specs=anywhere(),
        out_shape=jax.ShapeDtypeStruct(value.shape, value.dtype),
        input_output_aliases={0: 0},
        compiler_params=room(),
        name="gate",
    )(value, *after)


def variation_kernel(pick, at, each, n_after, info_ref, weight_ref, order_ref, *refs):
    own, above, below, back_ref = refs[:4]
    fg_out, bg_out, token_ref, source, first, second, flat_fg, flat_bg, fg_held, bg_held, sems = refs[
        4 + n_after :
    ]
    groups = (info_ref.shape[0] - 2) // 2
    chan = info_ref[groups + pick] * each + at
    edge = NSWEEP
    nf = PACK
    chans, rows, count, cols = own.shape
    chans -= 1
    tiles = cols // LANE
    lines = rows + 2 * edge
    lam = weight_ref[chan]
    up_flag = info_ref[2 * groups].astype(jnp.float32)
    down_flag = info_ref[2 * groups + 1].astype(jnp.float32)
    step = STEP_SIZE / lam
    end = lax.broadcasted_iota(jnp.int32, (nf, LANE), 1) == LANE - 1
    strips = ((0, above), (edge, own), (edge + rows, below))
    token_ref[...] = jnp.zeros_like(token_ref)

    def load(ref, i):
        return [ref[i, :, tile(j)] for j in range(tiles)]

    def divergence(over, here, beside):
        left = [pltpu.roll(beside[-1], 1, 1)] + beside[:-1]
        return [(here[j] - over[j]) + (beside[j] - left[j]) for j in range(tiles)]

    def smooth(i, over, here, beside):
        div = divergence(over, here, beside)
        image = load(source, i)
        return [image[j] - STEP_SIZE * div[j] for j in range(tiles)]

    @pl.loop(0, count // nf)
    def some_frames(g):
        some = pl.ds(pl.multiple_of(g * nf, nf), nf)
        copies = [
            pltpu.make_async_copy(held.at[g], out.at[some, chan], sems.at[n, g])
            for n, (held, out) in enumerate(((fg_held, fg_out), (bg_held, bg_out)))
        ]
        for h in range(rows):
            for j in range(tiles):
                back = back_ref[at, edge + h, some, tile(j)].astype(jnp.float32)
                flat_bg[j, pl.ds(h, nf, stride=rows), :] = back
        for j in range(tiles):
            bg_held[g, :, :, tile(j)] = flat_bg[j].astype(jnp.bfloat16).reshape(nf, rows, LANE)
        copies[1].start()

        moved = back_ref[at, :, some, :].reshape(lines * nf, cols)
        moved = short_dot(moved, order_ref[...], 1, 0)
        for start, frames in strips:
            for h in range(frames.shape[1]):
                image = frames[chan, h, some, :].astype(jnp.float32)
                source[start + h] = (image - moved[(start + h) * nf : (start + h + 1) * nf]) * step

        @pl.when(chan == chans - 1)
        def mask():
            for start, frames in strips:
                for h in range(frames.shape[1]):
                    valid = frames[chans, h, some, :].astype(jnp.float32)
                    source[start + h] = source[start + h] * valid

        for sweep in range(NSWEEP):
            here = beside = None
            if sweep:
                here, beside = load(first, sweep), load(second, sweep)
                now = smooth(sweep, load(first, sweep - 1), here, beside)
            else:
                now = load(source, 0)
            for i in range(sweep, lines - 1 - sweep):
                next_here = next_beside = None
                if sweep:
                    next_here, next_beside = load(first, i + 1), load(second, i + 1)
                    later = smooth(i + 1, here, next_here, next_beside)
                else:
                    later = load(source, i + 1)
                right = now[1:] + [jnp.where(end, now[-1], pltpu.roll(now[0], LANE - 1, 1))]
                for j in range(tiles):
                    down = later[j] - now[j]
                    if i == edge - 1:
                        down = down * up_flag
                    if i == edge + rows - 1:
                        down = down * down_flag
                    across = right[j] - now[j]
                    square = down * down + across * across
                    size = square * lax.rsqrt(jnp.maximum(square, 1e-30))
                    scale = pl.reciprocal(1.0 + size, approx=True)
                    first[i, :, tile(j)] = (here[j] - down if sweep else -down) * scale
                    second[i, :, tile(j)] = (beside[j] - across if sweep else -across) * scale
                now, here, beside = later, next_here, next_beside

        over = load(first, edge - 1)
        for h in range(rows):
            here, beside = load(first, edge + h), load(second, edge + h)
            image = smooth(edge + h, over, here, beside)
            for j in range(tiles):
                flat_fg[j, pl.ds(h, nf, stride=rows), :] = image[j] * (lam / STEP_SIZE)
            over = here
        fg = jnp.concatenate([flat_fg[j].astype(jnp.bfloat16) for j in range(tiles)], axis=1)
        fg = short_dot(fg, order_ref[...], 1, 1).astype(jnp.bfloat16)
        fg_held[g] = fg.reshape(nf, rows, cols)
        copies[0].start()

    for g in range(count // nf):
        for n, (held, out) in enumerate(((fg_held, fg_out), (bg_held, bg_out))):
            pltpu.make_async_copy(held.at[g], out.at[pl.ds(g * nf, nf), chan], sems.at[n, g]).wait()


def variation(info, weights, pick, at, order, own, above, below, back, outs, shape):
    count, chans, rows, cols = shape
    lines = rows + 2 * NSWEEP
    each = back.shape[0]
    flat = pltpu.VMEM((cols // LANE, PACK * rows, LANE), jnp.float32)
    field = pltpu.VMEM((lines, PACK, cols), jnp.float32)
    held = pltpu.VMEM((count // PACK, PACK, rows, cols), jnp.bfloat16)
    return pl.pallas_call(
        functools.partial(variation_kernel, pick, at, each, len(outs)),
        in_specs=[smem(), smem()] + [vmem()] * 5 + [anywhere()] * len(outs),
        out_specs=[anywhere(), anywhere(), vmem()],
        out_shape=[jax.ShapeDtypeStruct(shape, jnp.bfloat16)] * 2
        + [jax.ShapeDtypeStruct((SUB, LANE), jnp.float32)],
        scratch_shapes=[
            field,
            field,
            field,
            flat,
            flat,
            held,
            held,
            pltpu.SemaphoreType.DMA((2, count // PACK)),
        ],
        input_output_aliases={7 + n: n for n in range(len(outs))},
        compiler_params=room(field, field, field, flat, flat, held, held),
        cost_estimate=cost(8.5),
        name="variation",
    )(info, weights, order, own, above, below, back, *outs)


def body(frames, prev_fg, depth_valid, sketch, tv_weight):
    count, chans, rows, cols = frames.shape
    groups = lax.axis_size("frame")
    strips = lax.axis_size("pix")
    each = chans // groups
    nval = chans * rows * strips * cols
    tiles = cols // LANE
    me, strip = lax.axis_index("frame"), lax.axis_index("pix")
    targets = [partner(me, k, groups) for k in range(groups)]
    sources = [partner(me, k, groups, back=True) for k in range(groups)]
    ends = [strip > 0, strip < strips - 1]
    info = jnp.stack([jnp.asarray(one, jnp.int32) for one in targets + sources + ends])
    near = [k for k in range(1, groups) if power_of_two(k)]
    far = [k for k in range(1, groups) if not power_of_two(k)]

    resid = {}
    for picks in (near, far + [0]):
        resid.update(zip(picks, residual(info, picks, each, frames, prev_fg, depth_valid)))
    blocks = [resid[0]] + [swap(resid[k], "frame", k) for k in range(1, groups)]
    blocks = [block.reshape(each * rows, count, cols) for block in blocks]

    places = lax.broadcasted_iota(jnp.int32, (cols, cols), 1)
    places = places % LANE * tiles + places // LANE
    order = (places == lax.broadcasted_iota(jnp.int32, (cols, cols), 0)).astype(jnp.bfloat16)
    lined, top, bottom = interleaved(frames, depth_valid, order, tuple(resid.values()))
    lined_above = from_behind(bottom, "pix", 1)
    lined_below = from_behind(top, "pix", -1)

    terms, pixels, top, bottom = gram_terms(info, blocks, each, nval, ())
    gram = gate(all_sum(terms, "frame"), (lined_above, lined_below))
    gram = all_sum(gram, "pix")
    above = from_behind(gate(bottom, (gram,)), "pix", 1)
    below = from_behind(gate(top, (gram,)), "pix", -1)
    mixing = mixing_matrix(gram, sketch)
    pieces = spread(info, mixing, pixels, above, below, groups)
    arrived = {0: pieces[0]}
    for k in near:
        arrived[k] = swap(pieces[k], "frame", k)

    outs = []
    for k in [0] + near + far:
        for c in range(each):
            *outs, token = variation(
                info,
                tv_weight,
                k,
                c,
                order,
                lined,
                lined_above,
                lined_below,
                arrived[k],
                outs,
                frames.shape,
            )
        if k == 0:
            for other in far:
                held = gate(pieces[other], (token,) + tuple(arrived[one] for one in near))
                arrived[other] = swap(held, "frame", other)
    foreground, background = outs
    return (background, foreground)


def solution(mesh):
    placed = (
        P("frame", None, "pix", None),
        P("frame", None, "pix", None),
        P("frame", "pix", None),
        P(),
        P(),
    )
    return jax.shard_map(
        body,
        mesh=mesh,
        in_specs=placed,
        out_specs=(P("frame", None, "pix", None), P("frame", None, "pix", None)),
        check_vma=False,
    )
```

```python
import functools
import math

import jax
import jax.numpy as jnp
from jax import lax
from jax.experimental import pallas as pl
from jax.experimental.pallas import tpu as pltpu
from jax.sharding import PartitionSpec as P

POWER = 3
NSWEEP = 5
STEP_SIZE = 0.125
SUB = 8
LANE = 128
PACK = 16
SPARE_BYTES = 7 * 1024 * 1024
MOST_BYTES = 58 * 1024 * 1024


def power_of_two(count):
    return count & (count - 1) == 0


def partner(index, offset, count, back=False):
    if power_of_two(count):
        return index ^ offset
    return (index + (count - offset if back else offset)) % count


def pair_swap(value, axis, start):
    count = lax.axis_size(axis)
    pairs = []
    for lower in range(start, count - 1, 2):
        pairs += [(lower, lower + 1), (lower + 1, lower)]
    return lax.ppermute(value, axis, pairs)


def rims_swapped(rims):
    return [pair_swap(rim, "pix", start) for start, rim in enumerate(rims)]


def swap(value, axis, offset):
    count = lax.axis_size(axis)
    pairs = [(source, partner(source, offset, count)) for source in range(count)]
    return lax.ppermute(value, axis, pairs)


def all_sum(value, axis):
    count = lax.axis_size(axis)
    if not power_of_two(count):
        return lax.psum(value, axis)
    bit = 1
    while bit < count:
        fours = (count // bit).bit_length() % 2 == 1
        offsets = (bit, 2 * bit, 3 * bit) if fours else (bit,)
        others = [swap(value, axis, offset) for offset in offsets]
        for other in others:
            value = value + other
        bit *= len(offsets) + 1
    return value


def exact_dot(left, right, left_dim, right_dim):
    return lax.dot_general(
        left,
        right,
        (((left_dim,), (right_dim,)), ((), ())),
        precision=lax.Precision.HIGHEST,
        preferred_element_type=jnp.float32,
    )


def short_dot(left, right, left_dim, right_dim):
    return lax.dot_general(
        left,
        right,
        (((left_dim,), (right_dim,)), ((), ())),
        preferred_element_type=jnp.float32,
    )


def eliminate(square, sides):
    rank = square.shape[0]
    width = sides[0].shape[1]
    blocks = rank // SUB
    sub_ids = lax.broadcasted_iota(jnp.int32, (SUB, width), 0)
    square = jnp.concatenate([square, jnp.zeros((rank, width - rank), jnp.float32)], axis=1)

    def in_blocks(rows):
        return [rows[SUB * b : SUB * (b + 1)] for b in range(blocks)]

    def row_of(rows, j):
        return jnp.broadcast_to(rows[j : j + 1], (SUB, width))

    def col_of(rows, j):
        return jnp.broadcast_to(rows[:, j : j + 1], (SUB, width))

    square = in_blocks(square)
    sides = [in_blocks(side) for side in sides]
    solved = [[] for _ in sides]
    for k in range(blocks):
        below = range(k, blocks)
        cols = {b: [col_of(square[b], SUB * k + j) for j in range(SUB)] for b in below}
        pivots = jnp.ones((SUB, width), jnp.float32)
        for j in range(SUB):
            pivot = row_of(cols[k][j], j)
            inverse = 1.0 / pivot
            pivots = jnp.where(sub_ids == j, pivot, pivots)
            col_rows = {i: row_of(cols[k][i], j) for i in range(j + 1, SUB)}
            square_row = row_of(square[k], j)
            side_rows = [row_of(side[k], j) for side in sides]
            for b in below:
                ratio = cols[b][j] * inverse
                if b == k:
                    ratio = jnp.where(sub_ids > j, ratio, 0.0)
                for i in range(j + 1, SUB):
                    cols[b][i] = cols[b][i] - ratio * col_rows[i]
                square[b] = square[b] - ratio * square_row
                for side, side_row in zip(sides, side_rows):
                    side[b] = side[b] - ratio * side_row
        scale = lax.rsqrt(pivots)
        for rows, side in zip(solved, sides):
            rows.append(side[k] * scale)
    return [jnp.concatenate(rows, axis=0) for rows in solved]


def mixing_kernel(gram_ref, sketch_ref, mixing_ref):
    gram = gram_ref[...]
    basis = sketch_ref[...]
    for turn in range(POWER):
        image = exact_dot(basis, gram, 1, 1)
        (basis,) = eliminate(exact_dot(basis, image, 1, 1), [image])
    image = exact_dot(basis, gram, 1, 1)
    left, right = eliminate(exact_dot(basis, image, 1, 1), [basis, image])
    mixing_ref[...] = exact_dot(right, left, 0, 0).astype(mixing_ref.dtype)


def mixing_matrix(gram, sketch):
    return pl.pallas_call(
        mixing_kernel,
        out_shape=jax.ShapeDtypeStruct(gram.shape, jnp.bfloat16),
        compiler_params=room(),
        cost_estimate=cost(10.6),
        name="mixing",
    )(gram, sketch.T)


def tile(j):
    return pl.ds(LANE * j, LANE)


def vmem():
    return pl.BlockSpec(memory_space=pltpu.VMEM)


def smem():
    return pl.BlockSpec(memory_space=pltpu.SMEM)


def anywhere():
    return pl.BlockSpec(memory_space=pl.ANY)


def room(*scratch):
    held = sum(math.prod(ref.shape) * jnp.dtype(ref.dtype).itemsize for ref in scratch)
    return pltpu.CompilerParams(vmem_limit_bytes=SPARE_BYTES + held)


def cost(micros):
    return pl.CostEstimate(flops=0, bytes_accessed=int(micros * 3.6e6), transcendentals=0)


def residual_kernel(last, picks, info_ref, frames_ref, prev_ref, valid_ref, *refs):
    outs, (now, before, ok, sems) = refs[: len(picks)], refs[len(picks) :]
    _, each, count, rows, cols = now.shape
    valid_copy = pltpu.make_async_copy(valid_ref, ok, sems.at[0])
    copies = []
    for n, pick in enumerate(picks):
        for c in range(each):
            chan = info_ref[pick] * each + c
            at = 1 + 2 * (n * each + c)
            copies.append(
                (
                    pltpu.make_async_copy(frames_ref.at[:, chan], now.at[n, c], sems.at[at]),
                    pltpu.make_async_copy(prev_ref.at[:, chan], before.at[n, c], sems.at[at + 1]),
                )
            )
    for copy in copies[0]:
        copy.start()
    valid_copy.start()
    for pair in copies[1:]:
        for copy in pair:
            copy.start()
    valid_copy.wait()
    for n, pick in enumerate(picks):
        for c in range(each):
            for copy in copies[n * each + c]:
                copy.wait()
            keep = jnp.where(info_ref[pick] * each + c == last, 0.0, 1.0)
            for g in range(count // PACK):
                some = pl.ds(g * PACK, PACK)
                for j in range(cols // LANE):
                    valid = jnp.where(ok[some, :, tile(j)] != 0, 1.0, keep)
                    diff = now[n, c, some, :, tile(j)].astype(jnp.float32)
                    diff = diff - before[n, c, some, :, tile(j)].astype(jnp.float32)
                    turned = jnp.swapaxes(diff * valid, 0, 1)
                    outs[n][c, :, some, tile(j)] = turned.astype(jnp.bfloat16)


def residual(info, picks, each, frames, prev_fg, depth_valid):
    count, chans, rows, cols = frames.shape
    held = pltpu.VMEM((len(picks), each, count, rows, cols), jnp.bfloat16)
    return pl.pallas_call(
        functools.partial(residual_kernel, chans - 1, picks),
        in_specs=[smem()] + [anywhere()] * 3,
        out_specs=[vmem()] * len(picks),
        out_shape=[jax.ShapeDtypeStruct((each, rows, count, cols), jnp.bfloat16)] * len(picks),
        scratch_shapes=[
            held,
            held,
            pltpu.VMEM((count, rows, cols), jnp.int32),
            pltpu.SemaphoreType.DMA((1 + 2 * each * len(picks),)),
        ],
        compiler_params=pltpu.CompilerParams(vmem_limit_bytes=MOST_BYTES),
        cost_estimate=cost(3.0),
        name="residual",
    )(info, frames, prev_fg, depth_valid)


def interleave_kernel(info_ref, frames_ref, valid_ref, order_ref, *refs):
    out_ref, rims = refs[-3], refs[-2:]
    odd = info_ref[info_ref.shape[0] - 1]
    count, chans, rows, cols = frames_ref.shape
    for c in range(chans + 1):
        for g in range(count // PACK):
            some = pl.ds(g * PACK, PACK)
            if c < chans:
                lines = frames_ref[some, c]
            else:
                lines = valid_ref[some].astype(jnp.float32).astype(jnp.bfloat16)
            lines = short_dot(lines.reshape(PACK * rows, cols), order_ref[...], 1, 0)
            for j in range(cols // LANE):
                turned = lines[:, LANE * j : LANE * (j + 1)].reshape(PACK, rows, LANE)
                turned = jnp.swapaxes(turned, 0, 1).astype(jnp.bfloat16)
                out_ref[c, :, some, tile(j)] = turned
    write_rims(rims, odd, lambda h: out_ref[:, h], rows)


def write_rims(rims, odd, read, rows, axis_rows=NSWEEP):
    first = jnp.where(odd != 0, 0, rows - axis_rows)
    for h in range(axis_rows):
        rims[0][:, h] = read(first + h)
        rims[1][:, h] = read(rows - axis_rows - first + h)


def interleaved(info, frames, depth_valid, order, after):
    count, chans, rows, cols = frames.shape
    return pl.pallas_call(
        interleave_kernel,
        in_specs=[smem()] + [vmem()] * 3 + [anywhere()] * len(after),
        out_specs=[vmem()] * 3,
        out_shape=[
            jax.ShapeDtypeStruct((chans + 1, height, count, cols), jnp.bfloat16)
            for height in (rows, NSWEEP, NSWEEP)
        ],
        compiler_params=room(),
        cost_estimate=cost(3.3),
        name="interleave",
    )(info, frames, depth_valid, order, *after)


def gram_kernel(groups, each, nval, ids_ref, *refs):
    blocks, (gram_ref, all_ref), rims = refs[:groups], refs[-4:-2], refs[-2:]
    lines, count, cols = blocks[0].shape
    for k, block in enumerate(blocks):
        start = pl.multiple_of(ids_ref[groups + k] * count, count)
        all_ref[:, pl.ds(start, count), :] = block[...]
    rows = lines // each
    odd = ids_ref[ids_ref.shape[0] - 1]
    for c in range(each):
        some = [rim.at[pl.ds(c, 1)] for rim in rims]
        write_rims(some, odd, lambda h, c=c: all_ref[pl.ds(c * rows + h, 1)], rows)
    total = jnp.zeros(gram_ref.shape, jnp.float32)
    for r in range(lines):
        total = total + short_dot(all_ref[r], all_ref[r], 1, 1)
    gram_ref[...] = total / nval


def gram_terms(ids, blocks, each, nval, after):
    groups = len(blocks)
    lines, count, cols = blocks[0].shape
    every = groups * count
    return pl.pallas_call(
        functools.partial(gram_kernel, groups, each, nval),
        in_specs=[smem()] + [vmem()] * groups + [anywhere()] * len(after),
        out_specs=[vmem()] * 4,
        out_shape=[
            jax.ShapeDtypeStruct((every, every), jnp.float32),
            jax.ShapeDtypeStruct((lines, every, cols), jnp.bfloat16),
            jax.ShapeDtypeStruct((each, NSWEEP, every, cols), jnp.bfloat16),
            jax.ShapeDtypeStruct((each, NSWEEP, every, cols), jnp.bfloat16),
        ],
        compiler_params=room(),
        cost_estimate=cost(1.4),
        name="gram",
    )(ids, *blocks, *after)


def spread_kernel(picks, ids_ref, mixing_ref, all_ref, *refs):
    rims, pieces, weights = refs[:2], refs[2:-1], refs[-1]
    odd = ids_ref[ids_ref.shape[0] - 1] != 0
    each, lines, _, cols = pieces[0].shape
    halves = len(pieces) // len(picks)
    count = halves * PACK
    rows = lines - 2 * NSWEEP
    for k, pick in enumerate(picks):
        start = pl.multiple_of(ids_ref[pick] * count, count)
        weights[pl.ds(k * count, count), :] = mixing_ref[pl.ds(start, count), :]
    chosen = weights[...]
    for c in range(each):
        for at in range(lines):
            h = at - NSWEEP
            if h < 0:
                pixels = jnp.where(odd, rims[0][c, at], rims[1][c, at])
            elif h < rows:
                pixels = all_ref[c * rows + h]
            else:
                pixels = jnp.where(odd, rims[1][c, h - rows], rims[0][c, h - rows])
            back = short_dot(chosen, pixels, 1, 0).astype(jnp.bfloat16)
            for k, piece in enumerate(pieces):
                piece[c, at] = back[k * PACK : (k + 1) * PACK]


def spread(ids, mixing, pixels, rims, groups, picks):
    lines, every, cols = pixels.shape
    each = rims[0].shape[0]
    count = every // groups
    halves = count // PACK
    piece = jax.ShapeDtypeStruct((each, lines // each + 2 * NSWEEP, PACK, cols), jnp.bfloat16)
    pieces = pl.pallas_call(
        functools.partial(spread_kernel, picks),
        in_specs=[smem()] + [vmem()] * 4,
        out_specs=[vmem()] * len(picks) * halves,
        out_shape=[piece] * len(picks) * halves,
        scratch_shapes=[pltpu.VMEM((len(picks) * count, every), jnp.bfloat16)],
        compiler_params=room(),
        cost_estimate=cost(1.6),
        name="spread",
    )(ids, mixing, pixels, *rims)
    return [pieces[n * halves : (n + 1) * halves] for n in range(len(picks))]


def gate_kernel(*refs):
    pass


def gate(values, after):
    count = len(values)
    return pl.pallas_call(
        gate_kernel,
        in_specs=[anywhere()] * (count + len(after)),
        out_specs=[anywhere()] * count,
        out_shape=[jax.ShapeDtypeStruct(value.shape, value.dtype) for value in values],
        input_output_aliases={n: n for n in range(count)},
        compiler_params=room(),
        name="gate",
    )(*values, *after)


def variation_kernel(units, at, n_outs, info_ref, weight_ref, order_ref, *refs):
    n_back = len(units)
    own, rims, backs = refs[0], refs[1:3], refs[3 : 3 + n_back]
    fg_out, bg_out, token_ref, source, first, second, flat_fg, flat_bg, image_held, fg_held, bg_held, sems = refs[
        3 + n_back + n_outs :
    ]
    groups = (info_ref.shape[0] - 3) // 2
    odd = info_ref[2 * groups + 2] != 0
    channels = [info_ref[groups + pick] * backs[0].shape[0] + at for pick, _ in units]
    edge = NSWEEP
    nf = PACK
    chans, rows, count, cols = own.shape
    chans -= 1
    tiles = cols // LANE
    lines = rows + 2 * edge
    up_flag = info_ref[2 * groups].astype(jnp.float32)
    down_flag = info_ref[2 * groups + 1].astype(jnp.float32)
    end = lax.broadcasted_iota(jnp.int32, (nf, LANE), 1) == LANE - 1

    def frames_at(chan, h, some):
        if h < 0:
            return jnp.where(odd, rims[0][chan, h + edge, some, :], rims[1][chan, h + edge, some, :])
        if h < rows:
            return own[chan, h, some, :]
        return jnp.where(odd, rims[1][chan, h - rows, some, :], rims[0][chan, h - rows, some, :])

    def load(ref, i):
        return [ref[i, :, tile(j)] for j in range(tiles)]

    def divergence(over, here, beside):
        left = [pltpu.roll(beside[-1], 1, 1)] + beside[:-1]
        return [(here[j] - over[j]) + (beside[j] - left[j]) for j in range(tiles)]

    def smooth(i, over, here, beside):
        div = divergence(over, here, beside)
        image = load(source, i)
        return [image[j] - STEP_SIZE * div[j] for j in range(tiles)]

    def copy_of(held, out, n, g, chan, start):
        place = pl.ds(pl.multiple_of(start * nf, nf), nf)
        return pltpu.make_async_copy(held.at[g], out.at[place, chan], sems.at[n, g])

    for g, back in enumerate(backs):
        for h in range(rows):
            for j in range(tiles):
                line = back[at, edge + h, :, tile(j)].astype(jnp.float32)
                flat_bg[j, pl.ds(h, nf, stride=rows), :] = line
        for j in range(tiles):
            bg_held[g, :, :, tile(j)] = flat_bg[j].astype(jnp.bfloat16).reshape(nf, rows, LANE)
        moved = short_dot(back[at].reshape(lines * nf, cols), order_ref[...], 1, 0)
        for i in range(lines):
            image_held[g, i] = moved[i * nf : (i + 1) * nf]
        copy_of(bg_held, bg_out, 1, g, channels[g], units[g][1]).start()

    @pl.loop(0, n_back)
    def some_frames(g):
        chan, start = channels[0], units[0][1]
        for n in range(1, n_back):
            chan = jnp.where(g == n, channels[n], chan)
            start = jnp.where(g == n, units[n][1], start)
        some = pl.ds(pl.multiple_of(start * nf, nf), nf)
        lam = weight_ref[chan]
        step = STEP_SIZE / lam
        for i in range(lines):
            image = frames_at(chan, i - edge, some).astype(jnp.float32)
            source[i] = (image - image_held[g, i]) * step

        @pl.when(chan == chans - 1)
        def mask():
            for i in range(lines):
                source[i] = source[i] * frames_at(chans, i - edge, some).astype(jnp.float32)

        for sweep in range(NSWEEP):
            here = beside = None
            if sweep:
                here, beside = load(first, sweep), load(second, sweep)
                now = smooth(sweep, load(first, sweep - 1), here, beside)
            else:
                now = load(source, 0)
            for i in range(sweep, lines - 1 - sweep):
                next_here = next_beside = None
                if sweep:
                    next_here, next_beside = load(first, i + 1), load(second, i + 1)
                    later = smooth(i + 1, here, next_here, next_beside)
                else:
                    later = load(source, i + 1)
                right = now[1:] + [jnp.where(end, now[-1], pltpu.roll(now[0], LANE - 1, 1))]
                for j in range(tiles):
                    down = later[j] - now[j]
                    if i == edge - 1:
                        down = down * up_flag
                    if i == edge + rows - 1:
                        down = down * down_flag
                    across = right[j] - now[j]
                    square = down * down + across * across
                    size = square * lax.rsqrt(jnp.maximum(square, 1e-30))
                    scale = pl.reciprocal(1.0 + size, approx=True)
                    first[i, :, tile(j)] = (here[j] - down if sweep else -down) * scale
                    second[i, :, tile(j)] = (beside[j] - across if sweep else -across) * scale
                now, here, beside = later, next_here, next_beside

        over = load(first, edge - 1)
        for h in range(rows):
            here, beside = load(first, edge + h), load(second, edge + h)
            image = smooth(edge + h, over, here, beside)
            for j in range(tiles):
                flat_fg[j, pl.ds(h, nf, stride=rows), :] = image[j] * (lam / STEP_SIZE)
            over = here
        fg = jnp.concatenate([flat_fg[j].astype(jnp.bfloat16) for j in range(tiles)], axis=1)
        fg = short_dot(fg, order_ref[...], 1, 1).astype(jnp.bfloat16)
        fg_held[g] = fg.reshape(nf, rows, cols)
        copy_of(fg_held, fg_out, 0, g, chan, start).start()

    for g in range(n_back):
        copy_of(fg_held, fg_out, 0, g, channels[g], units[g][1]).wait()
        copy_of(bg_held, bg_out, 1, g, channels[g], units[g][1]).wait()


def variation(info, weights, units, at, order, own, rims, backs, outs, shape):
    count, chans, rows, cols = shape
    lines = rows + 2 * NSWEEP
    flat = pltpu.VMEM((cols // LANE, PACK * rows, LANE), jnp.float32)
    field = pltpu.VMEM((lines, PACK, cols), jnp.float32)
    held = pltpu.VMEM((len(backs), PACK, rows, cols), jnp.bfloat16)
    images = pltpu.VMEM((len(backs), lines, PACK, cols), jnp.float32)
    return pl.pallas_call(
        functools.partial(variation_kernel, units, at, len(outs)),
        in_specs=[smem(), smem()] + [vmem()] * (4 + len(backs)) + [anywhere()] * len(outs),
        out_specs=[anywhere(), anywhere(), vmem()],
        out_shape=[jax.ShapeDtypeStruct(shape, jnp.bfloat16)] * 2
        + [jax.ShapeDtypeStruct((SUB, LANE), jnp.float32)],
        scratch_shapes=[
            field,
            field,
            field,
            flat,
            flat,
            images,
            held,
            held,
            pltpu.SemaphoreType.DMA((2, len(backs))),
        ],
        input_output_aliases={6 + len(backs) + n: n for n in range(len(outs))},
        compiler_params=room(field, field, field, flat, flat, images, held, held),
        cost_estimate=cost(4.3 * len(backs)),
        name="variation",
    )(info, weights, order, own, *rims, *backs, *outs)


def body(frames, prev_fg, depth_valid, sketch, tv_weight):
    count, chans, rows, cols = frames.shape
    groups = lax.axis_size("frame")
    strips = lax.axis_size("pix")
    each = chans // groups
    nval = chans * rows * strips * cols
    tiles = cols // LANE
    me, strip = lax.axis_index("frame"), lax.axis_index("pix")
    targets = [partner(me, k, groups) for k in range(groups)]
    sources = [partner(me, k, groups, back=True) for k in range(groups)]
    ends = [strip > 0, strip < strips - 1, strip % 2]
    info = jnp.stack([jnp.asarray(one, jnp.int32) for one in targets + sources + ends])
    near = [k for k in range(1, groups) if power_of_two(k)]
    far = [k for k in range(1, groups) if not power_of_two(k)]

    resid = {}
    for picks in (near, far + [0]):
        resid.update(zip(picks, residual(info, picks, each, frames, prev_fg, depth_valid)))
    blocks = [resid[0]] + [swap(resid[k], "frame", k) for k in range(1, groups)]
    blocks = [block.reshape(each * rows, count, cols) for block in blocks]

    places = lax.broadcasted_iota(jnp.int32, (cols, cols), 1)
    places = places % LANE * tiles + places // LANE
    order = (places == lax.broadcasted_iota(jnp.int32, (cols, cols), 0)).astype(jnp.bfloat16)
    lined, *rims = interleaved(info, frames, depth_valid, order, tuple(resid.values()))
    lined_rims = rims_swapped(rims)

    terms, pixels, *rims = gram_terms(info, blocks, each, nval, ())
    (gram,) = gate([all_sum(terms, "frame")], lined_rims)
    gram = all_sum(gram, "pix")
    around = rims_swapped(gate(rims, [gram]))
    mixing = mixing_matrix(gram, sketch)
    picks = [0] + near + far
    pieces = dict(zip(picks, spread(info, mixing, pixels, around, groups, picks)))
    halves = range(count // PACK)
    arrived = {(0, g): pieces[0][g] for g in halves}
    for k in near:
        arrived[k, 0] = swap(pieces[k][0], "frame", k)

    outs = []

    def work_on(units, outs):
        parts = [arrived[unit] for unit in units]
        for c in range(each):
            *outs, token = variation(
                info, tv_weight, units, c, order, lined, lined_rims, parts, outs, frames.shape
            )
        return outs, token

    token = None
    stages = [[(0, g) for g in halves]] + [[(k, g) for k in near] for g in halves]
    stages += [[(k, g)] for k in far for g in halves]
    sends = [[(k, g) for k in near] for g in halves[1:]] + [[(k, g) for k in far for g in halves]]
    for n, stage in enumerate(stages):
        outs, token = work_on(stage, outs)
        following = sends[n] if n < len(sends) else []
        there = list(arrived.values()) if n else []
        for k, g in following:
            (held,) = gate([pieces[k][g]], [token] + there)
            arrived[k, g] = swap(held, "frame", k)
    foreground, background = outs
    return (background, foreground)


def solution(mesh):
    placed = (
        P("frame", None, "pix", None),
        P("frame", None, "pix", None),
        P("frame", "pix", None),
        P(),
        P(),
    )
    return jax.shard_map(
        body,
        mesh=mesh,
        in_specs=placed,
        out_specs=(P("frame", None, "pix", None), P("frame", None, "pix", None)),
        check_vma=False,
    )
```

```python
import functools
import math

import jax
import jax.numpy as jnp
from jax import lax
from jax.experimental import pallas as pl
from jax.experimental.pallas import tpu as pltpu
from jax.sharding import PartitionSpec as P

POWER = 3
NSWEEP = 5
STEP_SIZE = 0.125
SUB = 8
LANE = 128
PACK = 16
SPARE_BYTES = 7 * 1024 * 1024
MOST_BYTES = 58 * 1024 * 1024


def power_of_two(count):
    return count & (count - 1) == 0


def partner(index, offset, count, back=False):
    if power_of_two(count):
        return index ^ offset
    return (index + (count - offset if back else offset)) % count


def pair_swap(value, axis, start):
    count = lax.axis_size(axis)
    pairs = []
    for lower in range(start, count - 1, 2):
        pairs += [(lower, lower + 1), (lower + 1, lower)]
    return lax.ppermute(value, axis, pairs)


def rims_swapped(rims):
    return [pair_swap(rim, "pix", start) for start, rim in enumerate(rims)]


def swap(value, axis, offset):
    count = lax.axis_size(axis)
    pairs = [(source, partner(source, offset, count)) for source in range(count)]
    return lax.ppermute(value, axis, pairs)


def all_sum(value, axis):
    count = lax.axis_size(axis)
    if not power_of_two(count):
        return lax.psum(value, axis)
    bit = 1
    while bit < count:
        fours = (count // bit).bit_length() % 2 == 1
        offsets = (bit, 2 * bit, 3 * bit) if fours else (bit,)
        others = [swap(value, axis, offset) for offset in offsets]
        for other in others:
            value = value + other
        bit *= len(offsets) + 1
    return value


def exact_dot(left, right, left_dim, right_dim):
    return lax.dot_general(
        left,
        right,
        (((left_dim,), (right_dim,)), ((), ())),
        precision=lax.Precision.HIGHEST,
        preferred_element_type=jnp.float32,
    )


def short_dot(left, right, left_dim, right_dim):
    return lax.dot_general(
        left,
        right,
        (((left_dim,), (right_dim,)), ((), ())),
        preferred_element_type=jnp.float32,
    )


def eliminate(square, sides):
    rank = square.shape[0]
    width = sides[0].shape[1]
    blocks = rank // SUB
    sub_ids = lax.broadcasted_iota(jnp.int32, (SUB, width), 0)
    square = jnp.concatenate([square, jnp.zeros((rank, width - rank), jnp.float32)], axis=1)

    def in_blocks(rows):
        return [rows[SUB * b : SUB * (b + 1)] for b in range(blocks)]

    def row_of(rows, j):
        return jnp.broadcast_to(rows[j : j + 1], (SUB, width))

    def col_of(rows, j):
        return jnp.broadcast_to(rows[:, j : j + 1], (SUB, width))

    square = in_blocks(square)
    sides = [in_blocks(side) for side in sides]
    solved = [[] for _ in sides]
    for k in range(blocks):
        below = range(k, blocks)
        cols = {b: [col_of(square[b], SUB * k + j) for j in range(SUB)] for b in below}
        pivots = jnp.ones((SUB, width), jnp.float32)
        for j in range(0, SUB, 2):
            col, after = cols[k][j], cols[k][j + 1]
            corner, side_value, last = row_of(col, j), row_of(col, j + 1), row_of(after, j + 1)
            inverse = 1.0 / corner
            next_inverse = corner * (1.0 / (corner * last - side_value * side_value))
            link = side_value * inverse
            pivots = jnp.where(sub_ids == j, corner, pivots)
            pivots = jnp.where(sub_ids == j + 1, last - side_value * link, pivots)

            def two_rows(rows):
                upper = row_of(rows, j)
                return upper, row_of(rows, j + 1) - link * upper

            top = row_of(after, j)
            col_rows = {i: two_rows(cols[k][i]) for i in range(j + 2, SUB)}
            square_rows = two_rows(square[k])
            side_rows = [two_rows(side[k]) for side in sides]
            for b in below:
                ratio = cols[b][j] * inverse
                if b == k:
                    ratio = jnp.where(sub_ids > j, ratio, 0.0)
                next_ratio = (cols[b][j + 1] - ratio * top) * next_inverse
                if b == k:
                    next_ratio = jnp.where(sub_ids > j + 1, next_ratio, 0.0)

                def reduced(rows, pair):
                    return rows - ratio * pair[0] - next_ratio * pair[1]

                for i in range(j + 2, SUB):
                    cols[b][i] = reduced(cols[b][i], col_rows[i])
                square[b] = reduced(square[b], square_rows)
                for side, pair in zip(sides, side_rows):
                    side[b] = reduced(side[b], pair)
        scale = lax.rsqrt(pivots)
        for rows, side in zip(solved, sides):
            rows.append(side[k] * scale)
    return [jnp.concatenate(rows, axis=0) for rows in solved]


def corner_masks(size):
    shape = (size // 2, size)
    rows = lax.broadcasted_iota(jnp.int32, shape, 0)
    lanes = lax.broadcasted_iota(jnp.int32, shape, 1)
    return lanes < size // 2, rows >= lanes, rows == lanes


def packed(square):
    size = square.shape[0]
    left, lower, diagonal = corner_masks(size)
    upper_half = square[: size // 2]
    turned = pltpu.roll(square[size // 2 :], size // 2, 1)
    rows = jnp.where(left & ~lower, turned, upper_half)
    line = jnp.sum(jnp.where(left & diagonal, turned, 0.0), axis=0, keepdims=True)
    return jnp.concatenate([rows, jnp.broadcast_to(line, (SUB, size))], axis=0)


def unpacked(rows):
    size = rows.shape[1]
    half = size // 2
    left, lower, diagonal = corner_masks(size)
    line = rows[half : half + 1]
    rows = rows[:half]
    turned = jnp.concatenate([rows, jnp.zeros((half, size), jnp.float32)], axis=0).T
    upper_half = jnp.where(left & ~lower, turned[:half], rows)
    corner = jnp.where(diagonal, line, jnp.where(lower, turned[:half], rows))
    lower_half = jnp.where(left, turned[half:], pltpu.roll(corner, half, 1))
    return jnp.concatenate([upper_half, lower_half], axis=0)


def mixing_kernel(gram_ref, sketch_ref, mixing_ref):
    gram = unpacked(gram_ref[...])
    basis = sketch_ref[...]
    for turn in range(POWER):
        image = exact_dot(basis, gram, 1, 1)
        (basis,) = eliminate(exact_dot(basis, image, 1, 1), [image])
    image = exact_dot(basis, gram, 1, 1)
    left, right = eliminate(exact_dot(basis, image, 1, 1), [basis, image])
    mixing_ref[...] = exact_dot(right, left, 0, 0).astype(mixing_ref.dtype)


def mixing_matrix(gram, sketch):
    return pl.pallas_call(
        mixing_kernel,
        out_shape=jax.ShapeDtypeStruct(gram.shape[1:] * 2, jnp.bfloat16),
        compiler_params=room(),
        cost_estimate=cost(10.6),
        name="mixing",
    )(gram, sketch.T)


def tile(j):
    return pl.ds(LANE * j, LANE)


def vmem():
    return pl.BlockSpec(memory_space=pltpu.VMEM)


def smem():
    return pl.BlockSpec(memory_space=pltpu.SMEM)


def anywhere():
    return pl.BlockSpec(memory_space=pl.ANY)


def room(*scratch):
    held = sum(math.prod(ref.shape) * jnp.dtype(ref.dtype).itemsize for ref in scratch)
    return pltpu.CompilerParams(vmem_limit_bytes=SPARE_BYTES + held)


def cost(micros):
    return pl.CostEstimate(flops=0, bytes_accessed=int(micros * 3.6e6), transcendentals=0)


def residual_kernel(last, picks, info_ref, frames_ref, prev_ref, valid_ref, *refs):
    outs, (now, before, ok, sems) = refs[: len(picks)], refs[len(picks) :]
    _, each, count, rows, cols = now.shape
    valid_copy = pltpu.make_async_copy(valid_ref, ok, sems.at[0])
    copies = []
    for n, pick in enumerate(picks):
        for c in range(each):
            chan = info_ref[pick] * each + c
            at = 1 + 2 * (n * each + c)
            copies.append(
                (
                    pltpu.make_async_copy(frames_ref.at[:, chan], now.at[n, c], sems.at[at]),
                    pltpu.make_async_copy(prev_ref.at[:, chan], before.at[n, c], sems.at[at + 1]),
                )
            )
    for copy in copies[0]:
        copy.start()
    valid_copy.start()
    for pair in copies[1:]:
        for copy in pair:
            copy.start()
    valid_copy.wait()
    for n, pick in enumerate(picks):
        for c in range(each):
            for copy in copies[n * each + c]:
                copy.wait()
            keep = jnp.where(info_ref[pick] * each + c == last, 0.0, 1.0)
            for g in range(count // PACK):
                some = pl.ds(g * PACK, PACK)
                for j in range(cols // LANE):
                    valid = jnp.where(ok[some, :, tile(j)] != 0, 1.0, keep)
                    diff = now[n, c, some, :, tile(j)].astype(jnp.float32)
                    diff = diff - before[n, c, some, :, tile(j)].astype(jnp.float32)
                    turned = jnp.swapaxes(diff * valid, 0, 1)
                    outs[n][c, :, some, tile(j)] = turned.astype(jnp.bfloat16)


def residual(info, picks, each, frames, prev_fg, depth_valid):
    count, chans, rows, cols = frames.shape
    held = pltpu.VMEM((len(picks), each, count, rows, cols), jnp.bfloat16)
    return pl.pallas_call(
        functools.partial(residual_kernel, chans - 1, picks),
        in_specs=[smem()] + [anywhere()] * 3,
        out_specs=[vmem()] * len(picks),
        out_shape=[jax.ShapeDtypeStruct((each, rows, count, cols), jnp.bfloat16)] * len(picks),
        scratch_shapes=[
            held,
            held,
            pltpu.VMEM((count, rows, cols), jnp.int32),
            pltpu.SemaphoreType.DMA((1 + 2 * each * len(picks),)),
        ],
        compiler_params=pltpu.CompilerParams(vmem_limit_bytes=MOST_BYTES),
        cost_estimate=cost(3.0),
        name="residual",
    )(info, frames, prev_fg, depth_valid)


def interleave_kernel(info_ref, frames_ref, valid_ref, order_ref, *refs):
    out_ref, rims = refs[-3], refs[-2:]
    odd = info_ref[info_ref.shape[0] - 1]
    count, chans, rows, cols = frames_ref.shape
    for c in range(chans + 1):
        for g in range(count // PACK):
            some = pl.ds(g * PACK, PACK)
            if c < chans:
                lines = frames_ref[some, c]
            else:
                lines = valid_ref[some].astype(jnp.float32).astype(jnp.bfloat16)
            lines = short_dot(lines.reshape(PACK * rows, cols), order_ref[...], 1, 0)
            for j in range(cols // LANE):
                turned = lines[:, LANE * j : LANE * (j + 1)].reshape(PACK, rows, LANE)
                turned = jnp.swapaxes(turned, 0, 1).astype(jnp.bfloat16)
                out_ref[c, :, some, tile(j)] = turned
    write_rims(rims, odd, lambda h: out_ref[:, h], rows)


def write_rims(rims, odd, read, rows, axis_rows=NSWEEP):
    first = jnp.where(odd != 0, 0, rows - axis_rows)
    for h in range(axis_rows):
        rims[0][:, h] = read(first + h)
        rims[1][:, h] = read(rows - axis_rows - first + h)


def interleaved(info, frames, depth_valid, order, after):
    count, chans, rows, cols = frames.shape
    return pl.pallas_call(
        interleave_kernel,
        in_specs=[smem()] + [vmem()] * 3 + [anywhere()] * len(after),
        out_specs=[vmem()] * 3,
        out_shape=[
            jax.ShapeDtypeStruct((chans + 1, height, count, cols), jnp.bfloat16)
            for height in (rows, NSWEEP, NSWEEP)
        ],
        compiler_params=room(),
        cost_estimate=cost(3.3),
        name="interleave",
    )(info, frames, depth_valid, order, *after)


def gram_kernel(groups, each, nval, ids_ref, *refs):
    blocks, (gram_ref, all_ref), rims = refs[:groups], refs[-4:-2], refs[-2:]
    lines, count, cols = blocks[0].shape
    for k, block in enumerate(blocks):
        start = pl.multiple_of(ids_ref[groups + k] * count, count)
        all_ref[:, pl.ds(start, count), :] = block[...]
    rows = lines // each
    odd = ids_ref[ids_ref.shape[0] - 1]
    for c in range(each):
        some = [rim.at[pl.ds(c, 1)] for rim in rims]
        write_rims(some, odd, lambda h, c=c: all_ref[pl.ds(c * rows + h, 1)], rows)
    every = all_ref.shape[1]
    total = jnp.zeros((every, every), jnp.float32)
    for r in range(lines):
        total = total + short_dot(all_ref[r], all_ref[r], 1, 1)
    gram_ref[...] = packed(total / nval)


def gram_terms(ids, blocks, each, nval, after):
    groups = len(blocks)
    lines, count, cols = blocks[0].shape
    every = groups * count
    return pl.pallas_call(
        functools.partial(gram_kernel, groups, each, nval),
        in_specs=[smem()] + [vmem()] * groups + [anywhere()] * len(after),
        out_specs=[vmem()] * 4,
        out_shape=[
            jax.ShapeDtypeStruct((every // 2 + SUB, every), jnp.float32),
            jax.ShapeDtypeStruct((lines, every, cols), jnp.bfloat16),
            jax.ShapeDtypeStruct((each, NSWEEP, every, cols), jnp.bfloat16),
            jax.ShapeDtypeStruct((each, NSWEEP, every, cols), jnp.bfloat16),
        ],
        compiler_params=room(),
        cost_estimate=cost(1.4),
        name="gram",
    )(ids, *blocks, *after)


def spread_kernel(picks, ids_ref, mixing_ref, all_ref, *refs):
    rims, pieces, weights = refs[:2], refs[2:-1], refs[-1]
    odd = ids_ref[ids_ref.shape[0] - 1] != 0
    each, lines, _, cols = pieces[0].shape
    halves = len(pieces) // len(picks)
    count = halves * PACK
    rows = lines - 2 * NSWEEP
    for k, pick in enumerate(picks):
        start = pl.multiple_of(ids_ref[pick] * count, count)
        weights[pl.ds(k * count, count), :] = mixing_ref[pl.ds(start, count), :]
    chosen = weights[...]
    for c in range(each):
        for at in range(lines):
            h = at - NSWEEP
            if h < 0:
                pixels = jnp.where(odd, rims[0][c, at], rims[1][c, at])
            elif h < rows:
                pixels = all_ref[c * rows + h]
            else:
                pixels = jnp.where(odd, rims[1][c, h - rows], rims[0][c, h - rows])
            back = short_dot(chosen, pixels, 1, 0).astype(jnp.bfloat16)
            for k, piece in enumerate(pieces):
                piece[c, at] = back[k * PACK : (k + 1) * PACK]


def spread(ids, mixing, pixels, rims, groups, picks):
    lines, every, cols = pixels.shape
    each = rims[0].shape[0]
    count = every // groups
    halves = count // PACK
    piece = jax.ShapeDtypeStruct((each, lines // each + 2 * NSWEEP, PACK, cols), jnp.bfloat16)
    pieces = pl.pallas_call(
        functools.partial(spread_kernel, picks),
        in_specs=[smem()] + [vmem()] * 4,
        out_specs=[vmem()] * len(picks) * halves,
        out_shape=[piece] * len(picks) * halves,
        scratch_shapes=[pltpu.VMEM((len(picks) * count, every), jnp.bfloat16)],
        compiler_params=room(),
        cost_estimate=cost(1.6),
        name="spread",
    )(ids, mixing, pixels, *rims)
    return [pieces[n * halves : (n + 1) * halves] for n in range(len(picks))]


def gate_kernel(*refs):
    pass


def gate(values, after):
    count = len(values)
    return pl.pallas_call(
        gate_kernel,
        in_specs=[anywhere()] * (count + len(after)),
        out_specs=[anywhere()] * count,
        out_shape=[jax.ShapeDtypeStruct(value.shape, value.dtype) for value in values],
        input_output_aliases={n: n for n in range(count)},
        compiler_params=room(),
        name="gate",
    )(*values, *after)


def variation_kernel(units, at, n_outs, info_ref, weight_ref, order_ref, *refs):
    n_back = len(units)
    own, rims, backs = refs[0], refs[1:3], refs[3 : 3 + n_back]
    fg_out, bg_out, token_ref, source, first, second, flat_fg, flat_bg, image_held, fg_held, bg_held, sems = refs[
        3 + n_back + n_outs :
    ]
    groups = (info_ref.shape[0] - 3) // 2
    odd = info_ref[2 * groups + 2] != 0
    channels = [info_ref[groups + pick] * backs[0].shape[0] + at for pick, _ in units]
    edge = NSWEEP
    nf = PACK
    chans, rows, count, cols = own.shape
    chans -= 1
    tiles = cols // LANE
    lines = rows + 2 * edge
    up_flag = info_ref[2 * groups].astype(jnp.float32)
    down_flag = info_ref[2 * groups + 1].astype(jnp.float32)
    end = lax.broadcasted_iota(jnp.int32, (nf, LANE), 1) == LANE - 1

    def frames_at(chan, h, some):
        if h < 0:
            return jnp.where(odd, rims[0][chan, h + edge, some, :], rims[1][chan, h + edge, some, :])
        if h < rows:
            return own[chan, h, some, :]
        return jnp.where(odd, rims[1][chan, h - rows, some, :], rims[0][chan, h - rows, some, :])

    def load(ref, i):
        return [ref[i, :, tile(j)] for j in range(tiles)]

    def divergence(over, here, beside):
        left = [pltpu.roll(beside[-1], 1, 1)] + beside[:-1]
        return [(here[j] - over[j]) + (beside[j] - left[j]) for j in range(tiles)]

    def smooth(i, over, here, beside):
        div = divergence(over, here, beside)
        image = load(source, i)
        return [image[j] - STEP_SIZE * div[j] for j in range(tiles)]

    def copy_of(held, out, n, g, chan, start):
        place = pl.ds(pl.multiple_of(start * nf, nf), nf)
        return pltpu.make_async_copy(held.at[g], out.at[place, chan], sems.at[n, g])

    for g, back in enumerate(backs):
        for h in range(rows):
            for j in range(tiles):
                line = back[at, edge + h, :, tile(j)].astype(jnp.float32)
                flat_bg[j, pl.ds(h, nf, stride=rows), :] = line
        for j in range(tiles):
            bg_held[g, :, :, tile(j)] = flat_bg[j].astype(jnp.bfloat16).reshape(nf, rows, LANE)
        moved = short_dot(back[at].reshape(lines * nf, cols), order_ref[...], 1, 0)
        for i in range(lines):
            image_held[g, i] = moved[i * nf : (i + 1) * nf]
        copy_of(bg_held, bg_out, 1, g, channels[g], units[g][1]).start()

    @pl.loop(0, n_back)
    def some_frames(g):
        chan, start = channels[0], units[0][1]
        for n in range(1, n_back):
            chan = jnp.where(g == n, channels[n], chan)
            start = jnp.where(g == n, units[n][1], start)
        some = pl.ds(pl.multiple_of(start * nf, nf), nf)
        lam = weight_ref[chan]
        step = STEP_SIZE / lam
        for i in range(lines):
            image = frames_at(chan, i - edge, some).astype(jnp.float32)
            source[i] = (image - image_held[g, i]) * step

        @pl.when(chan == chans - 1)
        def mask():
            for i in range(lines):
                source[i] = source[i] * frames_at(chans, i - edge, some).astype(jnp.float32)

        for sweep in range(NSWEEP):
            here = beside = None
            if sweep:
                here, beside = load(first, sweep), load(second, sweep)
                now = smooth(sweep, load(first, sweep - 1), here, beside)
            else:
                now = load(source, 0)
            for i in range(sweep, lines - 1 - sweep):
                next_here = next_beside = None
                if sweep:
                    next_here, next_beside = load(first, i + 1), load(second, i + 1)
                    later = smooth(i + 1, here, next_here, next_beside)
                else:
                    later = load(source, i + 1)
                right = now[1:] + [jnp.where(end, now[-1], pltpu.roll(now[0], LANE - 1, 1))]
                for j in range(tiles):
                    down = later[j] - now[j]
                    if i == edge - 1:
                        down = down * up_flag
                    if i == edge + rows - 1:
                        down = down * down_flag
                    across = right[j] - now[j]
                    square = down * down + across * across
                    size = square * lax.rsqrt(jnp.maximum(square, 1e-30))
                    scale = pl.reciprocal(1.0 + size, approx=True)
                    first[i, :, tile(j)] = (here[j] - down if sweep else -down) * scale
                    second[i, :, tile(j)] = (beside[j] - across if sweep else -across) * scale
                now, here, beside = later, next_here, next_beside

        over = load(first, edge - 1)
        for h in range(rows):
            here, beside = load(first, edge + h), load(second, edge + h)
            image = smooth(edge + h, over, here, beside)
            for j in range(tiles):
                flat_fg[j, pl.ds(h, nf, stride=rows), :] = image[j] * (lam / STEP_SIZE)
            over = here
        fg = jnp.concatenate([flat_fg[j].astype(jnp.bfloat16) for j in range(tiles)], axis=1)
        fg = short_dot(fg, order_ref[...], 1, 1).astype(jnp.bfloat16)
        fg_held[g] = fg.reshape(nf, rows, cols)
        copy_of(fg_held, fg_out, 0, g, chan, start).start()

    for g in range(n_back):
        copy_of(fg_held, fg_out, 0, g, channels[g], units[g][1]).wait()
        copy_of(bg_held, bg_out, 1, g, channels[g], units[g][1]).wait()


def variation(info, weights, units, at, order, own, rims, backs, outs, shape):
    count, chans, rows, cols = shape
    lines = rows + 2 * NSWEEP
    flat = pltpu.VMEM((cols // LANE, PACK * rows, LANE), jnp.float32)
    field = pltpu.VMEM((lines, PACK, cols), jnp.float32)
    held = pltpu.VMEM((len(backs), PACK, rows, cols), jnp.bfloat16)
    images = pltpu.VMEM((len(backs), lines, PACK, cols), jnp.float32)
    return pl.pallas_call(
        functools.partial(variation_kernel, units, at, len(outs)),
        in_specs=[smem(), smem()] + [vmem()] * (4 + len(backs)) + [anywhere()] * len(outs),
        out_specs=[anywhere(), anywhere(), vmem()],
        out_shape=[jax.ShapeDtypeStruct(shape, jnp.bfloat16)] * 2
        + [jax.ShapeDtypeStruct((SUB, LANE), jnp.float32)],
        scratch_shapes=[
            field,
            field,
            field,
            flat,
            flat,
            images,
            held,
            held,
            pltpu.SemaphoreType.DMA((2, len(backs))),
        ],
        input_output_aliases={6 + len(backs) + n: n for n in range(len(outs))},
        compiler_params=room(field, field, field, flat, flat, images, held, held),
        cost_estimate=cost(4.3 * len(backs)),
        name="variation",
    )(info, weights, order, own, *rims, *backs, *outs)


def body(frames, prev_fg, depth_valid, sketch, tv_weight):
    count, chans, rows, cols = frames.shape
    groups = lax.axis_size("frame")
    strips = lax.axis_size("pix")
    each = chans // groups
    nval = chans * rows * strips * cols
    tiles = cols // LANE
    me, strip = lax.axis_index("frame"), lax.axis_index("pix")
    targets = [partner(me, k, groups) for k in range(groups)]
    sources = [partner(me, k, groups, back=True) for k in range(groups)]
    ends = [strip > 0, strip < strips - 1, strip % 2]
    info = jnp.stack([jnp.asarray(one, jnp.int32) for one in targets + sources + ends])
    near = [k for k in range(1, groups) if power_of_two(k)]
    far = [k for k in range(1, groups) if not power_of_two(k)]

    resid = {}
    for picks in (near, far + [0]):
        resid.update(zip(picks, residual(info, picks, each, frames, prev_fg, depth_valid)))
    blocks = [resid[0]] + [swap(resid[k], "frame", k) for k in range(1, groups)]
    blocks = [block.reshape(each * rows, count, cols) for block in blocks]

    places = lax.broadcasted_iota(jnp.int32, (cols, cols), 1)
    places = places % LANE * tiles + places // LANE
    order = (places == lax.broadcasted_iota(jnp.int32, (cols, cols), 0)).astype(jnp.bfloat16)
    lined, *rims = interleaved(info, frames, depth_valid, order, tuple(resid.values()))
    lined_rims = rims_swapped(rims)

    terms, pixels, *rims = gram_terms(info, blocks, each, nval, ())
    gram = all_sum(all_sum(terms, "frame"), "pix")
    gram, *rims = gate([gram] + rims, lined_rims)
    around = rims_swapped(rims)
    mixing = mixing_matrix(gram, sketch)
    picks = [0] + near + far
    pieces = dict(zip(picks, spread(info, mixing, pixels, around, groups, picks)))
    halves = range(count // PACK)
    arrived = {(0, g): pieces[0][g] for g in halves}
    for k in near:
        arrived[k, 0] = swap(pieces[k][0], "frame", k)

    outs = []

    def work_on(units, outs):
        parts = [arrived[unit] for unit in units]
        for c in range(each):
            *outs, token = variation(
                info, tv_weight, units, c, order, lined, lined_rims, parts, outs, frames.shape
            )
        return outs, token

    token = None
    stages = [[(0, g) for g in halves]] + [[(k, g) for k in near] for g in halves]
    stages += [[(k, g)] for k in far for g in halves]
    sends = [[(k, g) for k in near] for g in halves[1:]] + [[(k, g) for k in far for g in halves]]
    for n, stage in enumerate(stages):
        outs, token = work_on(stage, outs)
        following = sends[n] if n < len(sends) else []
        there = list(arrived.values()) if n else []
        for k, g in following:
            (held,) = gate([pieces[k][g]], [token] + there)
            arrived[k, g] = swap(held, "frame", k)
    foreground, background = outs
    return (background, foreground)


def solution(mesh):
    placed = (
        P("frame", None, "pix", None),
        P("frame", None, "pix", None),
        P("frame", "pix", None),
        P(),
        P(),
    )
    return jax.shard_map(
        body,
        mesh=mesh,
        in_specs=placed,
        out_specs=(P("frame", None, "pix", None), P("frame", None, "pix", None)),
        check_vma=False,
    )
```

```python
import functools
import math

import jax
import jax.numpy as jnp
from jax import lax
from jax.experimental import pallas as pl
from jax.experimental.pallas import tpu as pltpu
from jax.sharding import PartitionSpec as P

POWER = 3
NSWEEP = 5
STEP_SIZE = 0.125
SUB = 8
LANE = 128
PACK = 16
SPARE_BYTES = 7 * 1024 * 1024
MOST_BYTES = 58 * 1024 * 1024


def power_of_two(count):
    return count & (count - 1) == 0


def partner(index, offset, count, back=False):
    if power_of_two(count):
        return index ^ offset
    return (index + (count - offset if back else offset)) % count


def pair_swap(value, axis, start):
    count = lax.axis_size(axis)
    pairs = []
    for lower in range(start, count - 1, 2):
        pairs += [(lower, lower + 1), (lower + 1, lower)]
    return lax.ppermute(value, axis, pairs)


def rims_swapped(rims):
    return [pair_swap(rim, "pix", start) for start, rim in enumerate(rims)]


def swap(value, axis, offset):
    count = lax.axis_size(axis)
    pairs = [(source, partner(source, offset, count)) for source in range(count)]
    return lax.ppermute(value, axis, pairs)


def all_sum(value, axis):
    count = lax.axis_size(axis)
    if not power_of_two(count):
        return lax.psum(value, axis)
    bit = 1
    while bit < count:
        fours = (count // bit).bit_length() % 2 == 1
        offsets = (bit, 2 * bit, 3 * bit) if fours else (bit,)
        others = [swap(value, axis, offset) for offset in offsets]
        for other in others:
            value = value + other
        bit *= len(offsets) + 1
    return value


def exact_dot(left, right, left_dim, right_dim):
    return lax.dot_general(
        left,
        right,
        (((left_dim,), (right_dim,)), ((), ())),
        precision=lax.Precision.HIGHEST,
        preferred_element_type=jnp.float32,
    )


def short_dot(left, right, left_dim, right_dim):
    return lax.dot_general(
        left,
        right,
        (((left_dim,), (right_dim,)), ((), ())),
        preferred_element_type=jnp.float32,
    )


def eliminate(square, sides):
    rank = square.shape[0]
    width = sides[0].shape[1]
    blocks = rank // SUB
    sub_ids = lax.broadcasted_iota(jnp.int32, (SUB, width), 0)
    square = jnp.concatenate([square, jnp.zeros((rank, width - rank), jnp.float32)], axis=1)

    def in_blocks(rows):
        return [rows[SUB * b : SUB * (b + 1)] for b in range(blocks)]

    def row_of(rows, j):
        return jnp.broadcast_to(rows[j : j + 1], (SUB, width))

    def col_of(rows, j):
        return jnp.broadcast_to(rows[:, j : j + 1], (SUB, width))

    square = in_blocks(square)
    sides = [in_blocks(side) for side in sides]
    solved = [[] for _ in sides]
    for k in range(blocks):
        below = range(k, blocks)
        cols = {b: [col_of(square[b], SUB * k + j) for j in range(SUB)] for b in below}
        pivots = jnp.ones((SUB, width), jnp.float32)
        for j in range(0, SUB, 2):
            col, after = cols[k][j], cols[k][j + 1]
            corner, side_value, last = row_of(col, j), row_of(col, j + 1), row_of(after, j + 1)
            inverse = 1.0 / corner
            next_inverse = corner * (1.0 / (corner * last - side_value * side_value))
            link = side_value * inverse
            pivots = jnp.where(sub_ids == j, corner, pivots)
            pivots = jnp.where(sub_ids == j + 1, last - side_value * link, pivots)

            def two_rows(rows):
                upper = row_of(rows, j)
                return upper, row_of(rows, j + 1) - link * upper

            top = row_of(after, j)
            col_rows = {i: two_rows(cols[k][i]) for i in range(j + 2, SUB)}
            square_rows = two_rows(square[k])
            side_rows = [two_rows(side[k]) for side in sides]
            for b in below:
                ratio = cols[b][j] * inverse
                if b == k:
                    ratio = jnp.where(sub_ids > j, ratio, 0.0)
                next_ratio = (cols[b][j + 1] - ratio * top) * next_inverse
                if b == k:
                    next_ratio = jnp.where(sub_ids > j + 1, next_ratio, 0.0)

                def reduced(rows, pair):
                    return rows - ratio * pair[0] - next_ratio * pair[1]

                for i in range(j + 2, SUB):
                    cols[b][i] = reduced(cols[b][i], col_rows[i])
                square[b] = reduced(square[b], square_rows)
                for side, pair in zip(sides, side_rows):
                    side[b] = reduced(side[b], pair)
        scale = lax.rsqrt(pivots)
        for rows, side in zip(solved, sides):
            rows.append(side[k] * scale)
    return [jnp.concatenate(rows, axis=0) for rows in solved]


def corner_masks(size):
    shape = (size // 2, size)
    rows = lax.broadcasted_iota(jnp.int32, shape, 0)
    lanes = lax.broadcasted_iota(jnp.int32, shape, 1)
    return lanes < size // 2, rows >= lanes, rows == lanes


def packed(square):
    size = square.shape[0]
    left, lower, diagonal = corner_masks(size)
    upper_half = square[: size // 2]
    turned = pltpu.roll(square[size // 2 :], size // 2, 1)
    rows = jnp.where(left & ~lower, turned, upper_half)
    line = jnp.sum(jnp.where(left & diagonal, turned, 0.0), axis=0, keepdims=True)
    return jnp.concatenate([rows, jnp.broadcast_to(line, (SUB, size))], axis=0)


def unpacked(rows):
    size = rows.shape[1]
    half = size // 2
    left, lower, diagonal = corner_masks(size)
    line = rows[half : half + 1]
    rows = rows[:half]
    turned = jnp.concatenate([rows, jnp.zeros((half, size), jnp.float32)], axis=0).T
    upper_half = jnp.where(left & ~lower, turned[:half], rows)
    corner = jnp.where(diagonal, line, jnp.where(lower, turned[:half], rows))
    lower_half = jnp.where(left, turned[half:], pltpu.roll(corner, half, 1))
    return jnp.concatenate([upper_half, lower_half], axis=0)


def mixing_kernel(gram_ref, sketch_ref, mixing_ref):
    gram = unpacked(gram_ref[...])
    basis = sketch_ref[...]
    for turn in range(POWER):
        image = exact_dot(basis, gram, 1, 1)
        (basis,) = eliminate(exact_dot(basis, image, 1, 1), [image])
    image = exact_dot(basis, gram, 1, 1)
    left, right = eliminate(exact_dot(basis, image, 1, 1), [basis, image])
    mixing_ref[...] = exact_dot(right, left, 0, 0).astype(mixing_ref.dtype)


def mixing_matrix(gram, sketch):
    return pl.pallas_call(
        mixing_kernel,
        out_shape=jax.ShapeDtypeStruct(gram.shape[1:] * 2, jnp.bfloat16),
        compiler_params=room(),
        cost_estimate=cost(10.6),
        name="mixing",
    )(gram, sketch.T)


def tile(j):
    return pl.ds(LANE * j, LANE)


def vmem():
    return pl.BlockSpec(memory_space=pltpu.VMEM)


def smem():
    return pl.BlockSpec(memory_space=pltpu.SMEM)


def anywhere():
    return pl.BlockSpec(memory_space=pl.ANY)


def room(*scratch):
    held = sum(math.prod(ref.shape) * jnp.dtype(ref.dtype).itemsize for ref in scratch)
    return pltpu.CompilerParams(vmem_limit_bytes=SPARE_BYTES + held)


def cost(micros):
    return pl.CostEstimate(flops=0, bytes_accessed=int(micros * 3.6e6), transcendentals=0)


def residual_kernel(last, picks, info_ref, frames_ref, prev_ref, valid_ref, *refs):
    outs, (now, before, ok, sems) = refs[: len(picks)], refs[len(picks) :]
    _, each, count, rows, cols = now.shape
    valid_copy = pltpu.make_async_copy(valid_ref, ok, sems.at[0])
    copies = []
    for n, pick in enumerate(picks):
        for c in range(each):
            chan = info_ref[pick] * each + c
            at = 1 + 2 * (n * each + c)
            copies.append(
                (
                    pltpu.make_async_copy(frames_ref.at[:, chan], now.at[n, c], sems.at[at]),
                    pltpu.make_async_copy(prev_ref.at[:, chan], before.at[n, c], sems.at[at + 1]),
                )
            )
    for copy in copies[0]:
        copy.start()
    valid_copy.start()
    for pair in copies[1:]:
        for copy in pair:
            copy.start()
    valid_copy.wait()
    for n, pick in enumerate(picks):
        for c in range(each):
            for copy in copies[n * each + c]:
                copy.wait()
            keep = jnp.where(info_ref[pick] * each + c == last, 0.0, 1.0)
            for g in range(count // PACK):
                some = pl.ds(g * PACK, PACK)
                for j in range(cols // LANE):
                    valid = jnp.where(ok[some, :, tile(j)] != 0, 1.0, keep)
                    diff = now[n, c, some, :, tile(j)].astype(jnp.float32)
                    diff = diff - before[n, c, some, :, tile(j)].astype(jnp.float32)
                    turned = jnp.swapaxes(diff * valid, 0, 1)
                    outs[n][c, :, some, tile(j)] = turned.astype(jnp.bfloat16)


def residual(info, picks, each, frames, prev_fg, depth_valid):
    count, chans, rows, cols = frames.shape
    held = pltpu.VMEM((len(picks), each, count, rows, cols), jnp.bfloat16)
    return pl.pallas_call(
        functools.partial(residual_kernel, chans - 1, picks),
        in_specs=[smem()] + [anywhere()] * 3,
        out_specs=[vmem()] * len(picks),
        out_shape=[jax.ShapeDtypeStruct((each, rows, count, cols), jnp.bfloat16)] * len(picks),
        scratch_shapes=[
            held,
            held,
            pltpu.VMEM((count, rows, cols), jnp.int32),
            pltpu.SemaphoreType.DMA((1 + 2 * each * len(picks),)),
        ],
        compiler_params=pltpu.CompilerParams(vmem_limit_bytes=MOST_BYTES),
        cost_estimate=cost(3.0),
        name="residual",
    )(info, frames, prev_fg, depth_valid)


def interleave_kernel(info_ref, frames_ref, valid_ref, order_ref, *refs):
    out_ref, rims = refs[-3], refs[-2:]
    odd = info_ref[info_ref.shape[0] - 1]
    count, chans, rows, cols = frames_ref.shape
    for c in range(chans + 1):
        for g in range(count // PACK):
            some = pl.ds(g * PACK, PACK)
            if c < chans:
                lines = frames_ref[some, c]
            else:
                lines = valid_ref[some].astype(jnp.float32).astype(jnp.bfloat16)
            lines = short_dot(lines.reshape(PACK * rows, cols), order_ref[...], 1, 0)
            for j in range(cols // LANE):
                turned = lines[:, LANE * j : LANE * (j + 1)].reshape(PACK, rows, LANE)
                turned = jnp.swapaxes(turned, 0, 1).astype(jnp.bfloat16)
                out_ref[c, :, some, tile(j)] = turned
    write_rims(rims, odd, lambda h: out_ref[:, h], rows)


def write_rims(rims, odd, read, rows, axis_rows=NSWEEP):
    first = jnp.where(odd != 0, 0, rows - axis_rows)
    for h in range(axis_rows):
        rims[0][:, h] = read(first + h)
        rims[1][:, h] = read(rows - axis_rows - first + h)


def interleaved(info, frames, depth_valid, order, after):
    count, chans, rows, cols = frames.shape
    return pl.pallas_call(
        interleave_kernel,
        in_specs=[smem()] + [vmem()] * 3 + [anywhere()] * len(after),
        out_specs=[vmem()] * 3,
        out_shape=[
            jax.ShapeDtypeStruct((chans + 1, height, count, cols), jnp.bfloat16)
            for height in (rows, NSWEEP, NSWEEP)
        ],
        compiler_params=room(),
        cost_estimate=cost(3.3),
        name="interleave",
    )(info, frames, depth_valid, order, *after)


def gram_kernel(groups, each, nval, ids_ref, *refs):
    blocks, (gram_ref, all_ref), rims = refs[:groups], refs[-4:-2], refs[-2:]
    lines, count, cols = blocks[0].shape
    for k, block in enumerate(blocks):
        start = pl.multiple_of(ids_ref[groups + k] * count, count)
        all_ref[:, pl.ds(start, count), :] = block[...]
    rows = lines // each
    odd = ids_ref[ids_ref.shape[0] - 1]
    for c in range(each):
        some = [rim.at[pl.ds(c, 1)] for rim in rims]
        write_rims(some, odd, lambda h, c=c: all_ref[pl.ds(c * rows + h, 1)], rows)
    every = all_ref.shape[1]
    total = jnp.zeros((every, every), jnp.float32)
    for r in range(lines):
        total = total + short_dot(all_ref[r], all_ref[r], 1, 1)
    gram_ref[...] = packed(total / nval)


def gram_terms(ids, blocks, each, nval, after):
    groups = len(blocks)
    lines, count, cols = blocks[0].shape
    every = groups * count
    return pl.pallas_call(
        functools.partial(gram_kernel, groups, each, nval),
        in_specs=[smem()] + [vmem()] * groups + [anywhere()] * len(after),
        out_specs=[vmem()] * 4,
        out_shape=[
            jax.ShapeDtypeStruct((every // 2 + SUB, every), jnp.float32),
            jax.ShapeDtypeStruct((lines, every, cols), jnp.bfloat16),
            jax.ShapeDtypeStruct((each, NSWEEP, every, cols), jnp.bfloat16),
            jax.ShapeDtypeStruct((each, NSWEEP, every, cols), jnp.bfloat16),
        ],
        compiler_params=room(),
        cost_estimate=cost(1.4),
        name="gram",
    )(ids, *blocks, *after)


def spread_kernel(picks, ids_ref, mixing_ref, all_ref, *refs):
    rims, pieces, weights = refs[:2], refs[2:-1], refs[-1]
    odd = ids_ref[ids_ref.shape[0] - 1] != 0
    each, lines, _, cols = pieces[0].shape
    halves = len(pieces) // len(picks)
    count = halves * PACK
    rows = lines - 2 * NSWEEP
    for k, pick in enumerate(picks):
        start = pl.multiple_of(ids_ref[pick] * count, count)
        weights[pl.ds(k * count, count), :] = mixing_ref[pl.ds(start, count), :]
    chosen = weights[...]
    for c in range(each):
        for at in range(lines):
            h = at - NSWEEP
            if h < 0:
                pixels = jnp.where(odd, rims[0][c, at], rims[1][c, at])
            elif h < rows:
                pixels = all_ref[c * rows + h]
            else:
                pixels = jnp.where(odd, rims[1][c, h - rows], rims[0][c, h - rows])
            back = short_dot(chosen, pixels, 1, 0).astype(jnp.bfloat16)
            for k, piece in enumerate(pieces):
                piece[c, at] = back[k * PACK : (k + 1) * PACK]


def spread(ids, mixing, pixels, rims, groups, picks):
    lines, every, cols = pixels.shape
    each = rims[0].shape[0]
    count = every // groups
    halves = count // PACK
    piece = jax.ShapeDtypeStruct((each, lines // each + 2 * NSWEEP, PACK, cols), jnp.bfloat16)
    pieces = pl.pallas_call(
        functools.partial(spread_kernel, picks),
        in_specs=[smem()] + [vmem()] * 4,
        out_specs=[vmem()] * len(picks) * halves,
        out_shape=[piece] * len(picks) * halves,
        scratch_shapes=[pltpu.VMEM((len(picks) * count, every), jnp.bfloat16)],
        compiler_params=room(),
        cost_estimate=cost(1.6),
        name="spread",
    )(ids, mixing, pixels, *rims)
    return [pieces[n * halves : (n + 1) * halves] for n in range(len(picks))]


def gate_kernel(*refs):
    pass


def gate(values, after):
    count = len(values)
    return pl.pallas_call(
        gate_kernel,
        in_specs=[anywhere()] * (count + len(after)),
        out_specs=[anywhere()] * count,
        out_shape=[jax.ShapeDtypeStruct(value.shape, value.dtype) for value in values],
        input_output_aliases={n: n for n in range(count)},
        compiler_params=room(),
        name="gate",
    )(*values, *after)


def variation_kernel(units, at, n_outs, info_ref, weight_ref, order_ref, *refs):
    n_back = len(units)
    own, rims, backs = refs[0], refs[1:3], refs[3 : 3 + n_back]
    fg_out, bg_out, token_ref, source, first, second, flat_fg, flat_bg, image_held, fg_held, bg_held, sems = refs[
        3 + n_back + n_outs :
    ]
    groups = (info_ref.shape[0] - 3) // 2
    odd = info_ref[2 * groups + 2] != 0
    channels = [info_ref[groups + pick] * backs[0].shape[0] + at for pick, _ in units]
    edge = NSWEEP
    nf = PACK
    chans, rows, count, cols = own.shape
    chans -= 1
    tiles = cols // LANE
    lines = rows + 2 * edge
    up_flag = info_ref[2 * groups].astype(jnp.float32)
    down_flag = info_ref[2 * groups + 1].astype(jnp.float32)
    end = lax.broadcasted_iota(jnp.int32, (nf, LANE), 1) == LANE - 1

    def frames_at(chan, h, some):
        if h < 0:
            return jnp.where(odd, rims[0][chan, h + edge, some, :], rims[1][chan, h + edge, some, :])
        if h < rows:
            return own[chan, h, some, :]
        return jnp.where(odd, rims[1][chan, h - rows, some, :], rims[0][chan, h - rows, some, :])

    def load(ref, i):
        return [ref[i, :, tile(j)] for j in range(tiles)]

    def divergence(over, here, beside):
        left = [pltpu.roll(beside[-1], 1, 1)] + beside[:-1]
        return [(here[j] - over[j]) + (beside[j] - left[j]) for j in range(tiles)]

    def smooth(i, over, here, beside):
        div = divergence(over, here, beside)
        image = load(source, i)
        return [image[j] - STEP_SIZE * div[j] for j in range(tiles)]

    def copy_of(held, out, n, g, chan, start):
        place = pl.ds(pl.multiple_of(start * nf, nf), nf)
        return pltpu.make_async_copy(held.at[g], out.at[place, chan], sems.at[n, g])

    for g, back in enumerate(backs):
        for h in range(rows):
            for j in range(tiles):
                line = back[at, edge + h, :, tile(j)].astype(jnp.float32)
                flat_bg[j, pl.ds(h, nf, stride=rows), :] = line
        for j in range(tiles):
            bg_held[g, :, :, tile(j)] = flat_bg[j].astype(jnp.bfloat16).reshape(nf, rows, LANE)
        moved = short_dot(back[at].reshape(lines * nf, cols), order_ref[...], 1, 0)
        for i in range(lines):
            image_held[g, i] = moved[i * nf : (i + 1) * nf]
        copy_of(bg_held, bg_out, 1, g, channels[g], units[g][1]).start()

    @pl.loop(0, n_back)
    def some_frames(g):
        chan, start = channels[0], units[0][1]
        for n in range(1, n_back):
            chan = jnp.where(g == n, channels[n], chan)
            start = jnp.where(g == n, units[n][1], start)
        some = pl.ds(pl.multiple_of(start * nf, nf), nf)
        lam = weight_ref[chan]
        step = STEP_SIZE / lam
        for i in range(lines):
            image = frames_at(chan, i - edge, some).astype(jnp.float32)
            source[i] = (image - image_held[g, i]) * step

        @pl.when(chan == chans - 1)
        def mask():
            for i in range(lines):
                source[i] = source[i] * frames_at(chans, i - edge, some).astype(jnp.float32)

        for sweep in range(NSWEEP):
            here = beside = None
            if sweep:
                here, beside = load(first, sweep), load(second, sweep)
                now = smooth(sweep, load(first, sweep - 1), here, beside)
            else:
                now = load(source, 0)
            for i in range(sweep, lines - 1 - sweep):
                next_here = next_beside = None
                if sweep:
                    next_here, next_beside = load(first, i + 1), load(second, i + 1)
                    later = smooth(i + 1, here, next_here, next_beside)
                else:
                    later = load(source, i + 1)
                right = now[1:] + [jnp.where(end, now[-1], pltpu.roll(now[0], LANE - 1, 1))]
                for j in range(tiles):
                    down = later[j] - now[j]
                    if i == edge - 1:
                        down = down * up_flag
                    if i == edge + rows - 1:
                        down = down * down_flag
                    across = right[j] - now[j]
                    square = down * down + across * across
                    size = square * lax.rsqrt(jnp.maximum(square, 1e-30))
                    scale = pl.reciprocal(1.0 + size, approx=True)
                    first[i, :, tile(j)] = (here[j] - down if sweep else -down) * scale
                    second[i, :, tile(j)] = (beside[j] - across if sweep else -across) * scale
                now, here, beside = later, next_here, next_beside

        over = load(first, edge - 1)
        for h in range(rows):
            here, beside = load(first, edge + h), load(second, edge + h)
            image = smooth(edge + h, over, here, beside)
            for j in range(tiles):
                flat_fg[j, pl.ds(h, nf, stride=rows), :] = image[j] * (lam / STEP_SIZE)
            over = here
        fg = jnp.concatenate([flat_fg[j].astype(jnp.bfloat16) for j in range(tiles)], axis=1)
        fg = short_dot(fg, order_ref[...], 1, 1).astype(jnp.bfloat16)
        fg_held[g] = fg.reshape(nf, rows, cols)
        copy_of(fg_held, fg_out, 0, g, chan, start).start()

    for g in range(n_back):
        copy_of(fg_held, fg_out, 0, g, channels[g], units[g][1]).wait()
        copy_of(bg_held, bg_out, 1, g, channels[g], units[g][1]).wait()


def variation(info, weights, units, at, order, own, rims, backs, outs, shape):
    count, chans, rows, cols = shape
    lines = rows + 2 * NSWEEP
    flat = pltpu.VMEM((cols // LANE, PACK * rows, LANE), jnp.float32)
    field = pltpu.VMEM((lines, PACK, cols), jnp.float32)
    held = pltpu.VMEM((len(backs), PACK, rows, cols), jnp.bfloat16)
    images = pltpu.VMEM((len(backs), lines, PACK, cols), jnp.float32)
    return pl.pallas_call(
        functools.partial(variation_kernel, units, at, len(outs)),
        in_specs=[smem(), smem()] + [vmem()] * (4 + len(backs)) + [anywhere()] * len(outs),
        out_specs=[anywhere(), anywhere(), vmem()],
        out_shape=[jax.ShapeDtypeStruct(shape, jnp.bfloat16)] * 2
        + [jax.ShapeDtypeStruct((SUB, LANE), jnp.float32)],
        scratch_shapes=[
            field,
            field,
            field,
            flat,
            flat,
            images,
            held,
            held,
            pltpu.SemaphoreType.DMA((2, len(backs))),
        ],
        input_output_aliases={6 + len(backs) + n: n for n in range(len(outs))},
        compiler_params=room(field, field, field, flat, flat, images, held, held),
        cost_estimate=cost(4.3 * len(backs)),
        name="variation",
    )(info, weights, order, own, *rims, *backs, *outs)


def body(frames, prev_fg, depth_valid, sketch, tv_weight):
    count, chans, rows, cols = frames.shape
    groups = lax.axis_size("frame")
    strips = lax.axis_size("pix")
    each = chans // groups
    nval = chans * rows * strips * cols
    tiles = cols // LANE
    me, strip = lax.axis_index("frame"), lax.axis_index("pix")
    targets = [partner(me, k, groups) for k in range(groups)]
    sources = [partner(me, k, groups, back=True) for k in range(groups)]
    ends = [strip > 0, strip < strips - 1, strip % 2]
    info = jnp.stack([jnp.asarray(one, jnp.int32) for one in targets + sources + ends])
    near = [k for k in range(1, groups) if power_of_two(k)]
    far = [k for k in range(1, groups) if not power_of_two(k)]

    resid = {}
    for picks in (near, far + [0]):
        resid.update(zip(picks, residual(info, picks, each, frames, prev_fg, depth_valid)))
    blocks = [resid[0]] + [swap(resid[k], "frame", k) for k in range(1, groups)]
    blocks = [block.reshape(each * rows, count, cols) for block in blocks]

    places = lax.broadcasted_iota(jnp.int32, (cols, cols), 1)
    places = places % LANE * tiles + places // LANE
    order = (places == lax.broadcasted_iota(jnp.int32, (cols, cols), 0)).astype(jnp.bfloat16)
    lined, *rims = interleaved(info, frames, depth_valid, order, tuple(resid.values()))
    lined_rims = rims_swapped(rims)

    terms, pixels, *rims = gram_terms(info, blocks, each, nval, ())
    gram = all_sum(all_sum(terms, "frame"), "pix")
    gram, *rims = gate([gram] + rims, lined_rims)
    around = rims_swapped(rims)
    mixing = mixing_matrix(gram, sketch)
    picks = [0] + near + far
    pieces = dict(zip(picks, spread(info, mixing, pixels, around, groups, picks)))
    halves = range(count // PACK)
    arrived = {(0, g): pieces[0][g] for g in halves}
    for k in near:
        arrived[k, 0] = swap(pieces[k][0], "frame", k)

    outs = []

    def work_on(units, outs):
        parts = [arrived[unit] for unit in units]
        for c in range(each):
            *outs, token = variation(
                info, tv_weight, units, c, order, lined, lined_rims, parts, outs, frames.shape
            )
        return outs, token

    token = None
    stages = [[(0, g)] for g in halves] + [[(k, g) for k in near] for g in halves]
    stages += [[(k, g)] for k in far for g in halves]
    sends = {g - 1: [(k, g) for k in near] for g in halves[1:]}
    sends[len(halves)] = [(k, g) for k in far for g in halves]
    for n, stage in enumerate(stages):
        outs, token = work_on(stage, outs)
        there = list(arrived.values()) if n >= len(halves) else []
        for k, g in sends.get(n, []):
            (held,) = gate([pieces[k][g]], [token] + there)
            arrived[k, g] = swap(held, "frame", k)
    foreground, background = outs
    return (background, foreground)


def solution(mesh):
    placed = (
        P("frame", None, "pix", None),
        P("frame", None, "pix", None),
        P("frame", "pix", None),
        P(),
        P(),
    )
    return jax.shard_map(
        body,
        mesh=mesh,
        in_specs=placed,
        out_specs=(P("frame", None, "pix", None), P("frame", None, "pix", None)),
        check_vma=False,
    )
```

```python
import functools
import math

import jax
import jax.numpy as jnp
from jax import lax
from jax.experimental import pallas as pl
from jax.experimental.pallas import tpu as pltpu
from jax.sharding import PartitionSpec as P

POWER = 3
NSWEEP = 5
STEP_SIZE = 0.125
SUB = 8
LANE = 128
PACK = 16
SPARE_BYTES = 7 * 1024 * 1024
MOST_BYTES = 58 * 1024 * 1024


def power_of_two(count):
    return count & (count - 1) == 0


def partner(index, offset, count, back=False):
    if power_of_two(count):
        return index ^ offset
    return (index + (count - offset if back else offset)) % count


def pair_swap(value, axis, start):
    count = lax.axis_size(axis)
    pairs = []
    for lower in range(start, count - 1, 2):
        pairs += [(lower, lower + 1), (lower + 1, lower)]
    return lax.ppermute(value, axis, pairs)


def rims_swapped(rims):
    return [pair_swap(rim, "pix", start) for start, rim in enumerate(rims)]


def swap(value, axis, offset):
    count = lax.axis_size(axis)
    pairs = [(source, partner(source, offset, count)) for source in range(count)]
    return lax.ppermute(value, axis, pairs)


def all_sum(value, axis):
    count = lax.axis_size(axis)
    if not power_of_two(count):
        return lax.psum(value, axis)
    bit = 1
    while bit < count:
        fours = (count // bit).bit_length() % 2 == 1
        offsets = (bit, 2 * bit, 3 * bit) if fours else (bit,)
        others = [swap(value, axis, offset) for offset in offsets]
        for other in others:
            value = value + other
        bit *= len(offsets) + 1
    return value


def exact_dot(left, right, left_dim, right_dim):
    return lax.dot_general(
        left,
        right,
        (((left_dim,), (right_dim,)), ((), ())),
        precision=lax.Precision.HIGHEST,
        preferred_element_type=jnp.float32,
    )


def short_dot(left, right, left_dim, right_dim):
    return lax.dot_general(
        left,
        right,
        (((left_dim,), (right_dim,)), ((), ())),
        preferred_element_type=jnp.float32,
    )


def eliminate(square, sides):
    rank = square.shape[0]
    width = sides[0].shape[1]
    blocks = rank // SUB
    sub_ids = lax.broadcasted_iota(jnp.int32, (SUB, width), 0)
    square = jnp.concatenate([square, jnp.zeros((rank, width - rank), jnp.float32)], axis=1)

    def in_blocks(rows):
        return [rows[SUB * b : SUB * (b + 1)] for b in range(blocks)]

    def row_of(rows, j):
        return jnp.broadcast_to(rows[j : j + 1], (SUB, width))

    def col_of(rows, j):
        return jnp.broadcast_to(rows[:, j : j + 1], (SUB, width))

    square = in_blocks(square)
    sides = [in_blocks(side) for side in sides]
    solved = [[] for _ in sides]
    for k in range(blocks):
        below = range(k, blocks)
        cols = {b: [col_of(square[b], SUB * k + j) for j in range(SUB)] for b in below}
        pivots = jnp.ones((SUB, width), jnp.float32)
        for j in range(0, SUB, 2):
            col, after = cols[k][j], cols[k][j + 1]
            corner, side_value, last = row_of(col, j), row_of(col, j + 1), row_of(after, j + 1)
            inverse = 1.0 / corner
            next_inverse = corner * (1.0 / (corner * last - side_value * side_value))
            link = side_value * inverse
            pivots = jnp.where(sub_ids == j, corner, pivots)
            pivots = jnp.where(sub_ids == j + 1, last - side_value * link, pivots)

            def two_rows(rows):
                upper = row_of(rows, j)
                return upper, row_of(rows, j + 1) - link * upper

            top = row_of(after, j)
            col_rows = {i: two_rows(cols[k][i]) for i in range(j + 2, SUB)}
            square_rows = two_rows(square[k])
            side_rows = [two_rows(side[k]) for side in sides]
            for b in below:
                ratio = cols[b][j] * inverse
                if b == k:
                    ratio = jnp.where(sub_ids > j, ratio, 0.0)
                next_ratio = (cols[b][j + 1] - ratio * top) * next_inverse
                if b == k:
                    next_ratio = jnp.where(sub_ids > j + 1, next_ratio, 0.0)

                def reduced(rows, pair):
                    return rows - ratio * pair[0] - next_ratio * pair[1]

                for i in range(j + 2, SUB):
                    cols[b][i] = reduced(cols[b][i], col_rows[i])
                square[b] = reduced(square[b], square_rows)
                for side, pair in zip(sides, side_rows):
                    side[b] = reduced(side[b], pair)
        scale = lax.rsqrt(pivots)
        for rows, side in zip(solved, sides):
            rows.append(side[k] * scale)
    return [jnp.concatenate(rows, axis=0) for rows in solved]


def corner_masks(size):
    shape = (size // 2, size)
    rows = lax.broadcasted_iota(jnp.int32, shape, 0)
    lanes = lax.broadcasted_iota(jnp.int32, shape, 1)
    return lanes < size // 2, rows >= lanes, rows == lanes


def packed(square):
    size = square.shape[0]
    left, lower, diagonal = corner_masks(size)
    upper_half = square[: size // 2]
    turned = pltpu.roll(square[size // 2 :], size // 2, 1)
    rows = jnp.where(left & ~lower, turned, upper_half)
    line = jnp.sum(jnp.where(left & diagonal, turned, 0.0), axis=0, keepdims=True)
    return jnp.concatenate([rows, jnp.broadcast_to(line, (SUB, size))], axis=0)


def unpacked(rows):
    size = rows.shape[1]
    half = size // 2
    left, lower, diagonal = corner_masks(size)
    line = rows[half : half + 1]
    rows = rows[:half]
    turned = jnp.concatenate([rows, jnp.zeros((half, size), jnp.float32)], axis=0).T
    upper_half = jnp.where(left & ~lower, turned[:half], rows)
    corner = jnp.where(diagonal, line, jnp.where(lower, turned[:half], rows))
    lower_half = jnp.where(left, turned[half:], pltpu.roll(corner, half, 1))
    return jnp.concatenate([upper_half, lower_half], axis=0)


def mixing_kernel(gram_ref, sketch_ref, mixing_ref):
    gram = unpacked(gram_ref[...])
    basis = sketch_ref[...]
    for turn in range(POWER):
        image = exact_dot(basis, gram, 1, 1)
        (basis,) = eliminate(exact_dot(basis, image, 1, 1), [image])
    image = exact_dot(basis, gram, 1, 1)
    left, right = eliminate(exact_dot(basis, image, 1, 1), [basis, image])
    mixing_ref[...] = exact_dot(right, left, 0, 0).astype(mixing_ref.dtype)


def mixing_matrix(gram, sketch):
    return pl.pallas_call(
        mixing_kernel,
        out_shape=jax.ShapeDtypeStruct(gram.shape[1:] * 2, jnp.bfloat16),
        compiler_params=room(),
        cost_estimate=cost(10.6),
        name="mixing",
    )(gram, sketch.T)


def tile(j):
    return pl.ds(LANE * j, LANE)


def vmem():
    return pl.BlockSpec(memory_space=pltpu.VMEM)


def smem():
    return pl.BlockSpec(memory_space=pltpu.SMEM)


def anywhere():
    return pl.BlockSpec(memory_space=pl.ANY)


def room(*scratch):
    held = sum(math.prod(ref.shape) * jnp.dtype(ref.dtype).itemsize for ref in scratch)
    return pltpu.CompilerParams(vmem_limit_bytes=SPARE_BYTES + held)


def cost(micros):
    return pl.CostEstimate(flops=0, bytes_accessed=int(micros * 3.6e6), transcendentals=0)


def residual_kernel(last, picks, frames_ref, prev_ref, valid_ref, *refs):
    outs, (now, before, ok, sems) = refs[: len(picks)], refs[len(picks) :]
    _, each, count, rows, cols = now.shape
    me, groups = lax.axis_index("frame"), lax.axis_size("frame")
    firsts = [partner(me, pick, groups) * each for pick in picks]
    valid_copy = pltpu.make_async_copy(valid_ref, ok, sems.at[0])
    copies = []
    for n in range(len(picks)):
        for c in range(each):
            chan = firsts[n] + c
            at = 1 + 2 * (n * each + c)
            copies.append(
                (
                    pltpu.make_async_copy(frames_ref.at[:, chan], now.at[n, c], sems.at[at]),
                    pltpu.make_async_copy(prev_ref.at[:, chan], before.at[n, c], sems.at[at + 1]),
                )
            )
    valid_copy.start()
    for pair in copies:
        for copy in pair:
            copy.start()
    valid_copy.wait()
    for n in range(len(picks)):
        for c in range(each):
            for copy in copies[n * each + c]:
                copy.wait()
            keep = jnp.where(firsts[n] + c == last, 0.0, 1.0)
            for g in range(count // PACK):
                some = pl.ds(g * PACK, PACK)
                for j in range(cols // LANE):
                    valid = jnp.where(ok[some, :, tile(j)] != 0, 1.0, keep)
                    diff = now[n, c, some, :, tile(j)].astype(jnp.float32)
                    diff = diff - before[n, c, some, :, tile(j)].astype(jnp.float32)
                    turned = jnp.swapaxes(diff * valid, 0, 1)
                    outs[n][c, :, some, tile(j)] = turned.astype(jnp.bfloat16)


def residual(picks, each, frames, prev_fg, depth_valid):
    count, chans, rows, cols = frames.shape
    held = pltpu.VMEM((len(picks), each, count, rows, cols), jnp.bfloat16)
    return pl.pallas_call(
        functools.partial(residual_kernel, chans - 1, picks),
        in_specs=[anywhere()] * 3,
        out_specs=[vmem()] * len(picks),
        out_shape=[jax.ShapeDtypeStruct((each, rows, count, cols), jnp.bfloat16)] * len(picks),
        scratch_shapes=[
            held,
            held,
            pltpu.VMEM((count, rows, cols), jnp.int32),
            pltpu.SemaphoreType.DMA((1 + 2 * each * len(picks),)),
        ],
        compiler_params=pltpu.CompilerParams(vmem_limit_bytes=MOST_BYTES),
        cost_estimate=cost(3.0),
        name="residual",
    )(frames, prev_fg, depth_valid)


def interleave_kernel(info_ref, frames_ref, valid_ref, order_ref, *refs):
    out_ref, rims = refs[-3], refs[-2:]
    odd = info_ref[info_ref.shape[0] - 1]
    count, chans, rows, cols = frames_ref.shape
    for c in range(chans + 1):
        for g in range(count // PACK):
            some = pl.ds(g * PACK, PACK)
            if c < chans:
                lines = frames_ref[some, c]
            else:
                lines = valid_ref[some].astype(jnp.float32).astype(jnp.bfloat16)
            lines = short_dot(lines.reshape(PACK * rows, cols), order_ref[...], 1, 0)
            for j in range(cols // LANE):
                turned = lines[:, LANE * j : LANE * (j + 1)].reshape(PACK, rows, LANE)
                turned = jnp.swapaxes(turned, 0, 1).astype(jnp.bfloat16)
                out_ref[c, :, some, tile(j)] = turned
    write_rims(rims, odd, lambda h: out_ref[:, h], rows)


def write_rims(rims, odd, read, rows, axis_rows=NSWEEP):
    first = jnp.where(odd != 0, 0, rows - axis_rows)
    for h in range(axis_rows):
        rims[0][:, h] = read(first + h)
        rims[1][:, h] = read(rows - axis_rows - first + h)


def interleaved(info, frames, depth_valid, order, after):
    count, chans, rows, cols = frames.shape
    return pl.pallas_call(
        interleave_kernel,
        in_specs=[smem()] + [vmem()] * 3 + [anywhere()] * len(after),
        out_specs=[vmem()] * 3,
        out_shape=[
            jax.ShapeDtypeStruct((chans + 1, height, count, cols), jnp.bfloat16)
            for height in (rows, NSWEEP, NSWEEP)
        ],
        compiler_params=room(),
        cost_estimate=cost(3.3),
        name="interleave",
    )(info, frames, depth_valid, order, *after)


def gram_kernel(groups, each, nval, ids_ref, *refs):
    blocks, (gram_ref, all_ref), rims = refs[:groups], refs[-4:-2], refs[-2:]
    lines, count, cols = blocks[0].shape
    for k, block in enumerate(blocks):
        start = pl.multiple_of(ids_ref[groups + k] * count, count)
        all_ref[:, pl.ds(start, count), :] = block[...]
    rows = lines // each
    odd = ids_ref[ids_ref.shape[0] - 1]
    for c in range(each):
        some = [rim.at[pl.ds(c, 1)] for rim in rims]
        write_rims(some, odd, lambda h, c=c: all_ref[pl.ds(c * rows + h, 1)], rows)
    every = all_ref.shape[1]
    total = jnp.zeros((every, every), jnp.float32)
    for r in range(lines):
        total = total + short_dot(all_ref[r], all_ref[r], 1, 1)
    gram_ref[...] = packed(total / nval)


def gram_terms(ids, blocks, each, nval, after):
    groups = len(blocks)
    lines, count, cols = blocks[0].shape
    every = groups * count
    return pl.pallas_call(
        functools.partial(gram_kernel, groups, each, nval),
        in_specs=[smem()] + [vmem()] * groups + [anywhere()] * len(after),
        out_specs=[vmem()] * 4,
        out_shape=[
            jax.ShapeDtypeStruct((every // 2 + SUB, every), jnp.float32),
            jax.ShapeDtypeStruct((lines, every, cols), jnp.bfloat16),
            jax.ShapeDtypeStruct((each, NSWEEP, every, cols), jnp.bfloat16),
            jax.ShapeDtypeStruct((each, NSWEEP, every, cols), jnp.bfloat16),
        ],
        compiler_params=room(),
        cost_estimate=cost(1.4),
        name="gram",
    )(ids, *blocks, *after)


def spread_kernel(picks, ids_ref, mixing_ref, all_ref, *refs):
    rims, pieces, weights = refs[:2], refs[2:-1], refs[-1]
    odd = ids_ref[ids_ref.shape[0] - 1] != 0
    each, lines, _, cols = pieces[0].shape
    halves = len(pieces) // len(picks)
    count = halves * PACK
    rows = lines - 2 * NSWEEP
    for k, pick in enumerate(picks):
        start = pl.multiple_of(ids_ref[pick] * count, count)
        weights[pl.ds(k * count, count), :] = mixing_ref[pl.ds(start, count), :]
    chosen = weights[...]
    for c in range(each):
        for at in range(lines):
            h = at - NSWEEP
            if h < 0:
                pixels = jnp.where(odd, rims[0][c, at], rims[1][c, at])
            elif h < rows:
                pixels = all_ref[c * rows + h]
            else:
                pixels = jnp.where(odd, rims[1][c, h - rows], rims[0][c, h - rows])
            back = short_dot(chosen, pixels, 1, 0).astype(jnp.bfloat16)
            for k, piece in enumerate(pieces):
                piece[c, at] = back[k * PACK : (k + 1) * PACK]


def spread(ids, mixing, pixels, rims, groups, picks):
    lines, every, cols = pixels.shape
    each = rims[0].shape[0]
    count = every // groups
    halves = count // PACK
    piece = jax.ShapeDtypeStruct((each, lines // each + 2 * NSWEEP, PACK, cols), jnp.bfloat16)
    pieces = pl.pallas_call(
        functools.partial(spread_kernel, picks),
        in_specs=[smem()] + [vmem()] * 4,
        out_specs=[vmem()] * len(picks) * halves,
        out_shape=[piece] * len(picks) * halves,
        scratch_shapes=[pltpu.VMEM((len(picks) * count, every), jnp.bfloat16)],
        compiler_params=room(),
        cost_estimate=cost(1.6),
        name="spread",
    )(ids, mixing, pixels, *rims)
    return [pieces[n * halves : (n + 1) * halves] for n in range(len(picks))]


def gate_kernel(*refs):
    pass


def gate(values, after):
    count = len(values)
    return pl.pallas_call(
        gate_kernel,
        in_specs=[anywhere()] * (count + len(after)),
        out_specs=[anywhere()] * count,
        out_shape=[jax.ShapeDtypeStruct(value.shape, value.dtype) for value in values],
        input_output_aliases={n: n for n in range(count)},
        compiler_params=room(),
        name="gate",
    )(*values, *after)


def variation_kernel(units, at, n_outs, info_ref, weight_ref, order_ref, *refs):
    n_back = len(units)
    own, rims, backs = refs[0], refs[1:3], refs[3 : 3 + n_back]
    fg_out, bg_out, token_ref, source, first, second, flat_fg, flat_bg, image_held, fg_held, bg_held, sems = refs[
        3 + n_back + n_outs :
    ]
    groups = (info_ref.shape[0] - 3) // 2
    odd = info_ref[2 * groups + 2] != 0
    channels = [info_ref[groups + pick] * backs[0].shape[0] + at for pick, _ in units]
    edge = NSWEEP
    nf = PACK
    chans, rows, count, cols = own.shape
    chans -= 1
    tiles = cols // LANE
    lines = rows + 2 * edge
    up_flag = info_ref[2 * groups].astype(jnp.float32)
    down_flag = info_ref[2 * groups + 1].astype(jnp.float32)
    end = lax.broadcasted_iota(jnp.int32, (nf, LANE), 1) == LANE - 1

    def frames_at(chan, h, some):
        if h < 0:
            return jnp.where(odd, rims[0][chan, h + edge, some, :], rims[1][chan, h + edge, some, :])
        if h < rows:
            return own[chan, h, some, :]
        return jnp.where(odd, rims[1][chan, h - rows, some, :], rims[0][chan, h - rows, some, :])

    def load(ref, i):
        return [ref[i, :, tile(j)] for j in range(tiles)]

    def divergence(over, here, beside):
        left = [pltpu.roll(beside[-1], 1, 1)] + beside[:-1]
        return [(here[j] - over[j]) + (beside[j] - left[j]) for j in range(tiles)]

    def smooth(i, over, here, beside):
        div = divergence(over, here, beside)
        image = load(source, i)
        return [image[j] - STEP_SIZE * div[j] for j in range(tiles)]

    def copy_of(held, out, n, g, chan, start):
        place = pl.ds(pl.multiple_of(start * nf, nf), nf)
        return pltpu.make_async_copy(held.at[g], out.at[place, chan], sems.at[n, g])

    for g, back in enumerate(backs):
        for h in range(rows):
            for j in range(tiles):
                line = back[at, edge + h, :, tile(j)].astype(jnp.float32)
                flat_bg[j, pl.ds(h, nf, stride=rows), :] = line
        for j in range(tiles):
            bg_held[g, :, :, tile(j)] = flat_bg[j].astype(jnp.bfloat16).reshape(nf, rows, LANE)
        moved = short_dot(back[at].reshape(lines * nf, cols), order_ref[...], 1, 0)
        for i in range(lines):
            image_held[g, i] = moved[i * nf : (i + 1) * nf]
        copy_of(bg_held, bg_out, 1, g, channels[g], units[g][1]).start()

    @pl.loop(0, n_back)
    def some_frames(g):
        chan, start = channels[0], units[0][1]
        for n in range(1, n_back):
            chan = jnp.where(g == n, channels[n], chan)
            start = jnp.where(g == n, units[n][1], start)
        some = pl.ds(pl.multiple_of(start * nf, nf), nf)
        lam = weight_ref[chan]
        step = STEP_SIZE / lam
        for i in range(lines):
            image = frames_at(chan, i - edge, some).astype(jnp.float32)
            source[i] = (image - image_held[g, i]) * step

        @pl.when(chan == chans - 1)
        def mask():
            for i in range(lines):
                source[i] = source[i] * frames_at(chans, i - edge, some).astype(jnp.float32)

        for sweep in range(NSWEEP):
            here = beside = None
            if sweep:
                here, beside = load(first, sweep), load(second, sweep)
                now = smooth(sweep, load(first, sweep - 1), here, beside)
            else:
                now = load(source, 0)
            for i in range(sweep, lines - 1 - sweep):
                next_here = next_beside = None
                if sweep:
                    next_here, next_beside = load(first, i + 1), load(second, i + 1)
                    later = smooth(i + 1, here, next_here, next_beside)
                else:
                    later = load(source, i + 1)
                right = now[1:] + [jnp.where(end, now[-1], pltpu.roll(now[0], LANE - 1, 1))]
                for j in range(tiles):
                    down = later[j] - now[j]
                    if i == edge - 1:
                        down = down * up_flag
                    if i == edge + rows - 1:
                        down = down * down_flag
                    across = right[j] - now[j]
                    square = down * down + across * across
                    size = square * lax.rsqrt(jnp.maximum(square, 1e-30))
                    scale = pl.reciprocal(1.0 + size, approx=True)
                    first[i, :, tile(j)] = (here[j] - down if sweep else -down) * scale
                    second[i, :, tile(j)] = (beside[j] - across if sweep else -across) * scale
                now, here, beside = later, next_here, next_beside

        over = load(first, edge - 1)
        for h in range(rows):
            here, beside = load(first, edge + h), load(second, edge + h)
            image = smooth(edge + h, over, here, beside)
            for j in range(tiles):
                flat_fg[j, pl.ds(h, nf, stride=rows), :] = image[j] * (lam / STEP_SIZE)
            over = here
        fg = jnp.concatenate([flat_fg[j].astype(jnp.bfloat16) for j in range(tiles)], axis=1)
        fg = short_dot(fg, order_ref[...], 1, 1).astype(jnp.bfloat16)
        fg_held[g] = fg.reshape(nf, rows, cols)
        copy_of(fg_held, fg_out, 0, g, chan, start).start()

    for g in range(n_back):
        copy_of(fg_held, fg_out, 0, g, channels[g], units[g][1]).wait()
        copy_of(bg_held, bg_out, 1, g, channels[g], units[g][1]).wait()


def variation(info, weights, units, at, order, own, rims, backs, outs, shape):
    count, chans, rows, cols = shape
    lines = rows + 2 * NSWEEP
    flat = pltpu.VMEM((cols // LANE, PACK * rows, LANE), jnp.float32)
    field = pltpu.VMEM((lines, PACK, cols), jnp.float32)
    held = pltpu.VMEM((len(backs), PACK, rows, cols), jnp.bfloat16)
    images = pltpu.VMEM((len(backs), lines, PACK, cols), jnp.float32)
    return pl.pallas_call(
        functools.partial(variation_kernel, units, at, len(outs)),
        in_specs=[smem(), smem()] + [vmem()] * (4 + len(backs)) + [anywhere()] * len(outs),
        out_specs=[anywhere(), anywhere(), vmem()],
        out_shape=[jax.ShapeDtypeStruct(shape, jnp.bfloat16)] * 2
        + [jax.ShapeDtypeStruct((SUB, LANE), jnp.float32)],
        scratch_shapes=[
            field,
            field,
            field,
            flat,
            flat,
            images,
            held,
            held,
            pltpu.SemaphoreType.DMA((2, len(backs))),
        ],
        input_output_aliases={6 + len(backs) + n: n for n in range(len(outs))},
        compiler_params=room(field, field, field, flat, flat, images, held, held),
        cost_estimate=cost(4.3 * len(backs)),
        name="variation",
    )(info, weights, order, own, *rims, *backs, *outs)


def body(frames, prev_fg, depth_valid, sketch, tv_weight):
    count, chans, rows, cols = frames.shape
    groups = lax.axis_size("frame")
    strips = lax.axis_size("pix")
    each = chans // groups
    nval = chans * rows * strips * cols
    tiles = cols // LANE
    me, strip = lax.axis_index("frame"), lax.axis_index("pix")
    targets = [partner(me, k, groups) for k in range(groups)]
    sources = [partner(me, k, groups, back=True) for k in range(groups)]
    ends = [strip > 0, strip < strips - 1, strip % 2]
    info = jnp.stack([jnp.asarray(one, jnp.int32) for one in targets + sources + ends])
    near = [k for k in range(1, groups) if power_of_two(k)]
    far = [k for k in range(1, groups) if not power_of_two(k)]

    resid = {}
    for picks in (near, far + [0]):
        resid.update(zip(picks, residual(picks, each, frames, prev_fg, depth_valid)))
    blocks = [resid[0]] + [swap(resid[k], "frame", k) for k in range(1, groups)]
    blocks = [block.reshape(each * rows, count, cols) for block in blocks]

    places = lax.broadcasted_iota(jnp.int32, (cols, cols), 1)
    places = places % LANE * tiles + places // LANE
    order = (places == lax.broadcasted_iota(jnp.int32, (cols, cols), 0)).astype(jnp.bfloat16)
    lined, *rims = interleaved(info, frames, depth_valid, order, tuple(resid.values()))
    lined_rims = rims_swapped(rims)

    terms, pixels, *rims = gram_terms(info, blocks, each, nval, ())
    gram = all_sum(all_sum(terms, "pix"), "frame")
    gram, *rims = gate([gram] + rims, lined_rims)
    around = rims_swapped(rims)
    mixing = mixing_matrix(gram, sketch)
    picks = [0] + near + far
    pieces = dict(zip(picks, spread(info, mixing, pixels, around, groups, picks)))
    halves = range(count // PACK)
    arrived = {(0, g): pieces[0][g] for g in halves}
    for k in near:
        arrived[k, 0] = swap(pieces[k][0], "frame", k)

    outs = []

    def work_on(units, outs):
        parts = [arrived[unit] for unit in units]
        for c in range(each):
            *outs, token = variation(
                info, tv_weight, units, c, order, lined, lined_rims, parts, outs, frames.shape
            )
        return outs, token

    token = None
    stages = [[(0, g)] for g in halves] + [[(k, g) for k in near] for g in halves]
    stages += [[(k, g)] for k in far for g in halves]
    sends = {g - 1: [(k, g) for k in near] for g in halves[1:]}
    sends[len(halves)] = [(k, g) for k in far for g in halves]
    for n, stage in enumerate(stages):
        outs, token = work_on(stage, outs)
        there = list(arrived.values()) if n >= len(halves) else []
        for k, g in sends.get(n, []):
            (held,) = gate([pieces[k][g]], [token] + there)
            arrived[k, g] = swap(held, "frame", k)
    foreground, background = outs
    return (background, foreground)


def solution(mesh):
    placed = (
        P("frame", None, "pix", None),
        P("frame", None, "pix", None),
        P("frame", "pix", None),
        P(),
        P(),
    )
    return jax.shard_map(
        body,
        mesh=mesh,
        in_specs=placed,
        out_specs=(P("frame", None, "pix", None), P("frame", None, "pix", None)),
        check_vma=False,
    )
```
